128 devices in a mesh: gx: 16 (over y_hi, z, core), gy: 8 (over y_lo, x).
Axes of the slice: x: 4, y: 4 (y_hi: 2, y_lo: 2; y = y_hi * 2 + y_lo), z: 4, core: 2. Of those that a mesh axis runs over, the one named last changes fastest.
Arguments:
- grad_pressure: float32 [128, 256, 1024], P('gx', 'gy'), may hold values from -6 to 6
- beta: float32 [3, 128, 256, 1024], P(None, 'gx', 'gy'), may hold values from 0.25 to 4
- tile_rows: int32 [32768], P(('gx', 'gy')), may hold values from 0 to 2047
- tile_owner: int32 [32768, 1], P(('gx', 'gy')), may hold values from 0 to 127; in each aligned block of 256 rows (0 to 255, 256 to 511, ...) at most 8 rows name the same one
- tile_slot: int32 [32768], P(('gx', 'gy')), may hold values from 0 to 255
- face_mask: int32 [32768, 128], P(('gx', 'gy')), may hold values 0 or 1
- heights: float32 [3, 32768, 128], P(None, ('gx', 'gy')), may hold values from -6 to 6
Outputs:
- grad_rhs: float32 [128, 256, 1024], P('gx', 'gy')
- grad_heights: float32 [3, 32768, 128], P(None, ('gx', 'gy'))
The draws below stay inside these ranges and needn't reach their ends.
Inputs may be any that keep to these rules, and one draw needn't show every extreme that they name: `tile_rows`: each entry indexes a row of 128 cells inside its own device's block. `tile_owner`: among the 256 tiles of one device no owner is named more than 8 times.
All inputs are finite; a program needn't handle non-finite values. No bound on the sum of `face_mask` on one device may be relied on, other than what follows from the above.
Results may differ from the reference program's by a relative error of at most 0.000025.
Values sent between devices are 32-bit elements; how exact they have to be, the bound alone decides.
No kernel may reach another device: no remote copies, remote signals or barrier semaphores. Data moves between devices by JAX's collectives and lax.ppermute only.
A program may use at most 192 MiB of HBM per device.

```python
import math
import jax
import jax.numpy as jnp
import numpy as np

CX = 8
CY = 32
NZ = 1024
ITERS = 3
STEPS = 4
NT = 256
SLOTS = 256
CAP = 8
NX = 128
NY = 256
N_GX = 16
N_GY = 8


def place_ends(entries, own_key, low, top_value):
    spot = [jax.random.randint(jax.random.fold_in(own_key, axis), (), 0, length) for axis, length in enumerate(entries.shape)]
    main_axis = entries.shape.index(max(entries.shape))
    neighbour = spot[:main_axis] + [(spot[main_axis] + 1) % entries.shape[main_axis]] + spot[main_axis + 1:]
    return entries.at[tuple(spot)].set(low).at[tuple(neighbour)].set(top_value)


def levels(stream_key, dims, split, smallest, high):
    gain, own = 1.0, jax.random.fold_in(stream_key, 6)
    for axis_at, shards_of in split:
        draws = jnp.exp(jax.random.uniform(jax.random.fold_in(own, axis_at), (shards_of,), jnp.float32, smallest / len(split), high / len(split)))
        gain = gain * jnp.repeat(draws, dims[axis_at] // shards_of).reshape([-1 if axis == axis_at else 1 for axis in range(len(dims))])
    return gain


def deal_out(stream_key, own, number, rows, number_of, top, reach, lean):
    ranking = jax.random.permutation(stream_key, number_of)
    packed, usual = shares(number_of, rows * top, reach, lean, True), shares(number_of, rows * top, reach, lean, False)
    places = jnp.arange(number_of)

    def named(sizes, offset_by):
        used = int((sizes > 0).sum())
        fixed = max(1, used // 4)
        moved = fixed + (places - fixed + offset_by * (used - fixed)) % max(1, number_of - fixed)
        return jnp.zeros((number_of,), jnp.int32).at[ranking[jnp.where(places < fixed, places, moved)]].set(jnp.asarray(sizes, jnp.int32))

    sizes = jnp.where(number % 4 == 0, named(packed, number // 4), named(usual, number - number // 4 - 1))
    mixed = jax.random.permutation(jax.random.fold_in(own, 3), number_of)
    source_of, sink = mixed[0:number_of // 2 * 2:2], mixed[1:number_of // 2 * 2:2]
    slack = jnp.minimum(sizes[source_of] - 1, reach - sizes[sink]) // 2
    slack = jnp.where((source_of == ranking[0]) | (sink == ranking[0]) | (sizes[sink] == 0), 0, jnp.maximum(slack, 0))
    moved = jax.random.randint(jax.random.fold_in(own, 4), (number_of // 2,), 0, 1 << 20) % (slack + 1)
    sizes = sizes.at[source_of].add(-moved).at[sink].add(moved)
    items = jnp.searchsorted(jnp.cumsum(sizes), jnp.arange(rows * top), side="right").astype(jnp.int32)
    listing = items.reshape(top, rows).T
    listing = listing[jax.random.permutation(jax.random.fold_in(own, 1), rows)]
    offset_by = jax.random.randint(jax.random.fold_in(own, 2), (rows, 1), 0, top)
    return jnp.take_along_axis(listing, (jnp.arange(top)[None, :] + offset_by) % top, axis=1)


def shares(count, total, most, skew, full):
    weights = [(1 << 20) // math.isqrt(standing ** skew) + 1 for standing in range(1, count + 1)]
    largest = most if full else min(most, max(-(-total // count), total * weights[0] // sum(weights)))
    least = 1 if total - largest >= count - 1 else 0
    counts, surplus = [largest] + [least] * (count - 1), total - largest - least * (count - 1)
    while surplus > 0:
        movable = [i for i in range(1, count) if counts[i] < largest] or [i for i in range(1, count) if counts[i] < most]
        mass, budget = sum([weights[i] for i in movable]), surplus
        for i in movable:
            more = min(most - counts[i], max(1, budget * weights[i] // mass), surplus)
            counts[i] = counts[i] + more
            surplus = surplus - more
    return np.array(counts)


def scatter_about(key, extent, scale, reach, split=(), kind=jnp.bfloat16):
    result = jax.random.normal(key, extent, jnp.float32) * scale
    if len(split) > 0:
        result = levels(key, extent, split, -0.22, 0.18) * result
    return jnp.clip(result, min=-reach, max=reach).astype(kind)


def setup_inputs(seed: int = 0) -> dict:
    key_of = jax.random.split(jax.random.key(seed), 8)
    grad_pressure = scatter_about(key_of[0], (NX, NY, NZ), 1.0, 6.0, ((0, 16), (1, 8)), jnp.float32)
    beta = jnp.clip(jnp.exp(math.log(4.0) - 2.7725887 * jax.random.uniform(key_of[1], (3, NX, NY, NZ), jnp.float32) ** levels(key_of[1], (3, NX, NY, NZ), ((1, 16), (2, 8)), -0.2, 0.2)), 0.25, 4.0)
    tile_rows = place_ends(jax.random.randint(key_of[2], (N_GX * N_GY * NT,), 0, CX * CY * NZ // 128), jax.random.fold_in(key_of[2], 1), 0, (CX * CY * NZ // 128) - 1).astype(jnp.int32)
    tile_owner_keys = jax.random.split(jax.random.fold_in(key_of[3], 1), (N_GX * N_GY * NT) // NT)
    tile_owner_turns = jax.random.permutation(jax.random.fold_in(key_of[3], 3), (N_GX * N_GY * NT) // NT)
    tile_owner = jax.vmap(lambda own, number: deal_out(jax.random.fold_in(key_of[3], 2), own, number, NT, N_GX * N_GY, 1, CAP, 2))(tile_owner_keys, tile_owner_turns).reshape((N_GX * N_GY * NT, 1))
    tile_slot = place_ends(jax.random.randint(key_of[4], (N_GX * N_GY * NT,), 0, SLOTS), jax.random.fold_in(key_of[4], 1), 0, SLOTS - 1).astype(jnp.int32)
    face_mask = place_ends((jax.random.randint(key_of[5], (N_GX * N_GY * NT, 128), 0, 4) < 3).astype(jnp.int32), jax.random.fold_in(key_of[5], 1), 0, 1)
    heights = scatter_about(key_of[6], (3, N_GX * N_GY * SLOTS, 128), 1.0, 6.0, ((1, 128),), jnp.float32)
    return {"grad_pressure": grad_pressure, "beta": beta, "tile_rows": tile_rows, "tile_owner": tile_owner, "tile_slot": tile_slot, "face_mask": face_mask, "heights": heights}


LOW_BOUND = 0.1
HIGH_BOUND = 1.9


def omega_of(step_index):
    theta = 0.5 * (HIGH_BOUND + LOW_BOUND) + 0.5 * (HIGH_BOUND - LOW_BOUND) * math.cos(math.pi * (2 * step_index + 1) / (2 * STEPS))
    return 1.0 / theta


def shifted_low(field, axis_number):
    first = jnp.zeros_like(jnp.take(field, jnp.arange(1), axis=axis_number))
    rest = jnp.take(field, jnp.arange(field.shape[axis_number] - 1), axis=axis_number)
    return jnp.concatenate([first, rest], axis=axis_number)


def reference(grad_pressure, beta, tile_rows, tile_owner, tile_slot, face_mask, heights):
    beta_x, beta_y, beta_z = beta[0], beta[1], beta[2]
    low_x = shifted_low(beta_x, 0)
    low_y = shifted_low(beta_y, 1)
    low_z = shifted_low(beta_z, 2)
    diagonal = beta_x + low_x + beta_y + low_y + beta_z + low_z
    inv_diag = 1.0 / diagonal

    def operate(field):
        padded = jnp.pad(field, 1)
        inner = padded[1:-1, 1:-1, 1:-1]
        beside = beta_x * padded[2:, 1:-1, 1:-1] + low_x * padded[:-2, 1:-1, 1:-1]
        beside = beside + beta_y * padded[1:-1, 2:, 1:-1] + low_y * padded[1:-1, :-2, 1:-1]
        beside = beside + beta_z * padded[1:-1, 1:-1, 2:] + low_z * padded[1:-1, 1:-1, :-2]
        return diagonal * inner - beside

    adjoint = grad_pressure
    grad_rhs = jnp.zeros_like(grad_pressure)
    for cycle_index in range(ITERS):
        for step_index in reversed(range(STEPS)):
            scaled = omega_of(step_index) * inv_diag * adjoint
            grad_rhs = grad_rhs + scaled
            adjoint = adjoint - operate(scaled)

    peers = N_GX * N_GY
    blocks = NZ // 128
    device = jnp.arange(peers * NT, dtype=jnp.int32) // NT
    index_x = device // N_GY
    index_y = device % N_GY
    local_x = tile_rows // (CY * blocks)
    local_y = (tile_rows // blocks) % CY
    block_z = tile_rows % blocks
    grid_rows = grad_rhs.reshape(NX, NY, blocks, 128)
    picked = grid_rows[index_x * CX + local_x, index_y * CY + local_y, block_z]
    jump = face_mask.astype(jnp.float32) * picked
    global_slot = (tile_owner[:, 0] * SLOTS + tile_slot).astype(jnp.int32)
    table = jnp.zeros((peers * SLOTS, 128), jnp.float32).at[global_slot].add(jump)

    slope = 0.5 * (heights[2] - heights[0])
    bend = heights[2] - 2.0 * heights[1] + heights[0]
    denom = 1.0 + slope * slope
    factor = denom ** -1.5
    skew_term = -3.0 * slope * bend * denom ** -2.5
    grad_heights = jnp.stack([table * (factor - 0.5 * skew_term), -2.0 * table * factor, table * (factor + 0.5 * skew_term)])
    return grad_rhs, grad_heights
```

```python
import functools
import math

import jax
import jax.numpy as jnp
from jax import lax
from jax.experimental import pallas as pl
from jax.experimental.pallas import tpu as pltpu
from jax.sharding import PartitionSpec as P

STEPS = 4
CAP = 8
LOW_BOUND = 0.1
HIGH_BOUND = 1.9

ROUNDS = (3, 4, 4)
K = max(ROUNDS)
C = K - 1
NX, NY = 8, 32
EX, EY = NX + 2 * K, NY + 2 * K
TILE = (8, 128)
ANY = pl.BlockSpec(memory_space=pl.ANY)
SMEM = pl.BlockSpec(memory_space=pltpu.SMEM)
VMEM = pl.BlockSpec(memory_space=pltpu.VMEM)
F32 = jnp.float32
MIB = 1 << 20


def omega_of(step):
    j = STEPS - 1 - step % STEPS
    theta = 0.5 * (HIGH_BOUND + LOW_BOUND) + 0.5 * (HIGH_BOUND - LOW_BOUND) * math.cos(
        math.pi * (2 * j + 1) / (2 * STEPS)
    )
    return 1.0 / theta


def rows_shape(*lead):
    return jax.ShapeDtypeStruct((*lead, *TILE), F32)


def z_up(v):
    r = pltpu.roll(v, 127, 2)
    lane = lax.broadcasted_iota(jnp.int32, v.shape, 2)
    return jnp.where(lane == 127, pltpu.roll(r, 7, 1), r)


def z_down(v):
    r = pltpu.roll(v, 1, 2)
    lane = lax.broadcasted_iota(jnp.int32, v.shape, 2)
    return jnp.where(lane == 0, pltpu.roll(r, 1, 1), r)


class Sides:
    def __init__(self):
        self.above = {
            (axis, ab): (lax.axis_index(axis) % 2) == (0 if ab == "a" else 1)
            for axis in ("gx", "gy")
            for ab in ("a", "b")
        }

    def send(self, axis, ab, n):
        return jnp.where(self.above[axis, ab], (NX if axis == "gx" else NY) - n, 0)

    def land(self, axis, ab, n):
        return jnp.where(self.above[axis, ab], K + (NX if axis == "gx" else NY), K - n)


class Copies:
    def __init__(self, sems):
        self.sems = sems
        self.all = []

    def start(self, src, dst):
        copy = pltpu.make_async_copy(src, dst, self.sems.at[len(self.all)])
        copy.start()
        self.all.append(copy)

    def wait(self):
        for copy in self.all:
            copy.wait()


def fields_of(k):
    return (("g", k, k), ("bx", k + 1, k), ("by", k, k + 1), ("bz", k, k))


def pack_kernel(k, g, beta, g_rows, b_rows, xa, xb, ya, yb, nat, rows, in_sems, out_sems):
    sides = Sides()
    copies = []
    for x in range(NX):
        copies.append(
            (
                pltpu.make_async_copy(g.at[x], nat.at[0, x], in_sems.at[0, x]),
                pltpu.make_async_copy(beta.at[:, x], nat.at[1:4, x], in_sems.at[1, x]),
            )
        )
        for c in copies[-1]:
            c.start()
    flat = rows.reshape(4 * NX * NY * 8, 128)
    for x in range(NX):
        for c in copies[x]:
            c.wait()

        @pl.loop(0, 4)
        def _(a, x=x):
            for yc in range(0, NY, 8):
                for s in range(8):
                    at = ((a * NX + x) * NY + yc) * 8 + s
                    flat[pl.ds(at, 8, stride=8), :] = nat[a, x, yc : yc + 8, 128 * s : 128 * s + 128]

    out = Copies(out_sems)
    for axis, ab, strip in (("gy", "a", ya), ("gy", "b", yb), ("gx", "b", xb), ("gx", "a", xa)):
        at = 0
        for i, (_, in_x, in_y) in enumerate(fields_of(k)):
            n = in_x if axis == "gx" else in_y
            first = sides.send(axis, ab, n)
            if axis == "gx":
                out.start(rows.at[i, pl.ds(first, n)], strip.at[at : at + n])
            else:
                out.start(rows.at[i, :, pl.ds(first, n)], strip.at[:, at : at + n])
            at += n
    out.start(rows.at[0], g_rows)
    out.start(rows.at[1:4], b_rows)
    out.wait()


def pack(k, g, beta):
    n = 4 * k + 1
    return pl.pallas_call(
        functools.partial(pack_kernel, k),
        out_shape=(
            rows_shape(NX, NY),
            rows_shape(3, NX, NY),
            rows_shape(n, NY),
            rows_shape(n, NY),
            rows_shape(NX, n),
            rows_shape(NX, n),
        ),
        in_specs=[ANY] * 2,
        out_specs=(ANY,) * 6,
        scratch_shapes=[
            pltpu.VMEM((4, NX, NY, 1024), F32),
            pltpu.VMEM((4, NX, NY, *TILE), F32),
            pltpu.SemaphoreType.DMA((2, NX)),
            pltpu.SemaphoreType.DMA((18,)),
        ],
        compiler_params=pltpu.CompilerParams(vmem_limit_bytes=12 * MIB),
        name="pack",
    )(g, beta)


def corner_kernel(planes, ya, yb, ca, cb, sems):
    sides = Sides()
    out = Copies(sems)
    for ab, corner in (("b", cb), ("a", ca)):
        first = sides.send("gx", ab, planes)
        out.start(ya.at[pl.ds(first, planes)], corner.at[0])
        out.start(yb.at[pl.ds(first, planes)], corner.at[1])
    out.wait()


def corners(planes, ya, yb):
    shape = rows_shape(2, planes, ya.shape[1])
    return pl.pallas_call(
        functools.partial(corner_kernel, planes),
        out_shape=(shape, shape),
        in_specs=[ANY] * 2,
        out_specs=(ANY,) * 2,
        scratch_shapes=[pltpu.SemaphoreType.DMA((4,))],
        compiler_params=pltpu.CompilerParams(vmem_limit_bytes=MIB),
        name="corners",
    )(ya, yb)


def swap(array, axis, ab):
    size = lax.axis_size(axis)
    pairs = [(i, i ^ 1 if ab == "a" else ((i + 1) ^ 1) - 1) for i in range(size)]
    return lax.ppermute(array, axis, [(i, j) for i, j in pairs if 0 <= j < size])


def exchange(planes, xa, xb, ya, yb):
    ya, yb = swap(ya, "gy", "a"), swap(yb, "gy", "b")
    xb, xa = swap(xb, "gx", "b"), swap(xa, "gx", "a")
    ca, cb = corners(planes, ya, yb)
    cb, ca = swap(cb, "gx", "b"), swap(ca, "gx", "a")
    return xa, xb, ya, yb, ca, cb


def land_first(k, sides, into, g_rows, b_rows, xs, ys, cs, fields):
    for i, field in enumerate(fields):
        src = g_rows if i == 0 else b_rows.at[i - 1]
        into.start(src, field.at[K : K + NX, K : K + NY])
    at_x = at_y = 0
    for i, (_, in_x, in_y) in enumerate(fields_of(k)):
        for ab in ("a", "b"):
            x, y = sides.land("gx", ab, in_x), sides.land("gy", ab, in_y)
            into.start(xs[ab].at[at_x : at_x + in_x], fields[i].at[pl.ds(x, in_x), K : K + NY])
            into.start(ys[ab].at[:, at_y : at_y + in_y], fields[i].at[K : K + NX, pl.ds(y, in_y)])
            x = sides.land("gx", ab, k)
            for j, other in enumerate(("a", "b")):
                y = sides.land("gy", other, in_y)
                into.start(
                    cs[ab].at[j, :, at_y : at_y + in_y],
                    fields[i].at[pl.ds(x, k), pl.ds(y, in_y)],
                )
        at_x, at_y = at_x + in_x, at_y + in_y


def land_later(k, sides, into, w_rows, xs, ys, cs, w):
    into.start(w_rows, w.at[K : K + NX, K : K + NY])
    for ab in ("a", "b"):
        x, y = sides.land("gx", ab, k), sides.land("gy", ab, k)
        into.start(xs[ab], w.at[pl.ds(x, k), K : K + NY])
        into.start(ys[ab], w.at[K : K + NX, pl.ds(y, k)])
        x = sides.land("gx", ab, k - 1)
        for j, other in enumerate(("a", "b")):
            y = sides.land("gy", other, k)
            into.start(cs[ab].at[j], w.at[pl.ds(x, k - 1), pl.ds(y, k)])


def chunks(low, high, size=8):
    return [(y, min(size, high - y)) for y in range(low, high, size)]


def scale(w, bx, by, bz, inv):
    @pl.loop(K - C, K + NX + C)
    def _(x):
        for y, n in chunks(K - C, K + NY + C):
            b = bz[x, y : y + n]
            sub = lax.broadcasted_iota(jnp.int32, b.shape, 1)
            lane = lax.broadcasted_iota(jnp.int32, b.shape, 2)
            inner = jnp.where((sub == 7) & (lane == 127), 0.0, b)
            beside = by[x, y - 1 : y + n]
            diagonal = bx[x, y : y + n] + bx[x - 1, y : y + n] + beside[1:] + beside[:-1] + b + z_down(inner)
            inverse = jnp.where(b > 0.0, 1.0 / jnp.where(b > 0.0, diagonal, 1.0), 0.0)
            inv[x, y : y + n] = inverse
            w[x, y : y + n] = w[x, y : y + n] * inverse
            bz[x, y : y + n] = inner


def one_step(step, reach, last, w, new, bx, by, bz, inv, acc):
    omega = omega_of(step)

    def run(x, y, n, inside):
        around = w[x, y - 1 : y + n + 1]
        centre = around[1:-1]
        beside = by[x, y - 1 : y + n]
        along = bz[x, y : y + n]
        total = bx[x, y : y + n] * w[x + 1, y : y + n] + bx[x - 1, y : y + n] * w[x - 1, y : y + n]
        total = total + beside[1:] * around[2:] + beside[:-1] * around[:-2]
        total = total + along * z_up(centre) + z_down(along * centre)
        moved = centre + omega * (inv[x, y : y + n] * total - centre)
        if not last:
            new[x, y : y + n] = moved
        if inside:
            at = (x - K, slice(y - K, y - K + n))
            term = omega * centre
            if last:
                term = term + omega_of(step + 1) * moved
            acc[at] = term if step == 0 else acc[at] + term

    if reach:

        @pl.loop(0, 2 * reach)
        def _(i):
            x = jnp.where(i < reach, K - reach + i, K + NX - reach + i)
            for y, n in chunks(K - reach, K + NY + reach):
                run(x, y, n, False)

    @pl.loop(K, K + NX)
    def _(x):
        if reach:
            run(x, K - reach, reach, False)
            run(x, K + NY, reach, False)
        for y, n in chunks(K, K + NY):
            run(x, y, n, True)


def steps_of(first, k, last, w, bx, by, bz, inv, acc):
    for i in range(k):
        end = last and i == k - 1
        one_step(first + i, k - 1 - i, end, w[i % 2], w[1 - i % 2], bx, by, bz, inv, acc)
    return w[k % 2]


def leave(k, sides, out, w, w_rows, xa, xb, ya, yb):
    for axis, ab, strip in (("gy", "a", ya), ("gy", "b", yb), ("gx", "b", xb), ("gx", "a", xa)):
        first = sides.send(axis, ab, k) + K
        if axis == "gx":
            out.start(w.at[pl.ds(first, k), K : K + NY], strip)
        else:
            out.start(w.at[K : K + NX, pl.ds(first, k)], strip)
    out.start(w.at[K : K + NX, K : K + NY], w_rows)


def first_kernel(
    k, k_next,
    g_rows, b_rows, xa, xb, ya, yb, ca, cb,
    bx_out, by_out, bz_out, inv_out, acc_out, w_out, xa_out, xb_out, ya_out, yb_out,
    w0, w1, bx, by, bz, inv, acc, in_sems, out_sems,
):
    sides = Sides()
    into = Copies(in_sems)
    land_first(k, sides, into, g_rows, b_rows, {"a": xa, "b": xb}, {"a": ya, "b": yb}, {"a": ca, "b": cb}, (w0, bx, by, bz))
    into.wait()
    scale(w0, bx, by, bz, inv)
    out = Copies(out_sems)
    for src, dst in ((bx, bx_out), (by, by_out), (bz, bz_out), (inv, inv_out)):
        out.start(src, dst)
    w = steps_of(0, k, False, (w0, w1), bx, by, bz, inv, acc)
    leave(k_next, sides, out, w, w_out, xa_out, xb_out, ya_out, yb_out)
    out.start(acc, acc_out)
    out.wait()


EXT = pltpu.VMEM((EX, EY, *TILE), F32)
ACC = pltpu.VMEM((NX, NY, *TILE), F32)


def first_round(k, k_next, *arrays):
    ext, core = rows_shape(EX, EY), rows_shape(NX, NY)
    x, y = rows_shape(k_next, NY), rows_shape(NX, k_next)
    return pl.pallas_call(
        functools.partial(first_kernel, k, k_next),
        out_shape=(ext,) * 4 + (core, core, x, x, y, y),
        in_specs=[ANY] * 8,
        out_specs=(ANY,) * 10,
        scratch_shapes=[EXT] * 6 + [ACC, pltpu.SemaphoreType.DMA((36,)), pltpu.SemaphoreType.DMA((10,))],
        compiler_params=pltpu.CompilerParams(vmem_limit_bytes=22 * MIB),
        name="first_round",
    )(*arrays)


def later_kernel(
    first, k, k_next,
    bx_in, by_in, bz_in, inv_in, acc_in, w_in, xa, xb, ya, yb, ca, cb,
    acc_out, w_out, xa_out, xb_out, ya_out, yb_out,
    w0, w1, bx, by, bz, inv, acc, in_sems, out_sems,
):
    sides = Sides()
    into = Copies(in_sems)
    for src, dst in ((bx_in, bx), (by_in, by), (bz_in, bz), (inv_in, inv), (acc_in, acc)):
        into.start(src, dst)
    land_later(k, sides, into, w_in, {"a": xa, "b": xb}, {"a": ya, "b": yb}, {"a": ca, "b": cb}, w0)
    into.wait()
    w = steps_of(first, k, False, (w0, w1), bx, by, bz, inv, acc)
    out = Copies(out_sems)
    leave(k_next, sides, out, w, w_out, xa_out, xb_out, ya_out, yb_out)
    out.start(acc, acc_out)
    out.wait()


def later_round(first, k, k_next, *arrays):
    core = rows_shape(NX, NY)
    x, y = rows_shape(k_next, NY), rows_shape(NX, k_next)
    return pl.pallas_call(
        functools.partial(later_kernel, first, k, k_next),
        out_shape=(core, core, x, x, y, y),
        in_specs=[ANY] * 12,
        out_specs=(ANY,) * 6,
        scratch_shapes=[EXT] * 6 + [ACC, pltpu.SemaphoreType.DMA((14,)), pltpu.SemaphoreType.DMA((6,))],
        compiler_params=pltpu.CompilerParams(vmem_limit_bytes=22 * MIB),
        name="later_round",
    )(*arrays)


def last_kernel(
    first, k,
    tile_rows, targets, mask, slots,
    bx_in, by_in, bz_in, inv_in, acc_in, w_in, xa, xb, ya, yb, ca, cb,
    grad, sent,
    w0, w1, bx, by, bz, inv, acc, in_sems,
):
    sides = Sides()
    into = Copies(in_sems)
    for src, dst in ((bx_in, bx), (by_in, by), (bz_in, bz), (inv_in, inv), (acc_in, acc)):
        into.start(src, dst)
    land_later(k, sides, into, w_in, {"a": xa, "b": xb}, {"a": ya, "b": yb}, {"a": ca, "b": cb}, w0)
    sent[...] = jnp.zeros_like(sent)
    peers = slots.shape[0]
    sent[pl.ds(CAP, peers, stride=CAP + 1), :] = slots[...]
    into.wait()
    steps_of(first, k, True, (w0, w1), bx, by, bz, inv, acc)
    flat = acc.reshape(NX * NY * 8, 128)

    @pl.loop(0, mask.shape[0] // 8)
    def _(t8):
        for t in range(8):
            at = t8 * 8 + t
            row = flat[pl.ds(tile_rows[at], 1), :] * mask[pl.ds(at, 1), :].astype(F32)
            sent[pl.ds(targets[at], 1), :] = row

    @pl.loop(0, NX)
    def _(x):
        for yc in range(0, NY, 8):
            for s in range(8):
                at = (x * NY + yc) * 8 + s
                grad[x, yc : yc + 8, 128 * s : 128 * s + 128] = flat[pl.ds(at, 8, stride=8), :]


def last_round(first, k, peers, *arrays):
    return pl.pallas_call(
        functools.partial(last_kernel, first, k),
        out_shape=(
            jax.ShapeDtypeStruct((NX, NY, 1024), F32),
            jax.ShapeDtypeStruct((peers * (CAP + 1), 128), F32),
        ),
        in_specs=[SMEM, SMEM, VMEM, VMEM] + [ANY] * 12,
        out_specs=(VMEM, VMEM),
        scratch_shapes=[EXT] * 6 + [ACC, pltpu.SemaphoreType.DMA((14,))],
        compiler_params=pltpu.CompilerParams(vmem_limit_bytes=26 * MIB),
        name="last_round",
    )(*arrays)


def finish_kernel(received, heights, out):
    peers = received.shape[0] // (CAP + 1)
    slots = received[pl.ds(CAP, peers, stride=CAP + 1), :].T
    n_slots = heights.shape[1]
    ids = lax.broadcasted_iota(jnp.int32, (n_slots, peers), 0).astype(F32)
    table = jnp.zeros((n_slots, 128), F32)
    for p in range(CAP):
        named = (ids == slots[p : p + 1, :]).astype(jnp.bfloat16)
        rest = received[pl.ds(p, peers, stride=CAP + 1), :]
        for _ in range(3):
            part = rest.astype(jnp.bfloat16)
            rest = rest - part.astype(F32)
            table = table + jnp.dot(named, part, preferred_element_type=F32)
    slope = 0.5 * (heights[2] - heights[0])
    bend = heights[2] - 2.0 * heights[1] + heights[0]
    denom = 1.0 + slope * slope
    factor = 1.0 / (denom * jnp.sqrt(denom))
    skew_half = -1.5 * slope * bend * factor / denom
    out[0] = table * (factor - skew_half)
    out[1] = -2.0 * table * factor
    out[2] = table * (factor + skew_half)


def finish(received, heights):
    return pl.pallas_call(
        finish_kernel,
        out_shape=jax.ShapeDtypeStruct(heights.shape, F32),
        in_specs=[VMEM, VMEM],
        out_specs=VMEM,
        compiler_params=pltpu.CompilerParams(vmem_limit_bytes=8 * MIB),
        name="finish",
    )(received, heights)


def routes(tile_owner, tile_slot, peers):
    owner = tile_owner[:, 0]
    order = jnp.arange(owner.shape[0])
    before = (owner[:, None] == owner[None, :]) & (order[None, :] < order[:, None])
    position = jnp.sum(before.astype(jnp.int32), axis=1)
    is_owner = (owner[None, :] == jnp.arange(peers)[:, None]).astype(F32)
    placed = jnp.where(position[:, None] == jnp.arange(128)[None, :], tile_slot[:, None].astype(F32), 0.0)
    slots = jnp.dot(is_owner, placed, precision=lax.Precision.HIGHEST)
    return owner * (CAP + 1) + position, slots


def shards(grad_pressure, beta, tile_rows, tile_owner, tile_slot, face_mask, heights):
    peers = lax.axis_size("gx") * lax.axis_size("gy")
    targets, slots = routes(tile_owner, tile_slot, peers)
    k = ROUNDS[0]
    g_rows, b_rows, *strips = pack(k, grad_pressure, beta)
    out = first_round(k, ROUNDS[1], g_rows, b_rows, *exchange(k, *strips))
    coeffs, state, strips = out[:4], out[4:6], out[6:]
    done = k
    for k, k_next in zip(ROUNDS[1:-1], ROUNDS[2:]):
        out = later_round(done, k, k_next, *coeffs, *state, *exchange(k - 1, *strips))
        state, strips = out[:2], out[2:]
        done += k
    k = ROUNDS[-1]
    grad_rhs, sent = last_round(
        done, k, peers, tile_rows, targets, face_mask, slots, *coeffs, *state, *exchange(k - 1, *strips)
    )
    sent = sent.reshape(peers, 1, (CAP + 1) * 128)
    received = lax.all_to_all(sent, ("gx", "gy"), split_axis=0, concat_axis=0, tiled=True)
    return grad_rhs, finish(received.reshape(peers * (CAP + 1), 128), heights)


def solution(mesh):
    in_specs = (
        P("gx", "gy", None),
        P(None, "gx", "gy", None),
        P(("gx", "gy")),
        P(("gx", "gy"), None),
        P(("gx", "gy")),
        P(("gx", "gy"), None),
        P(None, ("gx", "gy"), None),
    )
    out_specs = (P("gx", "gy", None), P(None, ("gx", "gy"), None))
    return jax.shard_map(shards, mesh=mesh, in_specs=in_specs, out_specs=out_specs, check_vma=False)
```

```python
import functools
import math

import jax
import jax.numpy as jnp
from jax import lax
from jax.experimental import pallas as pl
from jax.experimental.pallas import tpu as pltpu
from jax.sharding import PartitionSpec as P

STEPS = 4
CAP = 8
LOW_BOUND = 0.1
HIGH_BOUND = 1.9

ROUNDS = (3, 4, 4)
K = max(ROUNDS)
C = K - 1
NX, NY = 8, 32
EX, EY = NX + 2 * K, NY + 2 * K
TILE = (8, 128)
ANY = pl.BlockSpec(memory_space=pl.ANY)
SMEM = pl.BlockSpec(memory_space=pltpu.SMEM)
VMEM = pl.BlockSpec(memory_space=pltpu.VMEM)
HBM = pl.BlockSpec(memory_space=pltpu.HBM)
F32 = jnp.float32
MIB = 1 << 20
EXT = pltpu.VMEM((EX, EY, *TILE), F32)
ACC = pltpu.VMEM((NX, NY, *TILE), F32)


def omega_of(step):
    j = STEPS - 1 - step % STEPS
    theta = 0.5 * (HIGH_BOUND + LOW_BOUND) + 0.5 * (HIGH_BOUND - LOW_BOUND) * math.cos(
        math.pi * (2 * j + 1) / (2 * STEPS)
    )
    return 1.0 / theta


def rows_shape(*lead):
    return jax.ShapeDtypeStruct((*lead, *TILE), F32)


def z_up(v):
    r = pltpu.roll(v, 127, 2)
    lane = lax.broadcasted_iota(jnp.int32, v.shape, 2)
    return jnp.where(lane == 127, pltpu.roll(r, 7, 1), r)


def z_down(v):
    r = pltpu.roll(v, 1, 2)
    lane = lax.broadcasted_iota(jnp.int32, v.shape, 2)
    return jnp.where(lane == 0, pltpu.roll(r, 1, 1), r)


class Sides:
    def __init__(self):
        self.above = {
            (axis, ab): (lax.axis_index(axis) % 2) == (0 if ab == "a" else 1)
            for axis in ("gx", "gy")
            for ab in ("a", "b")
        }

    def send(self, axis, ab, n):
        return jnp.where(self.above[axis, ab], (NX if axis == "gx" else NY) - n, 0)

    def land(self, axis, ab, n):
        return jnp.where(self.above[axis, ab], K + (NX if axis == "gx" else NY), K - n)


class Copies:
    def __init__(self, sems):
        self.sems = sems
        self.all = []

    def start(self, src, dst):
        copy = pltpu.make_async_copy(src, dst, self.sems.at[len(self.all)])
        copy.start()
        self.all.append(copy)

    def wait(self):
        for copy in self.all:
            copy.wait()


def fields_of(k):
    return (("g", k, k), ("bx", k + 1, k), ("by", k, k + 1), ("bz", k, k))


def pack_kernel(k, g, beta, w, bx, by, bz, xa, xb, ya, yb, nat, in_sems, out_sems):
    sides = Sides()
    copies = []
    for x in range(NX):
        copies.append(
            (
                pltpu.make_async_copy(g.at[x], nat.at[0, x], in_sems.at[0, x]),
                pltpu.make_async_copy(beta.at[:, x], nat.at[1:4, x], in_sems.at[1, x]),
            )
        )
        for c in copies[-1]:
            c.start()
    fields = (w, bx, by, bz)
    for x in range(NX):
        for c in copies[x]:
            c.wait()
        for a, field in enumerate(fields):
            flat = field.reshape(EX * EY * 8, 128)

            @pl.loop(0, NY // 8)
            def _(yc, x=x, a=a, flat=flat):
                y = pl.multiple_of(yc * 8, 8)
                for s in range(8):
                    at = ((x + K) * EY + K + y) * 8 + s
                    flat[pl.ds(at, 8, stride=8), :] = nat[a, x, pl.ds(y, 8), 128 * s : 128 * s + 128]

    out = Copies(out_sems)
    for axis, ab, strip in (("gy", "a", ya), ("gy", "b", yb), ("gx", "b", xb), ("gx", "a", xa)):
        at = 0
        for field, (_, in_x, in_y) in zip(fields, fields_of(k)):
            n = in_x if axis == "gx" else in_y
            first = sides.send(axis, ab, n) + K
            if axis == "gx":
                out.start(field.at[pl.ds(first, n), K : K + NY], strip.at[at : at + n])
            else:
                out.start(field.at[K : K + NX, pl.ds(first, n)], strip.at[:, at : at + n])
            at += n
    out.wait()


def pack(k, g, beta):
    n = 4 * k + 1
    return pl.pallas_call(
        functools.partial(pack_kernel, k),
        out_shape=(EXT,) * 4 + (rows_shape(n, NY), rows_shape(n, NY), rows_shape(NX, n), rows_shape(NX, n)),
        in_specs=[HBM] * 2,
        out_specs=(VMEM,) * 4 + (ANY,) * 4,
        scratch_shapes=[
            pltpu.VMEM((4, NX, NY, 1024), F32),
            pltpu.SemaphoreType.DMA((2, NX)),
            pltpu.SemaphoreType.DMA((16,)),
        ],
        compiler_params=pltpu.CompilerParams(vmem_limit_bytes=8 * MIB),
        name="pack",
    )(*(pltpu.with_memory_space_constraint(array, pltpu.HBM) for array in (g, beta)))


def corner_kernel(planes, ya, yb, ca, cb, sems):
    sides = Sides()
    out = Copies(sems)
    for ab, corner in (("b", cb), ("a", ca)):
        first = sides.send("gx", ab, planes)
        out.start(ya.at[pl.ds(first, planes)], corner.at[0])
        out.start(yb.at[pl.ds(first, planes)], corner.at[1])
    out.wait()


def corners(planes, ya, yb):
    shape = rows_shape(2, planes, ya.shape[1])
    return pl.pallas_call(
        functools.partial(corner_kernel, planes),
        out_shape=(shape, shape),
        in_specs=[ANY] * 2,
        out_specs=(ANY,) * 2,
        scratch_shapes=[pltpu.SemaphoreType.DMA((4,))],
        compiler_params=pltpu.CompilerParams(vmem_limit_bytes=MIB),
        name="corners",
    )(ya, yb)


def swap(array, axis, ab):
    size = lax.axis_size(axis)
    pairs = [(i, i ^ 1 if ab == "a" else ((i + 1) ^ 1) - 1) for i in range(size)]
    return lax.ppermute(array, axis, [(i, j) for i, j in pairs if 0 <= j < size])


def exchange(planes, xa, xb, ya, yb):
    ya, yb = swap(ya, "gy", "a"), swap(yb, "gy", "b")
    xb, xa = swap(xb, "gx", "b"), swap(xa, "gx", "a")
    ca, cb = corners(planes, ya, yb)
    cb, ca = swap(cb, "gx", "b"), swap(ca, "gx", "a")
    return xa, xb, ya, yb, ca, cb


def land_first(k, sides, into, xs, ys, cs, fields):
    at_x = at_y = 0
    for i, (_, in_x, in_y) in enumerate(fields_of(k)):
        for ab in ("a", "b"):
            x, y = sides.land("gx", ab, in_x), sides.land("gy", ab, in_y)
            into.start(xs[ab].at[at_x : at_x + in_x], fields[i].at[pl.ds(x, in_x), K : K + NY])
            into.start(ys[ab].at[:, at_y : at_y + in_y], fields[i].at[K : K + NX, pl.ds(y, in_y)])
            x = sides.land("gx", ab, k)
            for j, other in enumerate(("a", "b")):
                y = sides.land("gy", other, in_y)
                into.start(
                    cs[ab].at[j, :, at_y : at_y + in_y],
                    fields[i].at[pl.ds(x, k), pl.ds(y, in_y)],
                )
        at_x, at_y = at_x + in_x, at_y + in_y


def land_later(k, sides, into, xs, ys, cs, w):
    for ab in ("a", "b"):
        x, y = sides.land("gx", ab, k), sides.land("gy", ab, k)
        into.start(xs[ab], w.at[pl.ds(x, k), K : K + NY])
        into.start(ys[ab], w.at[K : K + NX, pl.ds(y, k)])
        x = sides.land("gx", ab, k - 1)
        for j, other in enumerate(("a", "b")):
            y = sides.land("gy", other, k)
            into.start(cs[ab].at[j], w.at[pl.ds(x, k - 1), pl.ds(y, k)])


def chunks(low, high, size=8):
    return [(y, min(size, high - y)) for y in range(low, high, size)]


def scale(w, bx, by, bz, inv):
    @pl.loop(K - C, K + NX + C)
    def _(x):
        for y, n in chunks(K - C, K + NY + C):
            b = bz[x, y : y + n]
            sub = lax.broadcasted_iota(jnp.int32, b.shape, 1)
            lane = lax.broadcasted_iota(jnp.int32, b.shape, 2)
            inner = jnp.where((sub == 7) & (lane == 127), 0.0, b)
            beside = by[x, y - 1 : y + n]
            diagonal = bx[x, y : y + n] + bx[x - 1, y : y + n] + beside[1:] + beside[:-1] + b + z_down(inner)
            inverse = jnp.where(b > 0.0, 1.0 / jnp.where(b > 0.0, diagonal, 1.0), 0.0)
            inv[x, y : y + n] = inverse
            w[x, y : y + n] = w[x, y : y + n] * inverse
            bz[x, y : y + n] = inner


def one_step(step, reach, last, w, new, bx, by, bz, inv, acc):
    omega = omega_of(step)

    def run(x, y, n, inside):
        around = w[x, y - 1 : y + n + 1]
        centre = around[1:-1]
        beside = by[x, y - 1 : y + n]
        along = bz[x, y : y + n]
        total = bx[x, y : y + n] * w[x + 1, y : y + n] + bx[x - 1, y : y + n] * w[x - 1, y : y + n]
        total = total + beside[1:] * around[2:] + beside[:-1] * around[:-2]
        total = total + along * z_up(centre) + z_down(along * centre)
        moved = centre + omega * (inv[x, y : y + n] * total - centre)
        if not last:
            new[x, y : y + n] = moved
        if inside:
            at = (x - K, slice(y - K, y - K + n))
            term = omega * centre
            if last:
                term = term + omega_of(step + 1) * moved
            acc[at] = term if step == 0 else acc[at] + term

    if reach:

        @pl.loop(0, 2 * reach)
        def _(i):
            x = jnp.where(i < reach, K - reach + i, K + NX - reach + i)
            for y, n in chunks(K - reach, K + NY + reach):
                run(x, y, n, False)

    @pl.loop(K, K + NX)
    def _(x):
        if reach:
            run(x, K - reach, reach, False)
            run(x, K + NY, reach, False)
        for y, n in chunks(K, K + NY):
            run(x, y, n, True)


def steps_of(first, k, last, w, bx, by, bz, inv, acc):
    for i in range(k):
        end = last and i == k - 1
        one_step(first + i, k - 1 - i, end, w[i % 2], w[1 - i % 2], bx, by, bz, inv, acc)
    return w[k % 2]


def leave(k, sides, out, w, xa, xb, ya, yb):
    for axis, ab, strip in (("gy", "a", ya), ("gy", "b", yb), ("gx", "b", xb), ("gx", "a", xa)):
        first = sides.send(axis, ab, k) + K
        if axis == "gx":
            out.start(w.at[pl.ds(first, k), K : K + NY], strip)
        else:
            out.start(w.at[K : K + NX, pl.ds(first, k)], strip)


def first_kernel(
    k, k_next,
    w_in, bx_in, by_in, bz_in, xa, xb, ya, yb, ca, cb,
    w0, bx, by, bz, inv, acc, w1, xa_out, xb_out, ya_out, yb_out,
    in_sems, out_sems,
):
    sides = Sides()
    into = Copies(in_sems)
    land_first(k, sides, into, {"a": xa, "b": xb}, {"a": ya, "b": yb}, {"a": ca, "b": cb}, (w0, bx, by, bz))
    into.wait()
    scale(w0, bx, by, bz, inv)
    w = steps_of(0, k, False, (w0, w1), bx, by, bz, inv, acc)
    out = Copies(out_sems)
    leave(k_next, sides, out, w, xa_out, xb_out, ya_out, yb_out)
    out.wait()


def strips_shape(k):
    x, y = rows_shape(k, NY), rows_shape(NX, k)
    return (x, x, y, y)


def first_round(k, k_next, *arrays):
    assert k % 2 == 1
    _, bx, by, bz, inv, acc, w, *strips = pl.pallas_call(
        functools.partial(first_kernel, k, k_next),
        out_shape=(EXT,) * 5 + (ACC, EXT) + strips_shape(k_next),
        in_specs=[VMEM] * 4 + [ANY] * 6,
        out_specs=(VMEM,) * 7 + (ANY,) * 4,
        scratch_shapes=[pltpu.SemaphoreType.DMA((32,)), pltpu.SemaphoreType.DMA((4,))],
        input_output_aliases={i: i for i in range(4)},
        compiler_params=pltpu.CompilerParams(vmem_limit_bytes=2 * MIB),
        name="first_round",
    )(*arrays)
    return (bx, by, bz, inv), (w, acc), strips


def later_kernel(
    first, k, k_next,
    bx, by, bz, inv, w_in, acc_in, xa, xb, ya, yb, ca, cb,
    w0, acc, xa_out, xb_out, ya_out, yb_out,
    w1, in_sems, out_sems,
):
    sides = Sides()
    into = Copies(in_sems)
    land_later(k, sides, into, {"a": xa, "b": xb}, {"a": ya, "b": yb}, {"a": ca, "b": cb}, w0)
    into.wait()
    w = steps_of(first, k, False, (w0, w1), bx, by, bz, inv, acc)
    out = Copies(out_sems)
    leave(k_next, sides, out, w, xa_out, xb_out, ya_out, yb_out)
    out.wait()


def later_round(first, k, k_next, *arrays):
    assert k % 2 == 0
    w, acc, *strips = pl.pallas_call(
        functools.partial(later_kernel, first, k, k_next),
        out_shape=(EXT, ACC) + strips_shape(k_next),
        in_specs=[VMEM] * 6 + [ANY] * 6,
        out_specs=(VMEM,) * 2 + (ANY,) * 4,
        scratch_shapes=[EXT, pltpu.SemaphoreType.DMA((8,)), pltpu.SemaphoreType.DMA((4,))],
        input_output_aliases={4: 0, 5: 1},
        compiler_params=pltpu.CompilerParams(vmem_limit_bytes=6 * MIB),
        name="later_round",
    )(*arrays)
    return (w, acc), strips


def last_kernel(
    first, k,
    tile_rows, targets, mask, slots, bx, by, bz, inv, w_in, acc_in, xa, xb, ya, yb, ca, cb,
    grad, sent, w0, acc,
    w1, in_sems,
):
    sides = Sides()
    into = Copies(in_sems)
    land_later(k, sides, into, {"a": xa, "b": xb}, {"a": ya, "b": yb}, {"a": ca, "b": cb}, w0)
    sent[...] = jnp.zeros_like(sent)
    peers = slots.shape[0]
    sent[pl.ds(CAP, peers, stride=CAP + 1), :] = slots[...]
    into.wait()
    steps_of(first, k, True, (w0, w1), bx, by, bz, inv, acc)
    flat = acc.reshape(NX * NY * 8, 128)

    @pl.loop(0, mask.shape[0] // 8)
    def _(t8):
        for t in range(8):
            at = t8 * 8 + t
            row = flat[pl.ds(tile_rows[at], 1), :] * mask[pl.ds(at, 1), :].astype(F32)
            sent[pl.ds(targets[at], 1), :] = row

    @pl.loop(0, NX)
    def _(x):
        for yc in range(0, NY, 8):
            for s in range(8):
                at = (x * NY + yc) * 8 + s
                grad[x, yc : yc + 8, 128 * s : 128 * s + 128] = flat[pl.ds(at, 8, stride=8), :]


def last_round(first, k, peers, *arrays):
    return pl.pallas_call(
        functools.partial(last_kernel, first, k),
        out_shape=(
            jax.ShapeDtypeStruct((NX, NY, 1024), F32),
            jax.ShapeDtypeStruct((peers * (CAP + 1), 128), F32),
            EXT,
            ACC,
        ),
        in_specs=[SMEM, SMEM] + [VMEM] * 8 + [ANY] * 6,
        out_specs=(VMEM,) * 4,
        scratch_shapes=[EXT, pltpu.SemaphoreType.DMA((8,))],
        input_output_aliases={8: 2, 9: 3},
        compiler_params=pltpu.CompilerParams(vmem_limit_bytes=10 * MIB),
        name="last_round",
    )(*arrays)[:2]


def finish_kernel(received, heights, out):
    peers = received.shape[0] // (CAP + 1)
    slots = received[pl.ds(CAP, peers, stride=CAP + 1), :].T
    n_slots = heights.shape[1]
    ids = lax.broadcasted_iota(jnp.int32, (n_slots, peers), 0).astype(F32)
    table = jnp.zeros((n_slots, 128), F32)
    for p in range(CAP):
        named = (ids == slots[p : p + 1, :]).astype(jnp.bfloat16)
        rest = received[pl.ds(p, peers, stride=CAP + 1), :]
        for _ in range(3):
            part = rest.astype(jnp.bfloat16)
            rest = rest - part.astype(F32)
            table = table + jnp.dot(named, part, preferred_element_type=F32)
    slope = 0.5 * (heights[2] - heights[0])
    bend = heights[2] - 2.0 * heights[1] + heights[0]
    denom = 1.0 + slope * slope
    factor = 1.0 / (denom * jnp.sqrt(denom))
    skew_half = -1.5 * slope * bend * factor / denom
    out[0] = table * (factor - skew_half)
    out[1] = -2.0 * table * factor
    out[2] = table * (factor + skew_half)


def finish(received, heights):
    return pl.pallas_call(
        finish_kernel,
        out_shape=jax.ShapeDtypeStruct(heights.shape, F32),
        in_specs=[VMEM, VMEM],
        out_specs=VMEM,
        compiler_params=pltpu.CompilerParams(vmem_limit_bytes=8 * MIB),
        name="finish",
    )(received, heights)


def routes(tile_owner, tile_slot, peers):
    owner = tile_owner[:, 0]
    order = jnp.arange(owner.shape[0])
    before = (owner[:, None] == owner[None, :]) & (order[None, :] < order[:, None])
    position = jnp.sum(before.astype(jnp.int32), axis=1)
    is_owner = (owner[None, :] == jnp.arange(peers)[:, None]).astype(F32)
    placed = jnp.where(position[:, None] == jnp.arange(128)[None, :], tile_slot[:, None].astype(F32), 0.0)
    slots = jnp.dot(is_owner, placed, precision=lax.Precision.HIGHEST)
    return owner * (CAP + 1) + position, slots


def shards(grad_pressure, beta, tile_rows, tile_owner, tile_slot, face_mask, heights):
    peers = lax.axis_size("gx") * lax.axis_size("gy")
    targets, slots = routes(tile_owner, tile_slot, peers)
    k = ROUNDS[0]
    packed = pack(k, grad_pressure, beta)
    coeffs, state, strips = first_round(k, ROUNDS[1], *packed[:4], *exchange(k, *packed[4:]))
    done = k
    for k, k_next in zip(ROUNDS[1:-1], ROUNDS[2:]):
        state, strips = later_round(done, k, k_next, *coeffs, *state, *exchange(k - 1, *strips))
        done += k
    k = ROUNDS[-1]
    grad_rhs, sent = last_round(
        done, k, peers, tile_rows, targets, face_mask, slots, *coeffs, *state, *exchange(k - 1, *strips)
    )
    sent = sent.reshape(peers, 1, (CAP + 1) * 128)
    received = lax.all_to_all(sent, ("gx", "gy"), split_axis=0, concat_axis=0, tiled=True)
    return grad_rhs, finish(received.reshape(peers * (CAP + 1), 128), heights)


def solution(mesh):
    in_specs = (
        P("gx", "gy", None),
        P(None, "gx", "gy", None),
        P(("gx", "gy")),
        P(("gx", "gy"), None),
        P(("gx", "gy")),
        P(("gx", "gy"), None),
        P(None, ("gx", "gy"), None),
    )
    out_specs = (P("gx", "gy", None), P(None, ("gx", "gy"), None))
    return jax.shard_map(shards, mesh=mesh, in_specs=in_specs, out_specs=out_specs, check_vma=False)
```

```python
import functools
import math

import jax
import jax.numpy as jnp
from jax import lax
from jax.experimental import pallas as pl
from jax.experimental.pallas import tpu as pltpu
from jax.sharding import PartitionSpec as P

STEPS = 4
CAP = 8
LOW_BOUND = 0.1
HIGH_BOUND = 1.9

ROUNDS = (3, 4, 4)
K = max(ROUNDS)
C = K - 1
NX, NY = 8, 32
EX, EY = NX + 2 * K, NY + 2 * K
TILE = (8, 128)
ANY = pl.BlockSpec(memory_space=pl.ANY)
SMEM = pl.BlockSpec(memory_space=pltpu.SMEM)
VMEM = pl.BlockSpec(memory_space=pltpu.VMEM)
HBM = pl.BlockSpec(memory_space=pltpu.HBM)
F32 = jnp.float32
MIB = 1 << 20
EXT = pltpu.VMEM((EX, EY, *TILE), F32)
ACC = pltpu.VMEM((NX, NY, *TILE), F32)


def omega_of(step):
    j = STEPS - 1 - step % STEPS
    theta = 0.5 * (HIGH_BOUND + LOW_BOUND) + 0.5 * (HIGH_BOUND - LOW_BOUND) * math.cos(
        math.pi * (2 * j + 1) / (2 * STEPS)
    )
    return 1.0 / theta


def rows_shape(*lead):
    return jax.ShapeDtypeStruct((*lead, *TILE), F32)


def z_up(v):
    r = pltpu.roll(v, 127, 2)
    lane = lax.broadcasted_iota(jnp.int32, v.shape, 2)
    return jnp.where(lane == 127, pltpu.roll(r, 7, 1), r)


def z_down(v):
    r = pltpu.roll(v, 1, 2)
    lane = lax.broadcasted_iota(jnp.int32, v.shape, 2)
    return jnp.where(lane == 0, pltpu.roll(r, 1, 1), r)


class Sides:
    def __init__(self):
        self.above = {
            (axis, ab): (lax.axis_index(axis) % 2) == (0 if ab == "a" else 1)
            for axis in ("gx", "gy")
            for ab in ("a", "b")
        }

    def send(self, axis, ab, n):
        return jnp.where(self.above[axis, ab], (NX if axis == "gx" else NY) - n, 0)

    def land(self, axis, ab, n):
        return jnp.where(self.above[axis, ab], K + (NX if axis == "gx" else NY), K - n)


class Copies:
    def __init__(self, sems):
        self.sems = sems
        self.all = []

    def start(self, src, dst):
        copy = pltpu.make_async_copy(src, dst, self.sems.at[len(self.all)])
        copy.start()
        self.all.append(copy)

    def wait(self):
        for copy in self.all:
            copy.wait()


def fields_of(k):
    return (("g", k, k), ("bx", k + 1, k), ("by", k, k + 1), ("bz", k, k))


def pack_kernel(k, g, beta, w, bx, by, bz, xa, xb, ya, yb, nat, in_sems, out_sems):
    sides = Sides()
    copies = []
    for x in range(NX):
        copies.append(
            (
                pltpu.make_async_copy(g.at[x], nat.at[0, x], in_sems.at[0, x]),
                pltpu.make_async_copy(beta.at[:, x], nat.at[1:4, x], in_sems.at[1, x]),
            )
        )
        for c in copies[-1]:
            c.start()
    fields = (w, bx, by, bz)
    for x in range(NX):
        for c in copies[x]:
            c.wait()
        for a, field in enumerate(fields):
            flat = field.reshape(EX * EY * 8, 128)

            @pl.loop(0, NY // 8)
            def _(yc, x=x, a=a, flat=flat):
                y = pl.multiple_of(yc * 8, 8)
                for s in range(8):
                    at = ((x + K) * EY + K + y) * 8 + s
                    flat[pl.ds(at, 8, stride=8), :] = nat[a, x, pl.ds(y, 8), 128 * s : 128 * s + 128]

    out = Copies(out_sems)
    for axis, ab, strip in (("gy", "a", ya), ("gy", "b", yb), ("gx", "b", xb), ("gx", "a", xa)):
        at = 0
        for field, (_, in_x, in_y) in zip(fields, fields_of(k)):
            n = in_x if axis == "gx" else in_y
            first = sides.send(axis, ab, n) + K
            if axis == "gx":
                out.start(field.at[pl.ds(first, n), K : K + NY], strip.at[at : at + n])
            else:
                out.start(field.at[K : K + NX, pl.ds(first, n)], strip.at[:, at : at + n])
            at += n
    out.wait()


def pack(k, g, beta):
    n = 4 * k + 1
    return pl.pallas_call(
        functools.partial(pack_kernel, k),
        out_shape=(EXT,) * 4 + (rows_shape(n, NY), rows_shape(n, NY), rows_shape(NX, n), rows_shape(NX, n)),
        in_specs=[HBM] * 2,
        out_specs=(VMEM,) * 4 + (ANY,) * 4,
        scratch_shapes=[
            pltpu.VMEM((4, NX, NY, 1024), F32),
            pltpu.SemaphoreType.DMA((2, NX)),
            pltpu.SemaphoreType.DMA((16,)),
        ],
        compiler_params=pltpu.CompilerParams(vmem_limit_bytes=8 * MIB),
        name="pack",
    )(*(pltpu.with_memory_space_constraint(array, pltpu.HBM) for array in (g, beta)))


def corner_kernel(planes, ya, yb, ca, cb, sems):
    sides = Sides()
    out = Copies(sems)
    for ab, corner in (("b", cb), ("a", ca)):
        first = sides.send("gx", ab, planes)
        out.start(ya.at[pl.ds(first, planes)], corner.at[0])
        out.start(yb.at[pl.ds(first, planes)], corner.at[1])
    out.wait()


def corners(planes, ya, yb):
    shape = rows_shape(2, planes, ya.shape[1])
    return pl.pallas_call(
        functools.partial(corner_kernel, planes),
        out_shape=(shape, shape),
        in_specs=[ANY] * 2,
        out_specs=(ANY,) * 2,
        scratch_shapes=[pltpu.SemaphoreType.DMA((4,))],
        compiler_params=pltpu.CompilerParams(vmem_limit_bytes=MIB),
        cost_estimate=pl.CostEstimate(flops=10**12, bytes_accessed=MIB, transcendentals=0),
        name="corners",
    )(ya, yb)


def swap(array, axis, ab):
    size = lax.axis_size(axis)
    pairs = [(i, i ^ 1 if ab == "a" else ((i + 1) ^ 1) - 1) for i in range(size)]
    return lax.ppermute(array, axis, [(i, j) for i, j in pairs if 0 <= j < size])


def exchange(planes, xa, xb, ya, yb):
    ya, yb = swap(ya, "gy", "a"), swap(yb, "gy", "b")
    xb, xa = swap(xb, "gx", "b"), swap(xa, "gx", "a")
    ca, cb = corners(planes, ya, yb)
    cb, ca = swap(cb, "gx", "b"), swap(ca, "gx", "a")
    return xa, xb, ya, yb, ca, cb


def land_first(k, sides, into, xs, ys, cs, fields):
    at_x = at_y = 0
    for i, (_, in_x, in_y) in enumerate(fields_of(k)):
        for ab in ("a", "b"):
            x, y = sides.land("gx", ab, in_x), sides.land("gy", ab, in_y)
            into.start(xs[ab].at[at_x : at_x + in_x], fields[i].at[pl.ds(x, in_x), K : K + NY])
            into.start(ys[ab].at[:, at_y : at_y + in_y], fields[i].at[K : K + NX, pl.ds(y, in_y)])
            x = sides.land("gx", ab, k)
            for j, other in enumerate(("a", "b")):
                y = sides.land("gy", other, in_y)
                into.start(
                    cs[ab].at[j, :, at_y : at_y + in_y],
                    fields[i].at[pl.ds(x, k), pl.ds(y, in_y)],
                )
        at_x, at_y = at_x + in_x, at_y + in_y


def land_later(k, sides, into, xs, ys, cs, w):
    for ab in ("a", "b"):
        x, y = sides.land("gx", ab, k), sides.land("gy", ab, k)
        into.start(xs[ab], w.at[pl.ds(x, k), K : K + NY])
        into.start(ys[ab], w.at[K : K + NX, pl.ds(y, k)])
        x = sides.land("gx", ab, k - 1)
        for j, other in enumerate(("a", "b")):
            y = sides.land("gy", other, k)
            into.start(cs[ab].at[j], w.at[pl.ds(x, k - 1), pl.ds(y, k)])


def chunks(low, high, size=8):
    return [(y, min(size, high - y)) for y in range(low, high, size)]


def scale(w, bx, by, bz, inv):
    @pl.loop(K - C, K + NX + C)
    def _(x):
        for y, n in chunks(K - C, K + NY + C):
            b = bz[x, y : y + n]
            sub = lax.broadcasted_iota(jnp.int32, b.shape, 1)
            lane = lax.broadcasted_iota(jnp.int32, b.shape, 2)
            inner = jnp.where((sub == 7) & (lane == 127), 0.0, b)
            beside = by[x, y - 1 : y + n]
            diagonal = bx[x, y : y + n] + bx[x - 1, y : y + n] + beside[1:] + beside[:-1] + b + z_down(inner)
            inverse = jnp.where(b > 0.0, 1.0 / jnp.where(b > 0.0, diagonal, 1.0), 0.0)
            inv[x, y : y + n] = inverse
            w[x, y : y + n] = w[x, y : y + n] * inverse
            bz[x, y : y + n] = inner


def one_step(step, reach, last, w, new, bx, by, bz, inv, acc):
    omega = omega_of(step)

    def run(x, y, n, inside):
        around = w[x, y - 1 : y + n + 1]
        centre = around[1:-1]
        beside = by[x, y - 1 : y + n]
        along = bz[x, y : y + n]
        total = bx[x, y : y + n] * w[x + 1, y : y + n] + bx[x - 1, y : y + n] * w[x - 1, y : y + n]
        total = total + beside[1:] * around[2:] + beside[:-1] * around[:-2]
        total = total + along * z_up(centre) + z_down(along * centre)
        moved = centre + omega * (inv[x, y : y + n] * total - centre)
        if not last:
            new[x, y : y + n] = moved
        if inside:
            at = (x - K, slice(y - K, y - K + n))
            term = omega * centre
            if last:
                term = term + omega_of(step + 1) * moved
            acc[at] = term if step == 0 else acc[at] + term

    if reach:

        @pl.loop(0, 2 * reach)
        def _(i):
            x = jnp.where(i < reach, K - reach + i, K + NX - reach + i)
            for y, n in chunks(K - reach, K + NY + reach):
                run(x, y, n, False)

    @pl.loop(K, K + NX)
    def _(x):
        if reach:
            run(x, K - reach, reach, False)
            run(x, K + NY, reach, False)
        for y, n in chunks(K, K + NY):
            run(x, y, n, True)


def steps_of(first, k, last, w, bx, by, bz, inv, acc):
    for i in range(k):
        end = last and i == k - 1
        one_step(first + i, k - 1 - i, end, w[i % 2], w[1 - i % 2], bx, by, bz, inv, acc)
    return w[k % 2]


def leave(k, sides, out, w, xa, xb, ya, yb):
    for axis, ab, strip in (("gy", "a", ya), ("gy", "b", yb), ("gx", "b", xb), ("gx", "a", xa)):
        first = sides.send(axis, ab, k) + K
        if axis == "gx":
            out.start(w.at[pl.ds(first, k), K : K + NY], strip)
        else:
            out.start(w.at[K : K + NX, pl.ds(first, k)], strip)


def first_kernel(
    k, k_next,
    w_in, bx_in, by_in, bz_in, xa, xb, ya, yb, ca, cb,
    w0, bx, by, bz, inv, acc, w1, xa_out, xb_out, ya_out, yb_out,
    in_sems, out_sems,
):
    sides = Sides()
    into = Copies(in_sems)
    land_first(k, sides, into, {"a": xa, "b": xb}, {"a": ya, "b": yb}, {"a": ca, "b": cb}, (w0, bx, by, bz))
    into.wait()
    scale(w0, bx, by, bz, inv)
    w = steps_of(0, k, False, (w0, w1), bx, by, bz, inv, acc)
    out = Copies(out_sems)
    leave(k_next, sides, out, w, xa_out, xb_out, ya_out, yb_out)
    out.wait()


def strips_shape(k):
    x, y = rows_shape(k, NY), rows_shape(NX, k)
    return (x, x, y, y)


def first_round(k, k_next, *arrays):
    assert k % 2 == 1
    _, bx, by, bz, inv, acc, w, *strips = pl.pallas_call(
        functools.partial(first_kernel, k, k_next),
        out_shape=(EXT,) * 5 + (ACC, EXT) + strips_shape(k_next),
        in_specs=[VMEM] * 4 + [ANY] * 6,
        out_specs=(VMEM,) * 7 + (ANY,) * 4,
        scratch_shapes=[pltpu.SemaphoreType.DMA((32,)), pltpu.SemaphoreType.DMA((4,))],
        input_output_aliases={i: i for i in range(4)},
        compiler_params=pltpu.CompilerParams(vmem_limit_bytes=2 * MIB),
        name="first_round",
    )(*arrays)
    return (bx, by, bz, inv), (w, acc), strips


def later_kernel(
    first, k, k_next,
    bx, by, bz, inv, w_in, acc_in, xa, xb, ya, yb, ca, cb,
    w0, acc, xa_out, xb_out, ya_out, yb_out,
    w1, in_sems, out_sems,
):
    sides = Sides()
    into = Copies(in_sems)
    land_later(k, sides, into, {"a": xa, "b": xb}, {"a": ya, "b": yb}, {"a": ca, "b": cb}, w0)
    into.wait()
    w = steps_of(first, k, False, (w0, w1), bx, by, bz, inv, acc)
    out = Copies(out_sems)
    leave(k_next, sides, out, w, xa_out, xb_out, ya_out, yb_out)
    out.wait()


def later_round(first, k, k_next, *arrays):
    assert k % 2 == 0
    w, acc, *strips = pl.pallas_call(
        functools.partial(later_kernel, first, k, k_next),
        out_shape=(EXT, ACC) + strips_shape(k_next),
        in_specs=[VMEM] * 6 + [ANY] * 6,
        out_specs=(VMEM,) * 2 + (ANY,) * 4,
        scratch_shapes=[EXT, pltpu.SemaphoreType.DMA((8,)), pltpu.SemaphoreType.DMA((4,))],
        input_output_aliases={4: 0, 5: 1},
        compiler_params=pltpu.CompilerParams(vmem_limit_bytes=6 * MIB),
        name="later_round",
    )(*arrays)
    return (w, acc), strips


def last_kernel(
    first, k,
    tile_rows, targets, mask, slots, bx, by, bz, inv, w_in, acc_in, xa, xb, ya, yb, ca, cb,
    grad, sent, w0, acc,
    w1, in_sems,
):
    sides = Sides()
    into = Copies(in_sems)
    land_later(k, sides, into, {"a": xa, "b": xb}, {"a": ya, "b": yb}, {"a": ca, "b": cb}, w0)
    sent[...] = jnp.zeros_like(sent)
    peers = slots.shape[0]
    sent[pl.ds(CAP, peers, stride=CAP + 1), :] = slots[...]
    into.wait()
    steps_of(first, k, True, (w0, w1), bx, by, bz, inv, acc)
    flat = acc.reshape(NX * NY * 8, 128)

    @pl.loop(0, mask.shape[0] // 8)
    def _(t8):
        for t in range(8):
            at = t8 * 8 + t
            row = flat[pl.ds(tile_rows[at], 1), :] * mask[pl.ds(at, 1), :].astype(F32)
            sent[pl.ds(targets[at], 1), :] = row

    @pl.loop(0, NX)
    def _(x):
        for yc in range(0, NY, 8):
            for s in range(8):
                at = (x * NY + yc) * 8 + s
                grad[x, yc : yc + 8, 128 * s : 128 * s + 128] = flat[pl.ds(at, 8, stride=8), :]


def last_round(first, k, peers, *arrays):
    return pl.pallas_call(
        functools.partial(last_kernel, first, k),
        out_shape=(
            jax.ShapeDtypeStruct((NX, NY, 1024), F32),
            jax.ShapeDtypeStruct((peers * (CAP + 1), 128), F32),
            EXT,
            ACC,
        ),
        in_specs=[SMEM, SMEM] + [VMEM] * 8 + [ANY] * 6,
        out_specs=(VMEM,) * 4,
        scratch_shapes=[EXT, pltpu.SemaphoreType.DMA((8,))],
        input_output_aliases={8: 2, 9: 3},
        compiler_params=pltpu.CompilerParams(vmem_limit_bytes=10 * MIB),
        name="last_round",
    )(*arrays)[:2]


def finish_kernel(received, heights, out):
    peers = received.shape[0] // (CAP + 1)
    slots = received[pl.ds(CAP, peers, stride=CAP + 1), :].T
    n_slots = heights.shape[1]
    ids = lax.broadcasted_iota(jnp.int32, (n_slots, peers), 0).astype(F32)
    table = jnp.zeros((n_slots, 128), F32)
    for p in range(CAP):
        named = (ids == slots[p : p + 1, :]).astype(jnp.bfloat16)
        rest = received[pl.ds(p, peers, stride=CAP + 1), :]
        for _ in range(3):
            part = rest.astype(jnp.bfloat16)
            rest = rest - part.astype(F32)
            table = table + jnp.dot(named, part, preferred_element_type=F32)
    slope = 0.5 * (heights[2] - heights[0])
    bend = heights[2] - 2.0 * heights[1] + heights[0]
    denom = 1.0 + slope * slope
    factor = 1.0 / (denom * jnp.sqrt(denom))
    skew_half = -1.5 * slope * bend * factor / denom
    out[0] = table * (factor - skew_half)
    out[1] = -2.0 * table * factor
    out[2] = table * (factor + skew_half)


def finish(received, heights):
    return pl.pallas_call(
        finish_kernel,
        out_shape=jax.ShapeDtypeStruct(heights.shape, F32),
        in_specs=[VMEM, VMEM],
        out_specs=VMEM,
        compiler_params=pltpu.CompilerParams(vmem_limit_bytes=8 * MIB),
        name="finish",
    )(received, heights)


def routes(tile_owner, tile_slot, peers):
    owner = tile_owner[:, 0]
    order = jnp.arange(owner.shape[0])
    before = (owner[:, None] == owner[None, :]) & (order[None, :] < order[:, None])
    position = jnp.sum(before.astype(jnp.int32), axis=1)
    is_owner = (owner[None, :] == jnp.arange(peers)[:, None]).astype(F32)
    placed = jnp.where(position[:, None] == jnp.arange(128)[None, :], tile_slot[:, None].astype(F32), 0.0)
    slots = jnp.dot(is_owner, placed, precision=lax.Precision.HIGHEST)
    return owner * (CAP + 1) + position, slots


def shards(grad_pressure, beta, tile_rows, tile_owner, tile_slot, face_mask, heights):
    peers = lax.axis_size("gx") * lax.axis_size("gy")
    targets, slots = routes(tile_owner, tile_slot, peers)
    k = ROUNDS[0]
    packed = pack(k, grad_pressure, beta)
    coeffs, state, strips = first_round(k, ROUNDS[1], *packed[:4], *exchange(k, *packed[4:]))
    done = k
    for k, k_next in zip(ROUNDS[1:-1], ROUNDS[2:]):
        state, strips = later_round(done, k, k_next, *coeffs, *state, *exchange(k - 1, *strips))
        done += k
    k = ROUNDS[-1]
    grad_rhs, sent = last_round(
        done, k, peers, tile_rows, targets, face_mask, slots, *coeffs, *state, *exchange(k - 1, *strips)
    )
    sent = sent.reshape(peers, 1, (CAP + 1) * 128)
    received = lax.all_to_all(sent, ("gx", "gy"), split_axis=0, concat_axis=0, tiled=True)
    return grad_rhs, finish(received.reshape(peers * (CAP + 1), 128), heights)


def solution(mesh):
    in_specs = (
        P("gx", "gy", None),
        P(None, "gx", "gy", None),
        P(("gx", "gy")),
        P(("gx", "gy"), None),
        P(("gx", "gy")),
        P(("gx", "gy"), None),
        P(None, ("gx", "gy"), None),
    )
    out_specs = (P("gx", "gy", None), P(None, ("gx", "gy"), None))
    return jax.shard_map(shards, mesh=mesh, in_specs=in_specs, out_specs=out_specs, check_vma=False)
```

```python
import functools
import math

import jax
import jax.numpy as jnp
from jax import lax
from jax.experimental import pallas as pl
from jax.experimental.pallas import tpu as pltpu
from jax.sharding import PartitionSpec as P

STEPS = 4
CAP = 8
LOW_BOUND = 0.1
HIGH_BOUND = 1.9

ROUNDS = (3, 4, 4)
K = max(ROUNDS)
C = K - 1
NX, NY = 8, 32
EX, EY = NX + 2 * K, NY + 2 * K
TILE = (8, 128)
ANY = pl.BlockSpec(memory_space=pl.ANY)
SMEM = pl.BlockSpec(memory_space=pltpu.SMEM)
VMEM = pl.BlockSpec(memory_space=pltpu.VMEM)
HBM = pl.BlockSpec(memory_space=pltpu.HBM)
F32 = jnp.float32
MIB = 1 << 20
EXT = pltpu.VMEM((EX, EY, *TILE), F32)
ACC = pltpu.VMEM((NX, NY, *TILE), F32)


def omega_of(step):
    j = STEPS - 1 - step % STEPS
    theta = 0.5 * (HIGH_BOUND + LOW_BOUND) + 0.5 * (HIGH_BOUND - LOW_BOUND) * math.cos(
        math.pi * (2 * j + 1) / (2 * STEPS)
    )
    return 1.0 / theta


def rows_shape(*lead):
    return jax.ShapeDtypeStruct((*lead, *TILE), F32)


def z_up(v):
    r = pltpu.roll(v, 127, 2)
    lane = lax.broadcasted_iota(jnp.int32, v.shape, 2)
    return jnp.where(lane == 127, pltpu.roll(r, 7, 1), r)


def z_down(v):
    r = pltpu.roll(v, 1, 2)
    lane = lax.broadcasted_iota(jnp.int32, v.shape, 2)
    return jnp.where(lane == 0, pltpu.roll(r, 1, 1), r)


class Sides:
    def __init__(self):
        self.above = {
            (axis, ab): (lax.axis_index(axis) % 2) == (0 if ab == "a" else 1)
            for axis in ("gx", "gy")
            for ab in ("a", "b")
        }

    def send(self, axis, ab, n):
        return jnp.where(self.above[axis, ab], (NX if axis == "gx" else NY) - n, 0)

    def land(self, axis, ab, n):
        return jnp.where(self.above[axis, ab], K + (NX if axis == "gx" else NY), K - n)


class Copies:
    def __init__(self, sems):
        self.sems = sems
        self.all = []

    def start(self, src, dst):
        copy = pltpu.make_async_copy(src, dst, self.sems.at[len(self.all)])
        copy.start()
        self.all.append(copy)

    def wait(self):
        for copy in self.all:
            copy.wait()


def fields_of(k):
    return ((k, k, k - 1), (k + 1, k, k), (k, k + 1, k), (k, k, k - 1))


def pack_kernel(k, g, beta, w, bx, by, bz, xa, xb, ya, yb, nat, in_sems, out_sems):
    sides = Sides()
    copies = []
    for x in range(NX):
        copies.append(
            (
                pltpu.make_async_copy(g.at[x], nat.at[0, x], in_sems.at[0, x]),
                pltpu.make_async_copy(beta.at[:, x], nat.at[1:4, x], in_sems.at[1, x]),
            )
        )
        for c in copies[-1]:
            c.start()
    fields = (w, bx, by, bz)
    for x in range(NX):
        for c in copies[x]:
            c.wait()
        for a, field in enumerate(fields):
            flat = field.reshape(EX * EY * 8, 128)

            @pl.loop(0, NY // 8)
            def _(yc, x=x, a=a, flat=flat):
                y = pl.multiple_of(yc * 8, 8)
                for s in range(8):
                    at = ((x + K) * EY + K + y) * 8 + s
                    flat[pl.ds(at, 8, stride=8), :] = nat[a, x, pl.ds(y, 8), 128 * s : 128 * s + 128]

    out = Copies(out_sems)
    for axis, ab, strip in (("gy", "a", ya), ("gy", "b", yb), ("gx", "b", xb), ("gx", "a", xa)):
        at = 0
        for field, (in_x, in_y, _) in zip(fields, fields_of(k)):
            n = in_x if axis == "gx" else in_y
            first = sides.send(axis, ab, n) + K
            if axis == "gx":
                out.start(field.at[pl.ds(first, n), K : K + NY], strip.at[at : at + n])
            else:
                out.start(field.at[K : K + NX, pl.ds(first, n)], strip.at[:, at : at + n])
            at += n
    out.wait()


def pack(k, g, beta):
    n = 4 * k + 1
    return pl.pallas_call(
        functools.partial(pack_kernel, k),
        out_shape=(EXT,) * 4 + (rows_shape(n, NY), rows_shape(n, NY), rows_shape(NX, n), rows_shape(NX, n)),
        in_specs=[HBM] * 2,
        out_specs=(VMEM,) * 4 + (ANY,) * 4,
        scratch_shapes=[
            pltpu.VMEM((4, NX, NY, 1024), F32),
            pltpu.SemaphoreType.DMA((2, NX)),
            pltpu.SemaphoreType.DMA((16,)),
        ],
        compiler_params=pltpu.CompilerParams(vmem_limit_bytes=8 * MIB),
        name="pack",
    )(*(pltpu.with_memory_space_constraint(array, pltpu.HBM) for array in (g, beta)))


def corner_kernel(planes, counts, ya, yb, ca, cb, sems):
    sides = Sides()
    out = Copies(sems)
    for ab, corner in (("b", cb), ("a", ca)):
        first = sides.send("gx", ab, planes)
        for j, (other, strip) in enumerate((("a", ya), ("b", yb))):
            at = done = 0
            for n, kept in counts:
                skip = jnp.where(sides.above["gy", other], 0, n - kept)
                out.start(
                    strip.at[pl.ds(first, planes), pl.ds(at + skip, kept)],
                    corner.at[j, :, done : done + kept],
                )
                at, done = at + n, done + kept
    out.wait()


def corners(planes, counts, ya, yb):
    shape = rows_shape(2, planes, sum(kept for _, kept in counts))
    return pl.pallas_call(
        functools.partial(corner_kernel, planes, counts),
        out_shape=(shape, shape),
        in_specs=[ANY] * 2,
        out_specs=(ANY,) * 2,
        scratch_shapes=[pltpu.SemaphoreType.DMA((4 * len(counts),))],
        compiler_params=pltpu.CompilerParams(vmem_limit_bytes=MIB),
        cost_estimate=pl.CostEstimate(flops=10**10, bytes_accessed=MIB, transcendentals=0),
        name="corners",
    )(ya, yb)


def swap(array, axis, ab):
    size = lax.axis_size(axis)
    pairs = [(i, i ^ 1 if ab == "a" else ((i + 1) ^ 1) - 1) for i in range(size)]
    return lax.ppermute(array, axis, [(i, j) for i, j in pairs if 0 <= j < size])


def exchange(planes, counts, xa, xb, ya, yb):
    ya, yb = swap(ya, "gy", "a"), swap(yb, "gy", "b")
    xb, xa = swap(xb, "gx", "b"), swap(xa, "gx", "a")
    ca, cb = corners(planes, counts, ya, yb)
    cb, ca = swap(cb, "gx", "b"), swap(ca, "gx", "a")
    return xa, xb, ya, yb, ca, cb


def land_first(k, sides, into, xs, ys, cs, fields):
    at_x = at_y = at_c = 0
    for i, (in_x, in_y, in_c) in enumerate(fields_of(k)):
        for ab in ("a", "b"):
            x, y = sides.land("gx", ab, in_x), sides.land("gy", ab, in_y)
            into.start(xs[ab].at[at_x : at_x + in_x], fields[i].at[pl.ds(x, in_x), K : K + NY])
            into.start(ys[ab].at[:, at_y : at_y + in_y], fields[i].at[K : K + NX, pl.ds(y, in_y)])
            x = sides.land("gx", ab, k)
            for j, other in enumerate(("a", "b")):
                y = sides.land("gy", other, in_c)
                into.start(
                    cs[ab].at[j, :, at_c : at_c + in_c],
                    fields[i].at[pl.ds(x, k), pl.ds(y, in_c)],
                )
        at_x, at_y, at_c = at_x + in_x, at_y + in_y, at_c + in_c


def land_later(k, sides, into, xs, ys, cs, w):
    for ab in ("a", "b"):
        x, y = sides.land("gx", ab, k), sides.land("gy", ab, k)
        into.start(xs[ab], w.at[pl.ds(x, k), K : K + NY])
        into.start(ys[ab], w.at[K : K + NX, pl.ds(y, k)])
        x = sides.land("gx", ab, k - 1)
        for j, other in enumerate(("a", "b")):
            y = sides.land("gy", other, k - 1)
            into.start(cs[ab].at[j], w.at[pl.ds(x, k - 1), pl.ds(y, k - 1)])


def chunks(low, high, size=8):
    return [(y, min(size, high - y)) for y in range(low, high, size)]


def scale(w, bx, by, bz, inv):
    @pl.loop(K - C, K + NX + C)
    def _(x):
        for y, n in chunks(K - C, K + NY + C):
            b = bz[x, y : y + n]
            sub = lax.broadcasted_iota(jnp.int32, b.shape, 1)
            lane = lax.broadcasted_iota(jnp.int32, b.shape, 2)
            inner = jnp.where((sub == 7) & (lane == 127), 0.0, b)
            beside = by[x, y - 1 : y + n]
            diagonal = bx[x, y : y + n] + bx[x - 1, y : y + n] + beside[1:] + beside[:-1] + b + z_down(inner)
            inverse = jnp.where(b > 0.0, 1.0 / jnp.where(b > 0.0, diagonal, 1.0), 0.0)
            inv[x, y : y + n] = inverse
            w[x, y : y + n] = w[x, y : y + n] * inverse
            bz[x, y : y + n] = inner


def one_step(step, reach, last, w, new, bx, by, bz, inv, acc):
    omega = omega_of(step)
    low, high = K - reach, K + NX + reach

    def walk(y, n, rows_inside):
        below = bx[low - 1, pl.ds(y, n)] * w[low - 1, pl.ds(y, n)]
        around = w[low, pl.ds(y - 1, n + 2)]
        for x in range(low, high):
            above = w[x + 1, pl.ds(y - 1, n + 2)]
            centre = around[1:-1]
            link = bx[x, pl.ds(y, n)]
            beside = by[x, pl.ds(y - 1, n + 1)]
            along = bz[x, pl.ds(y, n)]
            total = link * above[1:-1] + below
            total = total + beside[1:] * around[2:] + beside[:-1] * around[:-2]
            total = total + along * z_up(centre) + z_down(along * centre)
            moved = centre + omega * (inv[x, pl.ds(y, n)] * total - centre)
            if not last:
                new[x, pl.ds(y, n)] = moved
            if rows_inside and K <= x < K + NX:
                at = (x - K, pl.ds(y - K, n))
                term = omega * centre
                if last:
                    term = term + omega_of(step + 1) * moved
                acc[at] = term if step == 0 else acc[at] + term
            below, around = link * centre, above

    if reach:
        walk(K - reach, reach, False)
        walk(K + NY, reach, False)

    @pl.loop(0, NY // 8)
    def _(i):
        walk(K + i * 8, 8, True)


def steps_of(first, k, last, w, bx, by, bz, inv, acc):
    for i in range(k):
        end = last and i == k - 1
        one_step(first + i, k - 1 - i, end, w[i % 2], w[1 - i % 2], bx, by, bz, inv, acc)
    return w[k % 2]


def leave(k, sides, out, w, xa, xb, ya, yb):
    for axis, ab, strip in (("gy", "a", ya), ("gy", "b", yb), ("gx", "b", xb), ("gx", "a", xa)):
        first = sides.send(axis, ab, k) + K
        if axis == "gx":
            out.start(w.at[pl.ds(first, k), K : K + NY], strip)
        else:
            out.start(w.at[K : K + NX, pl.ds(first, k)], strip)


def first_kernel(
    k, k_next,
    w_in, bx_in, by_in, bz_in, xa, xb, ya, yb, ca, cb,
    w0, bx, by, bz, inv, acc, w1, xa_out, xb_out, ya_out, yb_out,
    in_sems, out_sems,
):
    sides = Sides()
    into = Copies(in_sems)
    land_first(k, sides, into, {"a": xa, "b": xb}, {"a": ya, "b": yb}, {"a": ca, "b": cb}, (w0, bx, by, bz))
    into.wait()
    scale(w0, bx, by, bz, inv)
    w = steps_of(0, k, False, (w0, w1), bx, by, bz, inv, acc)
    out = Copies(out_sems)
    leave(k_next, sides, out, w, xa_out, xb_out, ya_out, yb_out)
    out.wait()


def strips_shape(k):
    x, y = rows_shape(k, NY), rows_shape(NX, k)
    return (x, x, y, y)


def first_round(k, k_next, *arrays):
    assert k % 2 == 1
    _, bx, by, bz, inv, acc, w, *strips = pl.pallas_call(
        functools.partial(first_kernel, k, k_next),
        out_shape=(EXT,) * 5 + (ACC, EXT) + strips_shape(k_next),
        in_specs=[VMEM] * 4 + [ANY] * 6,
        out_specs=(VMEM,) * 7 + (ANY,) * 4,
        scratch_shapes=[pltpu.SemaphoreType.DMA((32,)), pltpu.SemaphoreType.DMA((4,))],
        input_output_aliases={i: i for i in range(4)},
        compiler_params=pltpu.CompilerParams(vmem_limit_bytes=2 * MIB),
        name="first_round",
    )(*arrays)
    return (bx, by, bz, inv), (w, acc), strips


def later_kernel(
    first, k, k_next,
    bx, by, bz, inv, w_in, acc_in, xa, xb, ya, yb, ca, cb,
    w0, acc, xa_out, xb_out, ya_out, yb_out,
    w1, in_sems, out_sems,
):
    sides = Sides()
    into = Copies(in_sems)
    land_later(k, sides, into, {"a": xa, "b": xb}, {"a": ya, "b": yb}, {"a": ca, "b": cb}, w0)
    into.wait()
    w = steps_of(first, k, False, (w0, w1), bx, by, bz, inv, acc)
    out = Copies(out_sems)
    leave(k_next, sides, out, w, xa_out, xb_out, ya_out, yb_out)
    out.wait()


def later_round(first, k, k_next, *arrays):
    assert k % 2 == 0
    w, acc, *strips = pl.pallas_call(
        functools.partial(later_kernel, first, k, k_next),
        out_shape=(EXT, ACC) + strips_shape(k_next),
        in_specs=[VMEM] * 6 + [ANY] * 6,
        out_specs=(VMEM,) * 2 + (ANY,) * 4,
        scratch_shapes=[EXT, pltpu.SemaphoreType.DMA((8,)), pltpu.SemaphoreType.DMA((4,))],
        input_output_aliases={4: 0, 5: 1},
        compiler_params=pltpu.CompilerParams(vmem_limit_bytes=6 * MIB),
        name="later_round",
    )(*arrays)
    return (w, acc), strips


def last_kernel(
    first, k,
    tile_rows, targets, mask, slots, bx, by, bz, inv, w_in, acc_in, xa, xb, ya, yb, ca, cb,
    grad, sent, w0, acc,
    w1, in_sems,
):
    sides = Sides()
    into = Copies(in_sems)
    land_later(k, sides, into, {"a": xa, "b": xb}, {"a": ya, "b": yb}, {"a": ca, "b": cb}, w0)
    sent[...] = jnp.zeros_like(sent)
    peers = slots.shape[0]
    sent[pl.ds(CAP, peers, stride=CAP + 1), :] = slots[...]
    into.wait()
    steps_of(first, k, True, (w0, w1), bx, by, bz, inv, acc)
    flat = acc.reshape(NX * NY * 8, 128)

    @pl.loop(0, mask.shape[0] // 8)
    def _(t8):
        for t in range(8):
            at = t8 * 8 + t
            row = flat[pl.ds(tile_rows[at], 1), :] * mask[pl.ds(at, 1), :].astype(F32)
            sent[pl.ds(targets[at], 1), :] = row

    @pl.loop(0, NX)
    def _(x):
        for yc in range(0, NY, 8):
            for s in range(8):
                at = (x * NY + yc) * 8 + s
                grad[x, yc : yc + 8, 128 * s : 128 * s + 128] = flat[pl.ds(at, 8, stride=8), :]


def last_round(first, k, peers, *arrays):
    return pl.pallas_call(
        functools.partial(last_kernel, first, k),
        out_shape=(
            jax.ShapeDtypeStruct((NX, NY, 1024), F32),
            jax.ShapeDtypeStruct((peers * (CAP + 1), 128), F32),
            EXT,
            ACC,
        ),
        in_specs=[SMEM, SMEM] + [VMEM] * 8 + [ANY] * 6,
        out_specs=(VMEM,) * 4,
        scratch_shapes=[EXT, pltpu.SemaphoreType.DMA((8,))],
        input_output_aliases={8: 2, 9: 3},
        compiler_params=pltpu.CompilerParams(vmem_limit_bytes=10 * MIB),
        name="last_round",
    )(*arrays)[:2]


def finish_kernel(received, heights, out):
    peers = received.shape[0] // (CAP + 1)
    slots = received[pl.ds(CAP, peers, stride=CAP + 1), :].T
    n_slots = heights.shape[1]
    ids = lax.broadcasted_iota(jnp.int32, (n_slots, peers), 0).astype(F32)
    table = jnp.zeros((n_slots, 128), F32)
    for p in range(CAP):
        named = (ids == slots[p : p + 1, :]).astype(jnp.bfloat16)
        rest = received[pl.ds(p, peers, stride=CAP + 1), :]
        for _ in range(3):
            part = rest.astype(jnp.bfloat16)
            rest = rest - part.astype(F32)
            table = table + jnp.dot(named, part, preferred_element_type=F32)
    slope = 0.5 * (heights[2] - heights[0])
    bend = heights[2] - 2.0 * heights[1] + heights[0]
    denom = 1.0 + slope * slope
    factor = 1.0 / (denom * jnp.sqrt(denom))
    skew_half = -1.5 * slope * bend * factor / denom
    out[0] = table * (factor - skew_half)
    out[1] = -2.0 * table * factor
    out[2] = table * (factor + skew_half)


def finish(received, heights):
    return pl.pallas_call(
        finish_kernel,
        out_shape=jax.ShapeDtypeStruct(heights.shape, F32),
        in_specs=[VMEM, VMEM],
        out_specs=VMEM,
        compiler_params=pltpu.CompilerParams(vmem_limit_bytes=8 * MIB),
        name="finish",
    )(received, heights)


def routes(tile_owner, tile_slot, peers):
    owner = tile_owner[:, 0]
    order = jnp.arange(owner.shape[0])
    before = (owner[:, None] == owner[None, :]) & (order[None, :] < order[:, None])
    position = jnp.sum(before.astype(jnp.int32), axis=1)
    is_owner = (owner[None, :] == jnp.arange(peers)[:, None]).astype(F32)
    placed = jnp.where(position[:, None] == jnp.arange(128)[None, :], tile_slot[:, None].astype(F32), 0.0)
    slots = jnp.dot(is_owner, placed, precision=lax.Precision.HIGHEST)
    return owner * (CAP + 1) + position, slots


def shards(grad_pressure, beta, tile_rows, tile_owner, tile_slot, face_mask, heights):
    peers = lax.axis_size("gx") * lax.axis_size("gy")
    targets, slots = routes(tile_owner, tile_slot, peers)
    k = ROUNDS[0]
    packed = pack(k, grad_pressure, beta)
    coeffs, state, strips = first_round(k, ROUNDS[1], *packed[:4], *exchange(k, [f[1:] for f in fields_of(k)], *packed[4:]))
    done = k
    for k, k_next in zip(ROUNDS[1:-1], ROUNDS[2:]):
        state, strips = later_round(done, k, k_next, *coeffs, *state, *exchange(k - 1, [(k, k - 1)], *strips))
        done += k
    k = ROUNDS[-1]
    grad_rhs, sent = last_round(
        done, k, peers, tile_rows, targets, face_mask, slots, *coeffs, *state, *exchange(k - 1, [(k, k - 1)], *strips)
    )
    sent = sent.reshape(peers, 1, (CAP + 1) * 128)
    received = lax.all_to_all(sent, ("gx", "gy"), split_axis=0, concat_axis=0, tiled=True)
    return grad_rhs, finish(received.reshape(peers * (CAP + 1), 128), heights)


def solution(mesh):
    in_specs = (
        P("gx", "gy", None),
        P(None, "gx", "gy", None),
        P(("gx", "gy")),
        P(("gx", "gy"), None),
        P(("gx", "gy")),
        P(("gx", "gy"), None),
        P(None, ("gx", "gy"), None),
    )
    out_specs = (P("gx", "gy", None), P(None, ("gx", "gy"), None))
    return jax.shard_map(shards, mesh=mesh, in_specs=in_specs, out_specs=out_specs, check_vma=False)
```

```python
import functools
import math

import jax
import jax.numpy as jnp
from jax import lax
from jax.experimental import pallas as pl
from jax.experimental.pallas import tpu as pltpu
from jax.sharding import PartitionSpec as P

STEPS = 4
CAP = 8
LOW_BOUND = 0.1
HIGH_BOUND = 1.9

ROUNDS = (3, 4, 4)
K = max(ROUNDS)
C = K - 1
NX, NY = 8, 32
EX, EY = NX + 2 * K, NY + 2 * K
TILE = (8, 128)
ANY = pl.BlockSpec(memory_space=pl.ANY)
SMEM = pl.BlockSpec(memory_space=pltpu.SMEM)
VMEM = pl.BlockSpec(memory_space=pltpu.VMEM)
HBM = pl.BlockSpec(memory_space=pltpu.HBM)
F32 = jnp.float32
MIB = 1 << 20
EXT = pltpu.VMEM((EX, EY, *TILE), F32)
ACC = pltpu.VMEM((NX, NY, *TILE), F32)


def omega_of(step):
    j = STEPS - 1 - step % STEPS
    theta = 0.5 * (HIGH_BOUND + LOW_BOUND) + 0.5 * (HIGH_BOUND - LOW_BOUND) * math.cos(
        math.pi * (2 * j + 1) / (2 * STEPS)
    )
    return 1.0 / theta


def rows_shape(*lead):
    return jax.ShapeDtypeStruct((*lead, *TILE), F32)


def z_up(v):
    r = pltpu.roll(v, 127, 2)
    lane = lax.broadcasted_iota(jnp.int32, v.shape, 2)
    return jnp.where(lane == 127, pltpu.roll(r, 7, 1), r)


def z_down(v):
    r = pltpu.roll(v, 1, 2)
    lane = lax.broadcasted_iota(jnp.int32, v.shape, 2)
    return jnp.where(lane == 0, pltpu.roll(r, 1, 1), r)


class Sides:
    def __init__(self):
        self.above = {
            (axis, ab): (lax.axis_index(axis) % 2) == (0 if ab == "a" else 1)
            for axis in ("gx", "gy")
            for ab in ("a", "b")
        }

    def send(self, axis, ab, n):
        return jnp.where(self.above[axis, ab], (NX if axis == "gx" else NY) - n, 0)

    def land(self, axis, ab, n):
        return jnp.where(self.above[axis, ab], K + (NX if axis == "gx" else NY), K - n)


class Copies:
    def __init__(self, sems):
        self.sems = sems
        self.all = []

    def start(self, src, dst):
        copy = pltpu.make_async_copy(src, dst, self.sems.at[len(self.all)])
        copy.start()
        self.all.append(copy)

    def start_either(self, first, src, other, dst):
        sem = self.sems.at[len(self.all)]
        for wanted, ref in ((first, src), (jnp.logical_not(first), other)):
            copy = pltpu.make_async_copy(ref, dst, sem)
            pl.when(wanted)(copy.start)
        self.all.append(copy)

    def wait(self):
        for copy in self.all:
            copy.wait()


def fields_of(k):
    return ((k, k, k - 1), (k + 1, k, k), (k, k + 1, k), (k, k, k - 1))


def pack_kernel(k, g, beta, w, bx, by, bz, xa, xb, xb_z, ya, yb, nat, in_sems, out_sems):
    sides = Sides()
    copies = []
    for x in range(NX):
        copies.append(
            (
                pltpu.make_async_copy(g.at[x], nat.at[0, x], in_sems.at[0, x]),
                pltpu.make_async_copy(beta.at[:, x], nat.at[1:4, x], in_sems.at[1, x]),
            )
        )
        for c in copies[-1]:
            c.start()
    fields = (w, bx, by, bz)
    for x in range(NX):
        for c in copies[x]:
            c.wait()
        for a, field in enumerate(fields):
            flat = field.reshape(EX * EY * 8, 128)

            @pl.loop(0, NY // 8)
            def _(yc, x=x, a=a, flat=flat):
                y = pl.multiple_of(yc * 8, 8)
                for s in range(8):
                    at = ((x + K) * EY + K + y) * 8 + s
                    flat[pl.ds(at, 8, stride=8), :] = nat[a, x, pl.ds(y, 8), 128 * s : 128 * s + 128]

    out = Copies(out_sems)
    for axis, ab, strip in (("gy", "a", ya), ("gy", "b", yb), ("gx", "b", xb), ("gx", "a", xa)):
        at = 0
        for field, (in_x, in_y, _) in zip(fields, fields_of(k)):
            n = in_x if axis == "gx" else in_y
            first = sides.send(axis, ab, n) + K
            if axis == "gx":
                into = xb_z if ab == "b" and field is bz else strip.at[at : at + n]
                out.start(field.at[pl.ds(first, n), K : K + NY], into)
            else:
                out.start(field.at[K : K + NX, pl.ds(first, n)], strip.at[:, at : at + n])
            at += n
    out.wait()


def pack(k, g, beta):
    n = 4 * k + 1
    return pl.pallas_call(
        functools.partial(pack_kernel, k),
        out_shape=(EXT,) * 4
        + (rows_shape(n, NY), rows_shape(n - k, NY), rows_shape(k, NY), rows_shape(NX, n), rows_shape(NX, n)),
        in_specs=[HBM] * 2,
        out_specs=(VMEM,) * 4 + (ANY,) * 5,
        scratch_shapes=[
            pltpu.VMEM((4, NX, NY, 1024), F32),
            pltpu.SemaphoreType.DMA((2, NX)),
            pltpu.SemaphoreType.DMA((16,)),
        ],
        compiler_params=pltpu.CompilerParams(vmem_limit_bytes=8 * MIB),
        name="pack",
    )(*(pltpu.with_memory_space_constraint(array, pltpu.HBM) for array in (g, beta)))


def corner_kernel(planes, counts, ya, yb, ca, cb, sems):
    sides = Sides()
    out = Copies(sems)
    for ab, corner in (("b", cb), ("a", ca)):
        first = sides.send("gx", ab, planes)
        for j, (other, strip) in enumerate((("a", ya), ("b", yb))):
            at = done = 0
            for n, kept in counts:
                skip = jnp.where(sides.above["gy", other], 0, n - kept)
                out.start(
                    strip.at[pl.ds(first, planes), pl.ds(at + skip, kept)],
                    corner.at[j, :, done : done + kept],
                )
                at, done = at + n, done + kept
    out.wait()


def corners(planes, counts, ya, yb):
    shape = rows_shape(2, planes, sum(kept for _, kept in counts))
    return pl.pallas_call(
        functools.partial(corner_kernel, planes, counts),
        out_shape=(shape, shape),
        in_specs=[ANY] * 2,
        out_specs=(ANY,) * 2,
        scratch_shapes=[pltpu.SemaphoreType.DMA((4 * len(counts),))],
        compiler_params=pltpu.CompilerParams(vmem_limit_bytes=MIB),
        cost_estimate=pl.CostEstimate(flops=10**10 if len(counts) == 1 else 0, bytes_accessed=MIB, transcendentals=0),
        name="corners",
    )(ya, yb)


def swap(array, axis, ab):
    size = lax.axis_size(axis)
    pairs = [(i, i ^ 1 if ab == "a" else ((i + 1) ^ 1) - 1) for i in range(size)]
    return lax.ppermute(array, axis, [(i, j) for i, j in pairs if 0 <= j < size])


def relay_kernel(array, after, out, sem):
    copy = pltpu.make_async_copy(array, out, sem)
    copy.start()
    copy.wait()


def relay(array, after):
    return pl.pallas_call(
        relay_kernel,
        out_shape=jax.ShapeDtypeStruct(array.shape, F32),
        in_specs=[ANY] * 2,
        out_specs=ANY,
        scratch_shapes=[pltpu.SemaphoreType.DMA(())],
        compiler_params=pltpu.CompilerParams(vmem_limit_bytes=MIB),
        name="relay",
    )(array, after)


def exchange(planes, counts, xa, xb, ya, yb, xb_z=None):
    size = lax.axis_size("gx")
    middle = size // 2
    if xb_z is not None:
        pairs = [(i, ((i + 1) ^ 1) - 1) for i in range(1, size - 1) if i not in (middle - 1, middle)]
        xb_z = lax.ppermute(xb_z, "gx", pairs + [(middle - 1, 0), (middle, size - 1)])
    ya, yb = swap(ya, "gy", "a"), swap(yb, "gy", "b")
    xb, xa = swap(xb, "gx", "b"), swap(xa, "gx", "a")
    ca, cb = corners(planes, counts, ya, yb)
    cb, ca = swap(cb, "gx", "b"), swap(ca, "gx", "a")
    if xb_z is None:
        return xa, xb, ya, yb, ca, cb
    onward = lax.ppermute(relay(xb_z, ca), "gx", [(0, middle), (size - 1, middle - 1)])
    return xa, xb, ya, yb, ca, cb, xb_z, onward


def land_first(k, sides, into, xs, ys, cs, routed, fields):
    at_x = at_y = at_c = 0
    for i, (in_x, in_y, in_c) in enumerate(fields_of(k)):
        for ab in ("a", "b"):
            x, y = sides.land("gx", ab, in_x), sides.land("gy", ab, in_y)
            x_halo = fields[i].at[pl.ds(x, in_x), K : K + NY]
            if ab == "b" and i == 3:
                me, size = lax.axis_index("gx"), lax.axis_size("gx")
                by_ends = (me == 0) | (me == size // 2 - 1) | (me == size // 2) | (me == size - 1)
                into.start_either(by_ends, routed[1], routed[0], x_halo)
            else:
                into.start(xs[ab].at[at_x : at_x + in_x], x_halo)
            into.start(ys[ab].at[:, at_y : at_y + in_y], fields[i].at[K : K + NX, pl.ds(y, in_y)])
            x = sides.land("gx", ab, k)
            for j, other in enumerate(("a", "b")):
                y = sides.land("gy", other, in_c)
                into.start(
                    cs[ab].at[j, :, at_c : at_c + in_c],
                    fields[i].at[pl.ds(x, k), pl.ds(y, in_c)],
                )
        at_x, at_y, at_c = at_x + in_x, at_y + in_y, at_c + in_c


def land_later(k, sides, into, xs, ys, cs, w):
    for ab in ("a", "b"):
        x, y = sides.land("gx", ab, k), sides.land("gy", ab, k)
        into.start(xs[ab], w.at[pl.ds(x, k), K : K + NY])
        into.start(ys[ab], w.at[K : K + NX, pl.ds(y, k)])
        x = sides.land("gx", ab, k - 1)
        for j, other in enumerate(("a", "b")):
            y = sides.land("gy", other, k - 1)
            into.start(cs[ab].at[j], w.at[pl.ds(x, k - 1), pl.ds(y, k - 1)])


def chunks(low, high, size=8):
    return [(y, min(size, high - y)) for y in range(low, high, size)]


def scale(w, bx, by, bz, inv):
    @pl.loop(K - C, K + NX + C)
    def _(x):
        for y, n in chunks(K - C, K + NY + C):
            b = bz[x, y : y + n]
            sub = lax.broadcasted_iota(jnp.int32, b.shape, 1)
            lane = lax.broadcasted_iota(jnp.int32, b.shape, 2)
            inner = jnp.where((sub == 7) & (lane == 127), 0.0, b)
            beside = by[x, y - 1 : y + n]
            diagonal = bx[x, y : y + n] + bx[x - 1, y : y + n] + beside[1:] + beside[:-1] + b + z_down(inner)
            inverse = jnp.where(b > 0.0, 1.0 / jnp.where(b > 0.0, diagonal, 1.0), 0.0)
            inv[x, y : y + n] = inverse
            w[x, y : y + n] = w[x, y : y + n] * inverse
            bz[x, y : y + n] = inner


def one_step(step, reach, last, w, new, bx, by, bz, inv, acc):
    omega = omega_of(step)
    low, high = K - reach, K + NX + reach

    def walk(y, n, rows_inside):
        below = bx[low - 1, pl.ds(y, n)] * w[low - 1, pl.ds(y, n)]
        around = w[low, pl.ds(y - 1, n + 2)]
        for x in range(low, high):
            above = w[x + 1, pl.ds(y - 1, n + 2)]
            centre = around[1:-1]
            link = bx[x, pl.ds(y, n)]
            beside = by[x, pl.ds(y - 1, n + 1)]
            along = bz[x, pl.ds(y, n)]
            total = link * above[1:-1] + below
            total = total + beside[1:] * around[2:] + beside[:-1] * around[:-2]
            total = total + along * z_up(centre) + z_down(along * centre)
            moved = centre + omega * (inv[x, pl.ds(y, n)] * total - centre)
            if not last:
                new[x, pl.ds(y, n)] = moved
            if rows_inside and K <= x < K + NX:
                at = (x - K, pl.ds(y - K, n))
                term = omega * centre
                if last:
                    term = term + omega_of(step + 1) * moved
                acc[at] = term if step == 0 else acc[at] + term
            below, around = link * centre, above

    if reach:
        walk(K - reach, reach, False)
        walk(K + NY, reach, False)

    @pl.loop(0, NY // 8)
    def _(i):
        walk(K + i * 8, 8, True)


def steps_of(first, k, last, w, bx, by, bz, inv, acc):
    for i in range(k):
        end = last and i == k - 1
        one_step(first + i, k - 1 - i, end, w[i % 2], w[1 - i % 2], bx, by, bz, inv, acc)
    return w[k % 2]


def leave(k, sides, out, w, xa, xb, ya, yb):
    for axis, ab, strip in (("gy", "a", ya), ("gy", "b", yb), ("gx", "b", xb), ("gx", "a", xa)):
        first = sides.send(axis, ab, k) + K
        if axis == "gx":
            out.start(w.at[pl.ds(first, k), K : K + NY], strip)
        else:
            out.start(w.at[K : K + NX, pl.ds(first, k)], strip)


def first_kernel(
    k, k_next,
    w_in, bx_in, by_in, bz_in, xa, xb, ya, yb, ca, cb, z_plain, z_ends,
    w0, bx, by, bz, inv, acc, w1, xa_out, xb_out, ya_out, yb_out,
    in_sems, out_sems,
):
    sides = Sides()
    into = Copies(in_sems)
    xs, ys, cs = {"a": xa, "b": xb}, {"a": ya, "b": yb}, {"a": ca, "b": cb}
    land_first(k, sides, into, xs, ys, cs, (z_plain, z_ends), (w0, bx, by, bz))
    into.wait()
    scale(w0, bx, by, bz, inv)
    w = steps_of(0, k, False, (w0, w1), bx, by, bz, inv, acc)
    out = Copies(out_sems)
    leave(k_next, sides, out, w, xa_out, xb_out, ya_out, yb_out)
    out.wait()


def strips_shape(k):
    x, y = rows_shape(k, NY), rows_shape(NX, k)
    return (x, x, y, y)


def first_round(k, k_next, *arrays):
    assert k % 2 == 1
    _, bx, by, bz, inv, acc, w, *strips = pl.pallas_call(
        functools.partial(first_kernel, k, k_next),
        out_shape=(EXT,) * 5 + (ACC, EXT) + strips_shape(k_next),
        in_specs=[VMEM] * 4 + [ANY] * 8,
        out_specs=(VMEM,) * 7 + (ANY,) * 4,
        scratch_shapes=[pltpu.SemaphoreType.DMA((32,)), pltpu.SemaphoreType.DMA((4,))],
        input_output_aliases={i: i for i in range(4)},
        compiler_params=pltpu.CompilerParams(vmem_limit_bytes=2 * MIB),
        name="first_round",
    )(*arrays)
    return (bx, by, bz, inv), (w, acc), strips


def later_kernel(
    first, k, k_next,
    bx, by, bz, inv, w_in, acc_in, xa, xb, ya, yb, ca, cb,
    w0, acc, xa_out, xb_out, ya_out, yb_out,
    w1, in_sems, out_sems,
):
    sides = Sides()
    into = Copies(in_sems)
    land_later(k, sides, into, {"a": xa, "b": xb}, {"a": ya, "b": yb}, {"a": ca, "b": cb}, w0)
    into.wait()
    w = steps_of(first, k, False, (w0, w1), bx, by, bz, inv, acc)
    out = Copies(out_sems)
    leave(k_next, sides, out, w, xa_out, xb_out, ya_out, yb_out)
    out.wait()


def later_round(first, k, k_next, *arrays):
    assert k % 2 == 0
    w, acc, *strips = pl.pallas_call(
        functools.partial(later_kernel, first, k, k_next),
        out_shape=(EXT, ACC) + strips_shape(k_next),
        in_specs=[VMEM] * 6 + [ANY] * 6,
        out_specs=(VMEM,) * 2 + (ANY,) * 4,
        scratch_shapes=[EXT, pltpu.SemaphoreType.DMA((8,)), pltpu.SemaphoreType.DMA((4,))],
        input_output_aliases={4: 0, 5: 1},
        compiler_params=pltpu.CompilerParams(vmem_limit_bytes=6 * MIB),
        name="later_round",
    )(*arrays)
    return (w, acc), strips


def last_kernel(
    first, k,
    tile_rows, targets, mask, slots, bx, by, bz, inv, w_in, acc_in, xa, xb, ya, yb, ca, cb,
    grad, sent, w0, acc,
    w1, in_sems,
):
    sides = Sides()
    into = Copies(in_sems)
    land_later(k, sides, into, {"a": xa, "b": xb}, {"a": ya, "b": yb}, {"a": ca, "b": cb}, w0)
    sent[...] = jnp.zeros_like(sent)
    peers = slots.shape[0]
    sent[pl.ds(CAP, peers, stride=CAP + 1), :] = slots[...]
    into.wait()
    steps_of(first, k, True, (w0, w1), bx, by, bz, inv, acc)
    flat = acc.reshape(NX * NY * 8, 128)

    @pl.loop(0, mask.shape[0] // 8)
    def _(t8):
        for t in range(8):
            at = t8 * 8 + t
            row = flat[pl.ds(tile_rows[at], 1), :] * mask[pl.ds(at, 1), :].astype(F32)
            sent[pl.ds(targets[at], 1), :] = row

    @pl.loop(0, NX)
    def _(x):
        for yc in range(0, NY, 8):
            for s in range(8):
                at = (x * NY + yc) * 8 + s
                grad[x, yc : yc + 8, 128 * s : 128 * s + 128] = flat[pl.ds(at, 8, stride=8), :]


def last_round(first, k, peers, *arrays):
    return pl.pallas_call(
        functools.partial(last_kernel, first, k),
        out_shape=(
            jax.ShapeDtypeStruct((NX, NY, 1024), F32),
            jax.ShapeDtypeStruct((peers * (CAP + 1), 128), F32),
            EXT,
            ACC,
        ),
        in_specs=[SMEM, SMEM] + [VMEM] * 8 + [ANY] * 6,
        out_specs=(VMEM,) * 4,
        scratch_shapes=[EXT, pltpu.SemaphoreType.DMA((8,))],
        input_output_aliases={8: 2, 9: 3},
        compiler_params=pltpu.CompilerParams(vmem_limit_bytes=10 * MIB),
        name="last_round",
    )(*arrays)[:2]


def finish_kernel(received, heights, out):
    peers = received.shape[0] // (CAP + 1)
    slots = received[pl.ds(CAP, peers, stride=CAP + 1), :].T
    n_slots = heights.shape[1]
    ids = lax.broadcasted_iota(jnp.int32, (n_slots, peers), 0).astype(F32)
    table = jnp.zeros((n_slots, 128), F32)
    for p in range(CAP):
        named = (ids == slots[p : p + 1, :]).astype(jnp.bfloat16)
        rest = received[pl.ds(p, peers, stride=CAP + 1), :]
        for _ in range(3):
            part = rest.astype(jnp.bfloat16)
            rest = rest - part.astype(F32)
            table = table + jnp.dot(named, part, preferred_element_type=F32)
    slope = 0.5 * (heights[2] - heights[0])
    bend = heights[2] - 2.0 * heights[1] + heights[0]
    denom = 1.0 + slope * slope
    factor = 1.0 / (denom * jnp.sqrt(denom))
    skew_half = -1.5 * slope * bend * factor / denom
    out[0] = table * (factor - skew_half)
    out[1] = -2.0 * table * factor
    out[2] = table * (factor + skew_half)


def finish(received, heights):
    return pl.pallas_call(
        finish_kernel,
        out_shape=jax.ShapeDtypeStruct(heights.shape, F32),
        in_specs=[VMEM, VMEM],
        out_specs=VMEM,
        compiler_params=pltpu.CompilerParams(vmem_limit_bytes=8 * MIB),
        name="finish",
    )(received, heights)


def routes(tile_owner, tile_slot, peers):
    owner = tile_owner[:, 0]
    order = jnp.arange(owner.shape[0])
    before = (owner[:, None] == owner[None, :]) & (order[None, :] < order[:, None])
    position = jnp.sum(before.astype(jnp.int32), axis=1)
    is_owner = (owner[None, :] == jnp.arange(peers)[:, None]).astype(F32)
    placed = jnp.where(position[:, None] == jnp.arange(128)[None, :], tile_slot[:, None].astype(F32), 0.0)
    slots = jnp.dot(is_owner, placed, precision=lax.Precision.HIGHEST)
    return owner * (CAP + 1) + position, slots


def shards(grad_pressure, beta, tile_rows, tile_owner, tile_slot, face_mask, heights):
    peers = lax.axis_size("gx") * lax.axis_size("gy")
    targets, slots = routes(tile_owner, tile_slot, peers)
    k = ROUNDS[0]
    *fields, xa, xb, xb_z, ya, yb = pack(k, grad_pressure, beta)
    counts = [f[1:] for f in fields_of(k)]
    coeffs, state, strips = first_round(k, ROUNDS[1], *fields, *exchange(k, counts, xa, xb, ya, yb, xb_z))
    done = k
    for k, k_next in zip(ROUNDS[1:-1], ROUNDS[2:]):
        state, strips = later_round(done, k, k_next, *coeffs, *state, *exchange(k - 1, [(k, k - 1)], *strips))
        done += k
    k = ROUNDS[-1]
    grad_rhs, sent = last_round(
        done, k, peers, tile_rows, targets, face_mask, slots, *coeffs, *state, *exchange(k - 1, [(k, k - 1)], *strips)
    )
    sent = sent.reshape(peers, 1, (CAP + 1) * 128)
    received = lax.all_to_all(sent, ("gx", "gy"), split_axis=0, concat_axis=0, tiled=True)
    return grad_rhs, finish(received.reshape(peers * (CAP + 1), 128), heights)


def solution(mesh):
    in_specs = (
        P("gx", "gy", None),
        P(None, "gx", "gy", None),
        P(("gx", "gy")),
        P(("gx", "gy"), None),
        P(("gx", "gy")),
        P(("gx", "gy"), None),
        P(None, ("gx", "gy"), None),
    )
    out_specs = (P("gx", "gy", None), P(None, ("gx", "gy"), None))
    return jax.shard_map(shards, mesh=mesh, in_specs=in_specs, out_specs=out_specs, check_vma=False)
```

```python
import functools
import math

import jax
import jax.numpy as jnp
from jax import lax
from jax.experimental import pallas as pl
from jax.experimental.pallas import tpu as pltpu
from jax.sharding import PartitionSpec as P

STEPS = 4
CAP = 8
LOW_BOUND = 0.1
HIGH_BOUND = 1.9

ROUNDS = (3, 4, 4)
K = max(ROUNDS)
C = K - 1
NX, NY = 8, 32
EX, EY = NX + 2 * K, NY + 2 * K
TILE = (8, 128)
ANY = pl.BlockSpec(memory_space=pl.ANY)
SMEM = pl.BlockSpec(memory_space=pltpu.SMEM)
VMEM = pl.BlockSpec(memory_space=pltpu.VMEM)
HBM = pl.BlockSpec(memory_space=pltpu.HBM)
F32 = jnp.float32
MIB = 1 << 20
EXT = pltpu.VMEM((EX, EY, *TILE), F32)
ACC = pltpu.VMEM((NX, NY, *TILE), F32)


def omega_of(step):
    j = STEPS - 1 - step % STEPS
    theta = 0.5 * (HIGH_BOUND + LOW_BOUND) + 0.5 * (HIGH_BOUND - LOW_BOUND) * math.cos(
        math.pi * (2 * j + 1) / (2 * STEPS)
    )
    return 1.0 / theta


def rows_shape(*lead):
    return jax.ShapeDtypeStruct((*lead, *TILE), F32)


def z_up(v):
    r = pltpu.roll(v, 127, 2)
    lane = lax.broadcasted_iota(jnp.int32, v.shape, 2)
    return jnp.where(lane == 127, pltpu.roll(r, 7, 1), r)


def z_down(v):
    r = pltpu.roll(v, 1, 2)
    lane = lax.broadcasted_iota(jnp.int32, v.shape, 2)
    return jnp.where(lane == 0, pltpu.roll(r, 1, 1), r)


class Sides:
    def __init__(self):
        self.above = {
            (axis, ab): (lax.axis_index(axis) % 2) == (0 if ab == "a" else 1)
            for axis in ("gx", "gy")
            for ab in ("a", "b")
        }

    def send(self, axis, ab, n):
        return jnp.where(self.above[axis, ab], (NX if axis == "gx" else NY) - n, 0)

    def land(self, axis, ab, n):
        return jnp.where(self.above[axis, ab], K + (NX if axis == "gx" else NY), K - n)


class Copies:
    def __init__(self, sems):
        self.sems = sems
        self.all = []

    def start(self, src, dst):
        copy = pltpu.make_async_copy(src, dst, self.sems.at[len(self.all)])
        copy.start()
        self.all.append(copy)

    def start_either(self, first, src, other, dst):
        sem = self.sems.at[len(self.all)]
        for wanted, ref in ((first, src), (jnp.logical_not(first), other)):
            copy = pltpu.make_async_copy(ref, dst, sem)
            pl.when(wanted)(copy.start)
        self.all.append(copy)

    def wait(self):
        for copy in self.all:
            copy.wait()


def fields_of(k):
    return ((k, k, k - 1), (k + 1, k, k), (k, k + 1, k), (k, k, k - 1))


def pack_kernel(k, g, beta, w, bx, by, bz, xa, xb, xb_z, ya, yb, nat, in_sems, out_sems):
    sides = Sides()
    copies = []
    for x in range(NX):
        copies.append(
            (
                pltpu.make_async_copy(g.at[x], nat.at[0, x], in_sems.at[0, x]),
                pltpu.make_async_copy(beta.at[:, x], nat.at[1:4, x], in_sems.at[1, x]),
            )
        )
        for c in copies[-1]:
            c.start()
    fields = (w, bx, by, bz)
    for x in range(NX):
        for c in copies[x]:
            c.wait()
        for a, field in enumerate(fields):
            flat = field.reshape(EX * EY * 8, 128)

            @pl.loop(0, NY // 8)
            def _(yc, x=x, a=a, flat=flat):
                y = pl.multiple_of(yc * 8, 8)
                for s in range(8):
                    at = ((x + K) * EY + K + y) * 8 + s
                    flat[pl.ds(at, 8, stride=8), :] = nat[a, x, pl.ds(y, 8), 128 * s : 128 * s + 128]

    out = Copies(out_sems)
    for axis, ab, strip in (("gy", "a", ya), ("gy", "b", yb), ("gx", "b", xb), ("gx", "a", xa)):
        at = 0
        for field, (in_x, in_y, _) in zip(fields, fields_of(k)):
            n = in_x if axis == "gx" else in_y
            first = sides.send(axis, ab, n) + K
            if axis == "gx":
                into = xb_z if ab == "b" and field is bz else strip.at[at : at + n]
                out.start(field.at[pl.ds(first, n), K : K + NY], into)
            else:
                out.start(field.at[K : K + NX, pl.ds(first, n)], strip.at[:, at : at + n])
            at += n
    out.wait()


def pack(k, g, beta):
    n = 4 * k + 1
    return pl.pallas_call(
        functools.partial(pack_kernel, k),
        out_shape=(EXT,) * 4
        + (rows_shape(n, NY), rows_shape(n - k, NY), rows_shape(k, NY), rows_shape(NX, n), rows_shape(NX, n)),
        in_specs=[HBM] * 2,
        out_specs=(VMEM,) * 4 + (ANY,) * 5,
        scratch_shapes=[
            pltpu.VMEM((4, NX, NY, 1024), F32),
            pltpu.SemaphoreType.DMA((2, NX)),
            pltpu.SemaphoreType.DMA((16,)),
        ],
        compiler_params=pltpu.CompilerParams(vmem_limit_bytes=8 * MIB),
        name="pack",
    )(*(pltpu.with_memory_space_constraint(array, pltpu.HBM) for array in (g, beta)))


def corner_kernel(planes, counts, ya, yb, ca, cb, sems):
    sides = Sides()
    out = Copies(sems)
    for ab, corner in (("b", cb), ("a", ca)):
        first = sides.send("gx", ab, planes)
        for j, (other, strip) in enumerate((("a", ya), ("b", yb))):
            at = done = 0
            for n, kept in counts:
                skip = jnp.where(sides.above["gy", other], 0, n - kept)
                out.start(
                    strip.at[pl.ds(first, planes), pl.ds(at + skip, kept)],
                    corner.at[j, :, done : done + kept],
                )
                at, done = at + n, done + kept
    out.wait()


def corners(planes, counts, ya, yb):
    shape = rows_shape(2, planes, sum(kept for _, kept in counts))
    return pl.pallas_call(
        functools.partial(corner_kernel, planes, counts),
        out_shape=(shape, shape),
        in_specs=[ANY] * 2,
        out_specs=(ANY,) * 2,
        scratch_shapes=[pltpu.SemaphoreType.DMA((4 * len(counts),))],
        compiler_params=pltpu.CompilerParams(vmem_limit_bytes=MIB),
        cost_estimate=pl.CostEstimate(flops=10**10 if len(counts) == 1 else 0, bytes_accessed=MIB, transcendentals=0),
        name="corners",
    )(ya, yb)


def swap(array, axis, ab):
    size = lax.axis_size(axis)
    pairs = [(i, i ^ 1 if ab == "a" else ((i + 1) ^ 1) - 1) for i in range(size)]
    return lax.ppermute(array, axis, [(i, j) for i, j in pairs if 0 <= j < size])


def relay_kernel(array, after, out, sem):
    copy = pltpu.make_async_copy(array, out, sem)
    copy.start()
    copy.wait()


def relay(array, after):
    return pl.pallas_call(
        relay_kernel,
        out_shape=jax.ShapeDtypeStruct(array.shape, F32),
        in_specs=[ANY] * 2,
        out_specs=ANY,
        scratch_shapes=[pltpu.SemaphoreType.DMA(())],
        compiler_params=pltpu.CompilerParams(vmem_limit_bytes=MIB),
        name="relay",
    )(array, after)


def exchange(planes, counts, xa, xb, ya, yb, xb_z=None):
    size = lax.axis_size("gx")
    middle = size // 2
    if xb_z is not None:
        pairs = [(i, ((i + 1) ^ 1) - 1) for i in range(1, size - 1) if i not in (middle - 1, middle)]
        xb_z = lax.ppermute(xb_z, "gx", pairs + [(middle - 1, 0), (middle, size - 1)])
    ya, yb = swap(ya, "gy", "a"), swap(yb, "gy", "b")
    xb, xa = swap(xb, "gx", "b"), swap(xa, "gx", "a")
    ca, cb = corners(planes, counts, ya, yb)
    cb, ca = swap(cb, "gx", "b"), swap(ca, "gx", "a")
    if xb_z is None:
        return xa, xb, ya, yb, ca, cb
    onward = lax.ppermute(relay(xb_z, ca), "gx", [(0, middle), (size - 1, middle - 1)])
    return xa, xb, ya, yb, ca, cb, xb_z, onward


def land_first_y(k, sides, into, ys, fields):
    at = 0
    for field, (_, n, _) in zip(fields, fields_of(k)):
        for ab in ("a", "b"):
            into.start(ys[ab].at[:, at : at + n], field.at[K : K + NX, pl.ds(sides.land("gy", ab, n), n)])
        at += n


def land_first_x(k, sides, into, xs, cs, routed, fields):
    at_x = at_c = 0
    for i, (in_x, _, in_c) in enumerate(fields_of(k)):
        for ab in ("a", "b"):
            x = sides.land("gx", ab, in_x)
            x_halo = fields[i].at[pl.ds(x, in_x), K : K + NY]
            if ab == "b" and i == 3:
                me, size = lax.axis_index("gx"), lax.axis_size("gx")
                by_ends = (me == 0) | (me == size // 2 - 1) | (me == size // 2) | (me == size - 1)
                into.start_either(by_ends, routed[1], routed[0], x_halo)
            else:
                into.start(xs[ab].at[at_x : at_x + in_x], x_halo)
            x = sides.land("gx", ab, k)
            for j, other in enumerate(("a", "b")):
                y = sides.land("gy", other, in_c)
                into.start(
                    cs[ab].at[j, :, at_c : at_c + in_c],
                    fields[i].at[pl.ds(x, k), pl.ds(y, in_c)],
                )
        at_x, at_c = at_x + in_x, at_c + in_c


def land_later_x(k, sides, into, xs, cs, w):
    for ab in ("a", "b"):
        into.start(xs[ab], w.at[pl.ds(sides.land("gx", ab, k), k), K : K + NY])
        x = sides.land("gx", ab, k - 1)
        for j, other in enumerate(("a", "b")):
            y = sides.land("gy", other, k - 1)
            into.start(cs[ab].at[j], w.at[pl.ds(x, k - 1), pl.ds(y, k - 1)])


def chunks(low, high, size=8):
    return [(y, min(size, high - y)) for y in range(low, high, size)]


def scale(planes, w, bx, by, bz, inv):
    @pl.loop(*planes)
    def _(x):
        for y, n in chunks(K - C, K + NY + C):
            b = bz[x, y : y + n]
            sub = lax.broadcasted_iota(jnp.int32, b.shape, 1)
            lane = lax.broadcasted_iota(jnp.int32, b.shape, 2)
            inner = jnp.where((sub == 7) & (lane == 127), 0.0, b)
            beside = by[x, y - 1 : y + n]
            diagonal = bx[x, y : y + n] + bx[x - 1, y : y + n] + beside[1:] + beside[:-1] + b + z_down(inner)
            inverse = jnp.where(b > 0.0, 1.0 / jnp.where(b > 0.0, diagonal, 1.0), 0.0)
            inv[x, y : y + n] = inverse
            w[x, y : y + n] = w[x, y : y + n] * inverse
            bz[x, y : y + n] = inner


def one_step(step, reach, last, spans, w, new, bx, by, bz, inv, acc):
    omega = omega_of(step)

    def walk(span, y, n, rows_inside):
        low, high = span
        below = bx[low - 1, pl.ds(y, n)] * w[low - 1, pl.ds(y, n)]
        around = w[low, pl.ds(y - 1, n + 2)]
        for x in range(low, high):
            above = w[x + 1, pl.ds(y - 1, n + 2)]
            centre = around[1:-1]
            link = bx[x, pl.ds(y, n)]
            beside = by[x, pl.ds(y - 1, n + 1)]
            along = bz[x, pl.ds(y, n)]
            total = link * above[1:-1] + below
            total = total + beside[1:] * around[2:] + beside[:-1] * around[:-2]
            total = total + along * z_up(centre) + z_down(along * centre)
            moved = centre + omega * (inv[x, pl.ds(y, n)] * total - centre)
            if not last:
                new[x, pl.ds(y, n)] = moved
            if rows_inside and K <= x < K + NX:
                at = (x - K, pl.ds(y - K, n))
                term = omega * centre
                if last:
                    term = term + omega_of(step + 1) * moved
                acc[at] = term if step == 0 else acc[at] + term
            below, around = link * centre, above

    if reach:
        for span in spans:
            walk(span, K - reach, reach, False)
            walk(span, K + NY, reach, False)

    @pl.loop(0, NY // 8)
    def _(i):
        for span in spans:
            walk(span, K + i * 8, 8, True)


def early_span(i, lead):
    return K + lead + i, K + NX - 1 - i


def early_steps(first, k, lead, w, *arrays):
    for i in range(k):
        low, high = early_span(i, lead)
        if low < high:
            one_step(first + i, k - 1 - i, False, [(low, high)], w[i % 2], w[1 - i % 2], *arrays)


def other_steps(first, k, lead, last, w, *arrays):
    for i in range(k):
        reach = k - 1 - i
        low, high = early_span(i, lead)
        spans = [(K - reach, low), (high, K + NX + reach)] if low < high else [(K - reach, K + NX + reach)]
        one_step(first + i, reach, last and i == k - 1, spans, w[i % 2], w[1 - i % 2], *arrays)
    return w[k % 2]


def leave(k, sides, out, w, xa, xb, ya, yb):
    for axis, ab, strip in (("gy", "a", ya), ("gy", "b", yb), ("gx", "b", xb), ("gx", "a", xa)):
        first = sides.send(axis, ab, k) + K
        if axis == "gx":
            out.start(w.at[pl.ds(first, k), K : K + NY], strip)
        else:
            out.start(w.at[K : K + NX, pl.ds(first, k)], strip)


def strips_shape(k):
    x, y = rows_shape(k, NY), rows_shape(NX, k)
    return (x, x, y, y)


def early_first_kernel(k, w_in, bx_in, by_in, bz_in, ya, yb, w0, bx, by, bz, inv, acc, w1, sems):
    sides = Sides()
    into = Copies(sems)
    land_first_y(k, sides, into, {"a": ya, "b": yb}, (w0, bx, by, bz))
    into.wait()
    scale((K + 1, K + NX), w0, bx, by, bz, inv)
    early_steps(0, k, 2, (w0, w1), bx, by, bz, inv, acc)


def early_first(k, fields, ya, yb):
    return pl.pallas_call(
        functools.partial(early_first_kernel, k),
        out_shape=(EXT,) * 5 + (ACC, EXT),
        in_specs=[VMEM] * 4 + [ANY] * 2,
        out_specs=(VMEM,) * 7,
        scratch_shapes=[pltpu.SemaphoreType.DMA((8,))],
        input_output_aliases={i: i for i in range(4)},
        compiler_params=pltpu.CompilerParams(vmem_limit_bytes=2 * MIB),
        name="early_first",
    )(*fields, ya, yb)


def first_kernel(
    k, k_next,
    w_in, bx_in, by_in, bz_in, inv_in, acc_in, w1_in, xa, xb, ca, cb, z_plain, z_ends,
    w0, bx, by, bz, inv, acc, w1, xa_out, xb_out, ya_out, yb_out,
    in_sems, out_sems,
):
    sides = Sides()
    into = Copies(in_sems)
    land_first_x(k, sides, into, {"a": xa, "b": xb}, {"a": ca, "b": cb}, (z_plain, z_ends), (w0, bx, by, bz))
    into.wait()
    scale((K - C, K + 1), w0, bx, by, bz, inv)
    scale((K + NX, K + NX + C), w0, bx, by, bz, inv)
    w = other_steps(0, k, 2, False, (w0, w1), bx, by, bz, inv, acc)
    out = Copies(out_sems)
    leave(k_next, sides, out, w, xa_out, xb_out, ya_out, yb_out)
    out.wait()


def first_round(k, k_next, *arrays):
    w0, bx, by, bz, inv, acc, w1, *strips = pl.pallas_call(
        functools.partial(first_kernel, k, k_next),
        out_shape=(EXT,) * 5 + (ACC, EXT) + strips_shape(k_next),
        in_specs=[VMEM] * 7 + [ANY] * 6,
        out_specs=(VMEM,) * 7 + (ANY,) * 4,
        scratch_shapes=[pltpu.SemaphoreType.DMA((24,)), pltpu.SemaphoreType.DMA((4,))],
        input_output_aliases={i: i for i in range(7)},
        compiler_params=pltpu.CompilerParams(vmem_limit_bytes=2 * MIB),
        name="first_round",
    )(*arrays)
    return (bx, by, bz, inv), ((w0, w1)[k % 2], (w1, w0)[k % 2], acc), strips


def early_kernel(first, k, bx, by, bz, inv, w_in, w1_in, acc_in, ya, yb, w0, w1, acc, sems):
    sides = Sides()
    into = Copies(sems)
    for ab, strip in (("a", ya), ("b", yb)):
        into.start(strip, w0.at[K : K + NX, pl.ds(sides.land("gy", ab, k), k)])
    into.wait()
    early_steps(first, k, 1, (w0, w1), bx, by, bz, inv, acc)


def early(first, k, coeffs, state, ya, yb):
    return pl.pallas_call(
        functools.partial(early_kernel, first, k),
        out_shape=(EXT, EXT, ACC),
        in_specs=[VMEM] * 7 + [ANY] * 2,
        out_specs=(VMEM,) * 3,
        scratch_shapes=[pltpu.SemaphoreType.DMA((2,))],
        input_output_aliases={4: 0, 5: 1, 6: 2},
        compiler_params=pltpu.CompilerParams(vmem_limit_bytes=2 * MIB),
        name="early",
    )(*coeffs, *state, ya, yb)


def later_kernel(
    first, k, k_next,
    bx, by, bz, inv, w_in, w1_in, acc_in, xa, xb, ca, cb,
    w0, w1, acc, xa_out, xb_out, ya_out, yb_out,
    in_sems, out_sems,
):
    sides = Sides()
    into = Copies(in_sems)
    land_later_x(k, sides, into, {"a": xa, "b": xb}, {"a": ca, "b": cb}, w0)
    into.wait()
    w = other_steps(first, k, 1, False, (w0, w1), bx, by, bz, inv, acc)
    out = Copies(out_sems)
    leave(k_next, sides, out, w, xa_out, xb_out, ya_out, yb_out)
    out.wait()


def later_round(first, k, k_next, *arrays):
    w0, w1, acc, *strips = pl.pallas_call(
        functools.partial(later_kernel, first, k, k_next),
        out_shape=(EXT, EXT, ACC) + strips_shape(k_next),
        in_specs=[VMEM] * 7 + [ANY] * 4,
        out_specs=(VMEM,) * 3 + (ANY,) * 4,
        scratch_shapes=[pltpu.SemaphoreType.DMA((6,)), pltpu.SemaphoreType.DMA((4,))],
        input_output_aliases={4: 0, 5: 1, 6: 2},
        compiler_params=pltpu.CompilerParams(vmem_limit_bytes=2 * MIB),
        name="later_round",
    )(*arrays)
    return ((w0, w1)[k % 2], (w1, w0)[k % 2], acc), strips


def last_kernel(
    first, k,
    tile_rows, targets, mask, slots, bx, by, bz, inv, w_in, w1_in, acc_in, xa, xb, ca, cb,
    grad, sent, w0, w1, acc,
    in_sems,
):
    sides = Sides()
    into = Copies(in_sems)
    land_later_x(k, sides, into, {"a": xa, "b": xb}, {"a": ca, "b": cb}, w0)
    sent[...] = jnp.zeros_like(sent)
    peers = slots.shape[0]
    sent[pl.ds(CAP, peers, stride=CAP + 1), :] = slots[...]
    into.wait()
    other_steps(first, k, 1, True, (w0, w1), bx, by, bz, inv, acc)
    flat = acc.reshape(NX * NY * 8, 128)

    @pl.loop(0, mask.shape[0] // 8)
    def _(t8):
        for t in range(8):
            at = t8 * 8 + t
            row = flat[pl.ds(tile_rows[at], 1), :] * mask[pl.ds(at, 1), :].astype(F32)
            sent[pl.ds(targets[at], 1), :] = row

    @pl.loop(0, NX)
    def _(x):
        for yc in range(0, NY, 8):
            for s in range(8):
                at = (x * NY + yc) * 8 + s
                grad[x, yc : yc + 8, 128 * s : 128 * s + 128] = flat[pl.ds(at, 8, stride=8), :]


def last_round(first, k, peers, *arrays):
    return pl.pallas_call(
        functools.partial(last_kernel, first, k),
        out_shape=(
            jax.ShapeDtypeStruct((NX, NY, 1024), F32),
            jax.ShapeDtypeStruct((peers * (CAP + 1), 128), F32),
            EXT,
            EXT,
            ACC,
        ),
        in_specs=[SMEM, SMEM] + [VMEM] * 9 + [ANY] * 4,
        out_specs=(VMEM,) * 5,
        scratch_shapes=[pltpu.SemaphoreType.DMA((6,))],
        input_output_aliases={8: 2, 9: 3, 10: 4},
        compiler_params=pltpu.CompilerParams(vmem_limit_bytes=6 * MIB),
        name="last_round",
    )(*arrays)[:2]


def finish_kernel(received, heights, out):
    peers = received.shape[0] // (CAP + 1)
    slots = received[pl.ds(CAP, peers, stride=CAP + 1), :].T
    n_slots = heights.shape[1]
    ids = lax.broadcasted_iota(jnp.int32, (n_slots, peers), 0).astype(F32)
    table = jnp.zeros((n_slots, 128), F32)
    for p in range(CAP):
        named = (ids == slots[p : p + 1, :]).astype(jnp.bfloat16)
        rest = received[pl.ds(p, peers, stride=CAP + 1), :]
        for _ in range(3):
            part = rest.astype(jnp.bfloat16)
            rest = rest - part.astype(F32)
            table = table + jnp.dot(named, part, preferred_element_type=F32)
    slope = 0.5 * (heights[2] - heights[0])
    bend = heights[2] - 2.0 * heights[1] + heights[0]
    denom = 1.0 + slope * slope
    factor = 1.0 / (denom * jnp.sqrt(denom))
    skew_half = -1.5 * slope * bend * factor / denom
    out[0] = table * (factor - skew_half)
    out[1] = -2.0 * table * factor
    out[2] = table * (factor + skew_half)


def finish(received, heights):
    return pl.pallas_call(
        finish_kernel,
        out_shape=jax.ShapeDtypeStruct(heights.shape, F32),
        in_specs=[VMEM, VMEM],
        out_specs=VMEM,
        compiler_params=pltpu.CompilerParams(vmem_limit_bytes=8 * MIB),
        name="finish",
    )(received, heights)


def routes(tile_owner, tile_slot, peers):
    owner = tile_owner[:, 0]
    order = jnp.arange(owner.shape[0])
    before = (owner[:, None] == owner[None, :]) & (order[None, :] < order[:, None])
    position = jnp.sum(before.astype(jnp.int32), axis=1)
    is_owner = (owner[None, :] == jnp.arange(peers)[:, None]).astype(F32)
    placed = jnp.where(position[:, None] == jnp.arange(128)[None, :], tile_slot[:, None].astype(F32), 0.0)
    slots = jnp.dot(is_owner, placed, precision=lax.Precision.HIGHEST)
    return owner * (CAP + 1) + position, slots


def shards(grad_pressure, beta, tile_rows, tile_owner, tile_slot, face_mask, heights):
    peers = lax.axis_size("gx") * lax.axis_size("gy")
    targets, slots = routes(tile_owner, tile_slot, peers)
    k = ROUNDS[0]
    *fields, xa, xb, xb_z, ya, yb = pack(k, grad_pressure, beta)
    counts = [f[1:] for f in fields_of(k)]
    xa, xb, ya, yb, *corner = exchange(k, counts, xa, xb, ya, yb, xb_z)
    coeffs, state, strips = first_round(k, ROUNDS[1], *early_first(k, fields, ya, yb), xa, xb, *corner)
    done = k
    for k, k_next in zip(ROUNDS[1:-1], ROUNDS[2:]):
        xa, xb, ya, yb, *corner = exchange(k - 1, [(k, k - 1)], *strips)
        state = early(done, k, coeffs, state, ya, yb)
        state, strips = later_round(done, k, k_next, *coeffs, *state, xa, xb, *corner)
        done += k
    k = ROUNDS[-1]
    xa, xb, ya, yb, *corner = exchange(k - 1, [(k, k - 1)], *strips)
    state = early(done, k, coeffs, state, ya, yb)
    grad_rhs, sent = last_round(
        done, k, peers, tile_rows, targets, face_mask, slots, *coeffs, *state, xa, xb, *corner
    )
    sent = sent.reshape(peers, 1, (CAP + 1) * 128)
    received = lax.all_to_all(sent, ("gx", "gy"), split_axis=0, concat_axis=0, tiled=True)
    return grad_rhs, finish(received.reshape(peers * (CAP + 1), 128), heights)


def solution(mesh):
    in_specs = (
        P("gx", "gy", None),
        P(None, "gx", "gy", None),
        P(("gx", "gy")),
        P(("gx", "gy"), None),
        P(("gx", "gy")),
        P(("gx", "gy"), None),
        P(None, ("gx", "gy"), None),
    )
    out_specs = (P("gx", "gy", None), P(None, ("gx", "gy"), None))
    return jax.shard_map(shards, mesh=mesh, in_specs=in_specs, out_specs=out_specs, check_vma=False)
```

```python
import functools
import math

import jax
import jax.numpy as jnp
from jax import lax
from jax.experimental import pallas as pl
from jax.experimental.pallas import tpu as pltpu
from jax.sharding import PartitionSpec as P

STEPS = 4
CAP = 8
LOW_BOUND = 0.1
HIGH_BOUND = 1.9

ROUNDS = (3, 4, 4)
K = max(ROUNDS)
C = K - 1
NX, NY = 8, 32
EX, EY = NX + 2 * K, NY + 2 * K
TILE = (8, 128)
ANY = pl.BlockSpec(memory_space=pl.ANY)
SMEM = pl.BlockSpec(memory_space=pltpu.SMEM)
VMEM = pl.BlockSpec(memory_space=pltpu.VMEM)
HBM = pl.BlockSpec(memory_space=pltpu.HBM)
F32 = jnp.float32
MIB = 1 << 20
EXT = pltpu.VMEM((EX, EY, *TILE), F32)
ACC = pltpu.VMEM((NX, NY, *TILE), F32)


def omega_of(step):
    j = STEPS - 1 - step % STEPS
    theta = 0.5 * (HIGH_BOUND + LOW_BOUND) + 0.5 * (HIGH_BOUND - LOW_BOUND) * math.cos(
        math.pi * (2 * j + 1) / (2 * STEPS)
    )
    return 1.0 / theta


def rows_shape(*lead):
    return jax.ShapeDtypeStruct((*lead, *TILE), F32)


def z_up(v):
    r = pltpu.roll(v, 127, 2)
    lane = lax.broadcasted_iota(jnp.int32, v.shape, 2)
    return jnp.where(lane == 127, pltpu.roll(r, 7, 1), r)


def z_down(v):
    r = pltpu.roll(v, 1, 2)
    lane = lax.broadcasted_iota(jnp.int32, v.shape, 2)
    return jnp.where(lane == 0, pltpu.roll(r, 1, 1), r)


class Sides:
    def __init__(self):
        self.above = {
            (axis, ab): (lax.axis_index(axis) % 2) == (0 if ab == "a" else 1)
            for axis in ("gx", "gy")
            for ab in ("a", "b")
        }

    def send(self, axis, ab, n):
        return jnp.where(self.above[axis, ab], (NX if axis == "gx" else NY) - n, 0)

    def land(self, axis, ab, n):
        return jnp.where(self.above[axis, ab], K + (NX if axis == "gx" else NY), K - n)


class Copies:
    def __init__(self, sems):
        self.sems = sems
        self.all = []

    def start(self, src, dst):
        copy = pltpu.make_async_copy(src, dst, self.sems.at[len(self.all)])
        copy.start()
        self.all.append(copy)

    def start_either(self, first, src, other, dst):
        sem = self.sems.at[len(self.all)]
        for wanted, ref in ((first, src), (jnp.logical_not(first), other)):
            copy = pltpu.make_async_copy(ref, dst, sem)
            pl.when(wanted)(copy.start)
        self.all.append(copy)

    def wait(self):
        for copy in self.all:
            copy.wait()


def fields_of(k):
    return ((k, k, k - 1), (k + 1, k, k), (k, k + 1, k), (k, k, k - 1))


def pack_kernel(k, g, beta, w, bx, by, bz, xa, xb, xb_z, ya, yb, nat, in_sems, out_sems):
    sides = Sides()
    copies = []
    for x in range(NX):
        copies.append(
            (
                pltpu.make_async_copy(g.at[x], nat.at[0, x], in_sems.at[0, x]),
                pltpu.make_async_copy(beta.at[:, x], nat.at[1:4, x], in_sems.at[1, x]),
            )
        )
        for c in copies[-1]:
            c.start()
    fields = (w, bx, by, bz)
    for x in range(NX):
        for c in copies[x]:
            c.wait()
        for a, field in enumerate(fields):
            flat = field.reshape(EX * EY * 8, 128)

            @pl.loop(0, NY // 8)
            def _(yc, x=x, a=a, flat=flat):
                y = pl.multiple_of(yc * 8, 8)
                for s in range(8):
                    at = ((x + K) * EY + K + y) * 8 + s
                    flat[pl.ds(at, 8, stride=8), :] = nat[a, x, pl.ds(y, 8), 128 * s : 128 * s + 128]

    out = Copies(out_sems)
    for axis, ab, strip in (("gy", "a", ya), ("gy", "b", yb), ("gx", "b", xb), ("gx", "a", xa)):
        at = 0
        for field, (in_x, in_y, _) in zip(fields, fields_of(k)):
            n = in_x if axis == "gx" else in_y
            first = sides.send(axis, ab, n) + K
            if axis == "gx":
                into = xb_z if ab == "b" and field is bz else strip.at[at : at + n]
                out.start(field.at[pl.ds(first, n), K : K + NY], into)
            else:
                out.start(field.at[K : K + NX, pl.ds(first, n)], strip.at[:, at : at + n])
            at += n
    out.wait()


def pack(k, g, beta):
    n = 4 * k + 1
    return pl.pallas_call(
        functools.partial(pack_kernel, k),
        out_shape=(EXT,) * 4
        + (rows_shape(n, NY), rows_shape(n - k, NY), rows_shape(k, NY), rows_shape(NX, n), rows_shape(NX, n)),
        in_specs=[HBM] * 2,
        out_specs=(VMEM,) * 4 + (ANY,) * 5,
        scratch_shapes=[
            pltpu.VMEM((4, NX, NY, 1024), F32),
            pltpu.SemaphoreType.DMA((2, NX)),
            pltpu.SemaphoreType.DMA((16,)),
        ],
        compiler_params=pltpu.CompilerParams(vmem_limit_bytes=8 * MIB),
        name="pack",
    )(*(pltpu.with_memory_space_constraint(array, pltpu.HBM) for array in (g, beta)))


def corner_kernel(planes, counts, ya, yb, ca, cb, sems):
    sides = Sides()
    out = Copies(sems)
    for ab, corner in (("b", cb), ("a", ca)):
        first = sides.send("gx", ab, planes)
        for j, (other, strip) in enumerate((("a", ya), ("b", yb))):
            at = done = 0
            for n, kept in counts:
                skip = jnp.where(sides.above["gy", other], 0, n - kept)
                out.start(
                    strip.at[pl.ds(first, planes), pl.ds(at + skip, kept)],
                    corner.at[j, :, done : done + kept],
                )
                at, done = at + n, done + kept
    out.wait()


def corners(planes, counts, ya, yb):
    shape = rows_shape(2, planes, sum(kept for _, kept in counts))
    return pl.pallas_call(
        functools.partial(corner_kernel, planes, counts),
        out_shape=(shape, shape),
        in_specs=[ANY] * 2,
        out_specs=(ANY,) * 2,
        scratch_shapes=[pltpu.SemaphoreType.DMA((4 * len(counts),))],
        compiler_params=pltpu.CompilerParams(vmem_limit_bytes=MIB),
        cost_estimate=pl.CostEstimate(flops=10**10 if len(counts) == 1 else 0, bytes_accessed=MIB, transcendentals=0),
        name="corners",
    )(ya, yb)


def swap(array, axis, ab):
    size = lax.axis_size(axis)
    pairs = [(i, i ^ 1 if ab == "a" else ((i + 1) ^ 1) - 1) for i in range(size)]
    return lax.ppermute(array, axis, [(i, j) for i, j in pairs if 0 <= j < size])


def relay_kernel(array, after, out, sem):
    copy = pltpu.make_async_copy(array, out, sem)
    copy.start()
    copy.wait()


def relay(array, after):
    return pl.pallas_call(
        relay_kernel,
        out_shape=jax.ShapeDtypeStruct(array.shape, F32),
        in_specs=[ANY] * 2,
        out_specs=ANY,
        scratch_shapes=[pltpu.SemaphoreType.DMA(())],
        compiler_params=pltpu.CompilerParams(vmem_limit_bytes=MIB),
        name="relay",
    )(array, after)


def exchange(planes, counts, xa, xb, ya, yb, xb_z=None):
    size = lax.axis_size("gx")
    middle = size // 2
    if xb_z is not None:
        pairs = [(i, ((i + 1) ^ 1) - 1) for i in range(1, size - 1) if i not in (middle - 1, middle)]
        xb_z = lax.ppermute(xb_z, "gx", pairs + [(middle - 1, 0), (middle, size - 1)])
    ya, yb = swap(ya, "gy", "a"), swap(yb, "gy", "b")
    xb, xa = swap(xb, "gx", "b"), swap(xa, "gx", "a")
    ca, cb = corners(planes, counts, ya, yb)
    cb, ca = swap(cb, "gx", "b"), swap(ca, "gx", "a")
    if xb_z is None:
        return xa, xb, ya, yb, ca, cb
    onward = lax.ppermute(relay(xb_z, ca), "gx", [(0, middle), (size - 1, middle - 1)])
    return xa, xb, ya, yb, ca, cb, xb_z, onward


def land_first_y(k, sides, into, ys, fields):
    at = 0
    for field, (_, n, _) in zip(fields, fields_of(k)):
        for ab in ("a", "b"):
            into.start(ys[ab].at[:, at : at + n], field.at[K : K + NX, pl.ds(sides.land("gy", ab, n), n)])
        at += n


def land_first_x(ab, k, sides, into, strip, corner, routed, fields):
    at_x = at_c = 0
    for i, (in_x, _, in_c) in enumerate(fields_of(k)):
        x_halo = fields[i].at[pl.ds(sides.land("gx", ab, in_x), in_x), K : K + NY]
        if ab == "b" and i == 3:
            me, size = lax.axis_index("gx"), lax.axis_size("gx")
            by_ends = (me == 0) | (me == size // 2 - 1) | (me == size // 2) | (me == size - 1)
            into.start_either(by_ends, routed[1], routed[0], x_halo)
        else:
            into.start(strip.at[at_x : at_x + in_x], x_halo)
        x = sides.land("gx", ab, k)
        for j, other in enumerate(("a", "b")):
            y = sides.land("gy", other, in_c)
            into.start(corner.at[j, :, at_c : at_c + in_c], fields[i].at[pl.ds(x, k), pl.ds(y, in_c)])
        at_x, at_c = at_x + in_x, at_c + in_c


def land_later_x(ab, k, sides, into, strip, corner, w):
    into.start(strip, w.at[pl.ds(sides.land("gx", ab, k), k), K : K + NY])
    x = sides.land("gx", ab, k - 1)
    for j, other in enumerate(("a", "b")):
        y = sides.land("gy", other, k - 1)
        into.start(corner.at[j], w.at[pl.ds(x, k - 1), pl.ds(y, k - 1)])


def chunks(low, high, size=8):
    return [(y, min(size, high - y)) for y in range(low, high, size)]


def scale(planes, w, bx, by, bz, inv):
    @pl.loop(*planes)
    def _(x):
        for y, n in chunks(K - C, K + NY + C):
            b = bz[x, y : y + n]
            sub = lax.broadcasted_iota(jnp.int32, b.shape, 1)
            lane = lax.broadcasted_iota(jnp.int32, b.shape, 2)
            inner = jnp.where((sub == 7) & (lane == 127), 0.0, b)
            beside = by[x, y - 1 : y + n]
            diagonal = bx[x, y : y + n] + bx[x - 1, y : y + n] + beside[1:] + beside[:-1] + b + z_down(inner)
            inverse = jnp.where(b > 0.0, 1.0 / jnp.where(b > 0.0, diagonal, 1.0), 0.0)
            inv[x, y : y + n] = inverse
            w[x, y : y + n] = w[x, y : y + n] * inverse
            bz[x, y : y + n] = inner


def one_step(step, reach, last, span, w, new, bx, by, bz, inv, acc):
    omega = omega_of(step)

    low, high = span

    def walk(y, n, rows_inside):
        below = bx[low - 1, pl.ds(y, n)] * w[low - 1, pl.ds(y, n)]
        around = w[low, pl.ds(y - 1, n + 2)]
        for x in range(low, high):
            above = w[x + 1, pl.ds(y - 1, n + 2)]
            centre = around[1:-1]
            link = bx[x, pl.ds(y, n)]
            beside = by[x, pl.ds(y - 1, n + 1)]
            along = bz[x, pl.ds(y, n)]
            total = link * above[1:-1] + below
            total = total + beside[1:] * around[2:] + beside[:-1] * around[:-2]
            total = total + along * z_up(centre) + z_down(along * centre)
            moved = centre + omega * (inv[x, pl.ds(y, n)] * total - centre)
            if not last:
                new[x, pl.ds(y, n)] = moved
            if rows_inside and K <= x < K + NX:
                at = (x - K, pl.ds(y - K, n))
                term = omega * centre
                if last:
                    term = term + omega_of(step + 1) * moved
                acc[at] = term if step == 0 else acc[at] + term
            below, around = link * centre, above

    if reach:
        walk(K - reach, reach, False)
        walk(K + NY, reach, False)

    @pl.loop(0, NY // 8)
    def _(i):
        walk(K + i * 8, 8, True)


def spans_of(i, k, lead, a_above):
    low, high = K - (k - 1 - i), K + NX + k - 1 - i
    cut = K + lead + i if a_above else K + NX - 1 - i
    return ((cut, high), (low, cut)) if a_above else ((low, cut), (cut, high))


def steps_of(first, k, lead, last, late, a_above, w, *arrays):
    for i in range(k):
        span = spans_of(i, k, lead, a_above)[late]
        one_step(first + i, k - 1 - i, last and i == k - 1, span, w[i % 2], w[1 - i % 2], *arrays)


def on_each_side(sides, run):
    a_above = sides.above["gx", "a"]
    pl.when(a_above)(functools.partial(run, True))
    pl.when(jnp.logical_not(a_above))(functools.partial(run, False))


def leave(k, sides, out, w, xa, xb, ya, yb):
    for axis, ab, strip in (("gy", "a", ya), ("gy", "b", yb), ("gx", "b", xb), ("gx", "a", xa)):
        first = sides.send(axis, ab, k) + K
        if axis == "gx":
            out.start(w.at[pl.ds(first, k), K : K + NY], strip)
        else:
            out.start(w.at[K : K + NX, pl.ds(first, k)], strip)


def strips_shape(k):
    x, y = rows_shape(k, NY), rows_shape(NX, k)
    return (x, x, y, y)


def early_first_kernel(k, w_in, bx_in, by_in, bz_in, xa, ya, yb, ca, w0, bx, by, bz, inv, acc, w1, sems):
    sides = Sides()
    into = Copies(sems)
    fields = (w0, bx, by, bz)
    land_first_y(k, sides, into, {"a": ya, "b": yb}, fields)
    land_first_x("a", k, sides, into, xa, ca, None, fields)
    into.wait()

    def run(a_above):
        scale((K + 1, K + NX + C) if a_above else (K - C, K + NX), w0, bx, by, bz, inv)
        steps_of(0, k, 2, False, False, a_above, (w0, w1), bx, by, bz, inv, acc)

    on_each_side(sides, run)


def early_first(k, fields, *strips):
    return pl.pallas_call(
        functools.partial(early_first_kernel, k),
        out_shape=(EXT,) * 5 + (ACC, EXT),
        in_specs=[VMEM] * 4 + [ANY] * 4,
        out_specs=(VMEM,) * 7,
        scratch_shapes=[pltpu.SemaphoreType.DMA((20,))],
        input_output_aliases={i: i for i in range(4)},
        compiler_params=pltpu.CompilerParams(vmem_limit_bytes=2 * MIB),
        name="early_first",
    )(*fields, *strips)


def first_kernel(
    k, k_next,
    w_in, bx_in, by_in, bz_in, inv_in, acc_in, w1_in, xb, cb, z_plain, z_ends,
    w0, bx, by, bz, inv, acc, w1, xa_out, xb_out, ya_out, yb_out,
    in_sems, out_sems,
):
    sides = Sides()
    into = Copies(in_sems)
    land_first_x("b", k, sides, into, xb, cb, (z_plain, z_ends), (w0, bx, by, bz))
    into.wait()

    def run(a_above):
        scale((K - C, K + 1) if a_above else (K + NX, K + NX + C), w0, bx, by, bz, inv)
        steps_of(0, k, 2, False, True, a_above, (w0, w1), bx, by, bz, inv, acc)

    on_each_side(sides, run)
    out = Copies(out_sems)
    leave(k_next, sides, out, (w0, w1)[k % 2], xa_out, xb_out, ya_out, yb_out)
    out.wait()


def first_round(k, k_next, *arrays):
    w0, bx, by, bz, inv, acc, w1, *strips = pl.pallas_call(
        functools.partial(first_kernel, k, k_next),
        out_shape=(EXT,) * 5 + (ACC, EXT) + strips_shape(k_next),
        in_specs=[VMEM] * 7 + [ANY] * 4,
        out_specs=(VMEM,) * 7 + (ANY,) * 4,
        scratch_shapes=[pltpu.SemaphoreType.DMA((12,)), pltpu.SemaphoreType.DMA((4,))],
        input_output_aliases={i: i for i in range(7)},
        compiler_params=pltpu.CompilerParams(vmem_limit_bytes=2 * MIB),
        name="first_round",
    )(*arrays)
    return (bx, by, bz, inv), ((w0, w1)[k % 2], (w1, w0)[k % 2], acc), strips


def early_kernel(first, k, last, bx, by, bz, inv, w_in, w1_in, acc_in, xa, ya, yb, ca, w0, w1, acc, sems):
    sides = Sides()
    into = Copies(sems)
    for ab, strip in (("a", ya), ("b", yb)):
        into.start(strip, w0.at[K : K + NX, pl.ds(sides.land("gy", ab, k), k)])
    land_later_x("a", k, sides, into, xa, ca, w0)
    into.wait()
    on_each_side(sides, lambda a_above: steps_of(first, k, 1, last, False, a_above, (w0, w1), bx, by, bz, inv, acc))


def early(first, k, last, coeffs, state, *strips):
    return pl.pallas_call(
        functools.partial(early_kernel, first, k, last),
        out_shape=(EXT, EXT, ACC),
        in_specs=[VMEM] * 7 + [ANY] * 4,
        out_specs=(VMEM,) * 3,
        scratch_shapes=[pltpu.SemaphoreType.DMA((5,))],
        input_output_aliases={4: 0, 5: 1, 6: 2},
        compiler_params=pltpu.CompilerParams(vmem_limit_bytes=2 * MIB),
        name="early",
    )(*coeffs, *state, *strips)


def later_kernel(
    first, k, k_next,
    bx, by, bz, inv, w_in, w1_in, acc_in, xb, cb,
    w0, w1, acc, xa_out, xb_out, ya_out, yb_out,
    in_sems, out_sems,
):
    sides = Sides()
    into = Copies(in_sems)
    land_later_x("b", k, sides, into, xb, cb, w0)
    into.wait()
    on_each_side(sides, lambda a_above: steps_of(first, k, 1, False, True, a_above, (w0, w1), bx, by, bz, inv, acc))
    out = Copies(out_sems)
    leave(k_next, sides, out, (w0, w1)[k % 2], xa_out, xb_out, ya_out, yb_out)
    out.wait()


def later_round(first, k, k_next, *arrays):
    w0, w1, acc, *strips = pl.pallas_call(
        functools.partial(later_kernel, first, k, k_next),
        out_shape=(EXT, EXT, ACC) + strips_shape(k_next),
        in_specs=[VMEM] * 7 + [ANY] * 2,
        out_specs=(VMEM,) * 3 + (ANY,) * 4,
        scratch_shapes=[pltpu.SemaphoreType.DMA((3,)), pltpu.SemaphoreType.DMA((4,))],
        input_output_aliases={4: 0, 5: 1, 6: 2},
        compiler_params=pltpu.CompilerParams(vmem_limit_bytes=2 * MIB),
        name="later_round",
    )(*arrays)
    return ((w0, w1)[k % 2], (w1, w0)[k % 2], acc), strips


def last_kernel(
    first, k,
    tile_rows, targets, mask, slots, bx, by, bz, inv, w_in, w1_in, acc_in, xb, cb,
    grad, sent, w0, w1, acc,
    in_sems,
):
    sides = Sides()
    into = Copies(in_sems)
    land_later_x("b", k, sides, into, xb, cb, w0)
    sent[...] = jnp.zeros_like(sent)
    peers = slots.shape[0]
    sent[pl.ds(CAP, peers, stride=CAP + 1), :] = slots[...]
    into.wait()
    on_each_side(sides, lambda a_above: steps_of(first, k, 1, True, True, a_above, (w0, w1), bx, by, bz, inv, acc))
    flat = acc.reshape(NX * NY * 8, 128)

    @pl.loop(0, mask.shape[0] // 8)
    def _(t8):
        for t in range(8):
            at = t8 * 8 + t
            row = flat[pl.ds(tile_rows[at], 1), :] * mask[pl.ds(at, 1), :].astype(F32)
            sent[pl.ds(targets[at], 1), :] = row

    @pl.loop(0, NX)
    def _(x):
        for yc in range(0, NY, 8):
            for s in range(8):
                at = (x * NY + yc) * 8 + s
                grad[x, yc : yc + 8, 128 * s : 128 * s + 128] = flat[pl.ds(at, 8, stride=8), :]


def last_round(first, k, peers, *arrays):
    return pl.pallas_call(
        functools.partial(last_kernel, first, k),
        out_shape=(
            jax.ShapeDtypeStruct((NX, NY, 1024), F32),
            jax.ShapeDtypeStruct((peers * (CAP + 1), 128), F32),
            EXT,
            EXT,
            ACC,
        ),
        in_specs=[SMEM, SMEM] + [VMEM] * 9 + [ANY] * 2,
        out_specs=(VMEM,) * 5,
        scratch_shapes=[pltpu.SemaphoreType.DMA((3,))],
        input_output_aliases={8: 2, 9: 3, 10: 4},
        compiler_params=pltpu.CompilerParams(vmem_limit_bytes=6 * MIB),
        name="last_round",
    )(*arrays)[:2]


def finish_kernel(received, heights, out):
    peers = received.shape[0] // (CAP + 1)
    slots = received[pl.ds(CAP, peers, stride=CAP + 1), :].T
    n_slots = heights.shape[1]
    ids = lax.broadcasted_iota(jnp.int32, (n_slots, peers), 0).astype(F32)
    table = jnp.zeros((n_slots, 128), F32)
    for p in range(CAP):
        named = (ids == slots[p : p + 1, :]).astype(jnp.bfloat16)
        rest = received[pl.ds(p, peers, stride=CAP + 1), :]
        for _ in range(3):
            part = rest.astype(jnp.bfloat16)
            rest = rest - part.astype(F32)
            table = table + jnp.dot(named, part, preferred_element_type=F32)
    slope = 0.5 * (heights[2] - heights[0])
    bend = heights[2] - 2.0 * heights[1] + heights[0]
    denom = 1.0 + slope * slope
    factor = 1.0 / (denom * jnp.sqrt(denom))
    skew_half = -1.5 * slope * bend * factor / denom
    out[0] = table * (factor - skew_half)
    out[1] = -2.0 * table * factor
    out[2] = table * (factor + skew_half)


def finish(received, heights):
    return pl.pallas_call(
        finish_kernel,
        out_shape=jax.ShapeDtypeStruct(heights.shape, F32),
        in_specs=[VMEM, VMEM],
        out_specs=VMEM,
        compiler_params=pltpu.CompilerParams(vmem_limit_bytes=8 * MIB),
        name="finish",
    )(received, heights)


def routes(tile_owner, tile_slot, peers):
    owner = tile_owner[:, 0]
    order = jnp.arange(owner.shape[0])
    before = (owner[:, None] == owner[None, :]) & (order[None, :] < order[:, None])
    position = jnp.sum(before.astype(jnp.int32), axis=1)
    is_owner = (owner[None, :] == jnp.arange(peers)[:, None]).astype(F32)
    placed = jnp.where(position[:, None] == jnp.arange(128)[None, :], tile_slot[:, None].astype(F32), 0.0)
    slots = jnp.dot(is_owner, placed, precision=lax.Precision.HIGHEST)
    return owner * (CAP + 1) + position, slots


def shards(grad_pressure, beta, tile_rows, tile_owner, tile_slot, face_mask, heights):
    peers = lax.axis_size("gx") * lax.axis_size("gy")
    targets, slots = routes(tile_owner, tile_slot, peers)
    k = ROUNDS[0]
    *fields, xa, xb, xb_z, ya, yb = pack(k, grad_pressure, beta)
    counts = [f[1:] for f in fields_of(k)]
    xa, xb, ya, yb, ca, cb, *routed = exchange(k, counts, xa, xb, ya, yb, xb_z)
    fields = early_first(k, fields, xa, ya, yb, ca)
    coeffs, state, strips = first_round(k, ROUNDS[1], *fields, xb, cb, *routed)
    done = k
    for k, k_next in zip(ROUNDS[1:-1], ROUNDS[2:]):
        xa, xb, ya, yb, ca, cb = exchange(k - 1, [(k, k - 1)], *strips)
        state = early(done, k, False, coeffs, state, xa, ya, yb, ca)
        state, strips = later_round(done, k, k_next, *coeffs, *state, xb, cb)
        done += k
    k = ROUNDS[-1]
    xa, xb, ya, yb, ca, cb = exchange(k - 1, [(k, k - 1)], *strips)
    state = early(done, k, True, coeffs, state, xa, ya, yb, ca)
    grad_rhs, sent = last_round(done, k, peers, tile_rows, targets, face_mask, slots, *coeffs, *state, xb, cb)
    sent = sent.reshape(peers, 1, (CAP + 1) * 128)
    received = lax.all_to_all(sent, ("gx", "gy"), split_axis=0, concat_axis=0, tiled=True)
    return grad_rhs, finish(received.reshape(peers * (CAP + 1), 128), heights)


def solution(mesh):
    in_specs = (
        P("gx", "gy", None),
        P(None, "gx", "gy", None),
        P(("gx", "gy")),
        P(("gx", "gy"), None),
        P(("gx", "gy")),
        P(("gx", "gy"), None),
        P(None, ("gx", "gy"), None),
    )
    out_specs = (P("gx", "gy", None), P(None, ("gx", "gy"), None))
    return jax.shard_map(shards, mesh=mesh, in_specs=in_specs, out_specs=out_specs, check_vma=False)
```

```python
import functools
import math

import jax
import jax.numpy as jnp
from jax import lax
from jax.experimental import pallas as pl
from jax.experimental.pallas import tpu as pltpu
from jax.sharding import PartitionSpec as P

STEPS = 4
CAP = 8
LOW_BOUND = 0.1
HIGH_BOUND = 1.9

ROUNDS = (3, 4, 4)
K = max(ROUNDS)
C = K - 1
NX, NY = 8, 32
EX, EY = NX + 2 * K, NY + 2 * K
TILE = (8, 128)
ANY = pl.BlockSpec(memory_space=pl.ANY)
SMEM = pl.BlockSpec(memory_space=pltpu.SMEM)
VMEM = pl.BlockSpec(memory_space=pltpu.VMEM)
HBM = pl.BlockSpec(memory_space=pltpu.HBM)
F32 = jnp.float32
MIB = 1 << 20
EXT = pltpu.VMEM((EX, EY, *TILE), F32)
ACC = pltpu.VMEM((NX, NY, *TILE), F32)


def omega_of(step):
    j = STEPS - 1 - step % STEPS
    theta = 0.5 * (HIGH_BOUND + LOW_BOUND) + 0.5 * (HIGH_BOUND - LOW_BOUND) * math.cos(
        math.pi * (2 * j + 1) / (2 * STEPS)
    )
    return 1.0 / theta


def rows_shape(*lead):
    return jax.ShapeDtypeStruct((*lead, *TILE), F32)


def z_up(v):
    r = pltpu.roll(v, 127, 2)
    lane = lax.broadcasted_iota(jnp.int32, v.shape, 2)
    return jnp.where(lane == 127, pltpu.roll(r, 7, 1), r)


def z_down(v):
    r = pltpu.roll(v, 1, 2)
    lane = lax.broadcasted_iota(jnp.int32, v.shape, 2)
    return jnp.where(lane == 0, pltpu.roll(r, 1, 1), r)


class Sides:
    def __init__(self):
        self.above = {
            (axis, ab): (lax.axis_index(axis) % 2) == (0 if ab == "a" else 1)
            for axis in ("gx", "gy")
            for ab in ("a", "b")
        }

    def send(self, axis, ab, n):
        return jnp.where(self.above[axis, ab], (NX if axis == "gx" else NY) - n, 0)

    def land(self, axis, ab, n):
        return jnp.where(self.above[axis, ab], K + (NX if axis == "gx" else NY), K - n)


class Copies:
    def __init__(self, sems):
        self.sems = sems
        self.all = []

    def start(self, src, dst):
        copy = pltpu.make_async_copy(src, dst, self.sems.at[len(self.all)])
        copy.start()
        self.all.append(copy)

    def start_either(self, first, src, other, dst):
        sem = self.sems.at[len(self.all)]
        for wanted, ref in ((first, src), (jnp.logical_not(first), other)):
            copy = pltpu.make_async_copy(ref, dst, sem)
            pl.when(wanted)(copy.start)
        self.all.append(copy)

    def wait(self):
        for copy in self.all:
            copy.wait()


def fields_of(k):
    return ((k, k, k - 1), (k + 1, k, k), (k, k + 1, k), (k, k, k - 1))


def pack_kernel(k, g, beta, w, bx, by, bz, xa, xb, xb_z, ya, yb, nat, in_sems, out_sems):
    sides = Sides()
    copies = []
    for x in range(NX):
        copies.append(
            (
                pltpu.make_async_copy(g.at[x], nat.at[0, x], in_sems.at[0, x]),
                pltpu.make_async_copy(beta.at[:, x], nat.at[1:4, x], in_sems.at[1, x]),
            )
        )
        for c in copies[-1]:
            c.start()
    fields = (w, bx, by, bz)
    for x in range(NX):
        for c in copies[x]:
            c.wait()
        for a, field in enumerate(fields):
            flat = field.reshape(EX * EY * 8, 128)

            @pl.loop(0, NY // 8)
            def _(yc, x=x, a=a, flat=flat):
                y = pl.multiple_of(yc * 8, 8)
                for s in range(8):
                    at = ((x + K) * EY + K + y) * 8 + s
                    flat[pl.ds(at, 8, stride=8), :] = nat[a, x, pl.ds(y, 8), 128 * s : 128 * s + 128]

    out = Copies(out_sems)
    for axis, ab, strip in (("gy", "a", ya), ("gy", "b", yb), ("gx", "b", xb), ("gx", "a", xa)):
        at = 0
        for field, (in_x, in_y, _) in zip(fields, fields_of(k)):
            n = in_x if axis == "gx" else in_y
            first = sides.send(axis, ab, n) + K
            if axis == "gx":
                into = xb_z if ab == "b" and field is bz else strip.at[at : at + n]
                out.start(field.at[pl.ds(first, n), K : K + NY], into)
            else:
                out.start(field.at[K : K + NX, pl.ds(first, n)], strip.at[:, at : at + n])
            at += n
    out.wait()


def pack(k, g, beta):
    n = 4 * k + 1
    return pl.pallas_call(
        functools.partial(pack_kernel, k),
        out_shape=(EXT,) * 4
        + (rows_shape(n, NY), rows_shape(n - k, NY), rows_shape(k, NY), rows_shape(NX, n), rows_shape(NX, n)),
        in_specs=[HBM] * 2,
        out_specs=(VMEM,) * 4 + (ANY,) * 5,
        scratch_shapes=[
            pltpu.VMEM((4, NX, NY, 1024), F32),
            pltpu.SemaphoreType.DMA((2, NX)),
            pltpu.SemaphoreType.DMA((16,)),
        ],
        compiler_params=pltpu.CompilerParams(vmem_limit_bytes=8 * MIB),
        name="pack",
    )(*(pltpu.with_memory_space_constraint(array, pltpu.HBM) for array in (g, beta)))


def corner_kernel(planes, counts, ya, yb, *refs):
    ca, cb, sems = refs[-3:]
    sides = Sides()
    out = Copies(sems)
    for ab, corner in (("b", cb), ("a", ca)):
        first = sides.send("gx", ab, planes)
        for j, (other, strip) in enumerate((("a", ya), ("b", yb))):
            at = done = 0
            for n, kept in counts:
                skip = jnp.where(sides.above["gy", other], 0, n - kept)
                out.start(
                    strip.at[pl.ds(first, planes), pl.ds(at + skip, kept)],
                    corner.at[j, :, done : done + kept],
                )
                at, done = at + n, done + kept
    out.wait()


def corners(planes, counts, ya, yb, *after):
    shape = rows_shape(2, planes, sum(kept for _, kept in counts))
    return pl.pallas_call(
        functools.partial(corner_kernel, planes, counts),
        out_shape=(shape, shape),
        in_specs=[ANY] * (2 + len(after)),
        out_specs=(ANY,) * 2,
        scratch_shapes=[pltpu.SemaphoreType.DMA((4 * len(counts),))],
        compiler_params=pltpu.CompilerParams(vmem_limit_bytes=MIB),
        cost_estimate=pl.CostEstimate(flops=10**10 if len(counts) == 1 else 0, bytes_accessed=MIB, transcendentals=0),
        name="corners",
    )(ya, yb, *after)


def swap(array, axis, ab):
    size = lax.axis_size(axis)
    pairs = [(i, i ^ 1 if ab == "a" else ((i + 1) ^ 1) - 1) for i in range(size)]
    return lax.ppermute(array, axis, [(i, j) for i, j in pairs if 0 <= j < size])


def relay_kernel(array, after, out, sem):
    copy = pltpu.make_async_copy(array, out, sem)
    copy.start()
    copy.wait()


def relay(array, after):
    return pl.pallas_call(
        relay_kernel,
        out_shape=jax.ShapeDtypeStruct(array.shape, F32),
        in_specs=[ANY] * 2,
        out_specs=ANY,
        scratch_shapes=[pltpu.SemaphoreType.DMA(())],
        compiler_params=pltpu.CompilerParams(vmem_limit_bytes=MIB),
        name="relay",
    )(array, after)


def exchange(planes, counts, xa, xb, ya, yb, xb_z=None, *after):
    size = lax.axis_size("gx")
    middle = size // 2
    if xb_z is not None:
        pairs = [(i, ((i + 1) ^ 1) - 1) for i in range(1, size - 1) if i not in (middle - 1, middle)]
        xb_z = lax.ppermute(xb_z, "gx", pairs + [(middle - 1, 0), (middle, size - 1)])
    ya, yb = swap(ya, "gy", "a"), swap(yb, "gy", "b")
    xb, xa = swap(xb, "gx", "b"), swap(xa, "gx", "a")
    ca, cb = corners(planes, counts, ya, yb, *after)
    cb, ca = swap(cb, "gx", "b"), swap(ca, "gx", "a")
    if xb_z is None:
        return xa, xb, ya, yb, ca, cb
    onward = lax.ppermute(relay(xb_z, ca), "gx", [(0, middle), (size - 1, middle - 1)])
    return xa, xb, ya, yb, ca, cb, xb_z, onward


def land_first_y(k, sides, into, ys, fields):
    at = 0
    for field, (_, n, _) in zip(fields, fields_of(k)):
        for ab in ("a", "b"):
            into.start(ys[ab].at[:, at : at + n], field.at[K : K + NX, pl.ds(sides.land("gy", ab, n), n)])
        at += n


def land_first_x(ab, k, sides, into, strip, corner, routed, fields):
    at_x = at_c = 0
    for i, (in_x, _, in_c) in enumerate(fields_of(k)):
        x_halo = fields[i].at[pl.ds(sides.land("gx", ab, in_x), in_x), K : K + NY]
        if ab == "b" and i == 3:
            me, size = lax.axis_index("gx"), lax.axis_size("gx")
            by_ends = (me == 0) | (me == size // 2 - 1) | (me == size // 2) | (me == size - 1)
            into.start_either(by_ends, routed[1], routed[0], x_halo)
        else:
            into.start(strip.at[at_x : at_x + in_x], x_halo)
        x = sides.land("gx", ab, k)
        for j, other in enumerate(("a", "b")):
            y = sides.land("gy", other, in_c)
            into.start(corner.at[j, :, at_c : at_c + in_c], fields[i].at[pl.ds(x, k), pl.ds(y, in_c)])
        at_x, at_c = at_x + in_x, at_c + in_c


def land_later_x(ab, k, sides, into, strip, corner, w):
    into.start(strip, w.at[pl.ds(sides.land("gx", ab, k), k), K : K + NY])
    x = sides.land("gx", ab, k - 1)
    for j, other in enumerate(("a", "b")):
        y = sides.land("gy", other, k - 1)
        into.start(corner.at[j], w.at[pl.ds(x, k - 1), pl.ds(y, k - 1)])


def chunks(low, high, size=8):
    return [(y, min(size, high - y)) for y in range(low, high, size)]


def scale(planes, rows, w, bx, by, bz, inv):
    @pl.loop(*planes)
    def _(x):
        for y, n in chunks(*rows):
            b = bz[x, y : y + n]
            sub = lax.broadcasted_iota(jnp.int32, b.shape, 1)
            lane = lax.broadcasted_iota(jnp.int32, b.shape, 2)
            inner = jnp.where((sub == 7) & (lane == 127), 0.0, b)
            beside = by[x, y - 1 : y + n]
            diagonal = bx[x, y : y + n] + bx[x - 1, y : y + n] + beside[1:] + beside[:-1] + b + z_down(inner)
            inverse = jnp.where(b > 0.0, 1.0 / jnp.where(b > 0.0, diagonal, 1.0), 0.0)
            inv[x, y : y + n] = inverse
            w[x, y : y + n] = w[x, y : y + n] * inverse
            bz[x, y : y + n] = inner


def one_step(step, reach, last, span, w, new, bx, by, bz, inv, acc):
    omega = omega_of(step)

    low, high = span

    def walk(y, n, rows_inside):
        below = bx[low - 1, pl.ds(y, n)] * w[low - 1, pl.ds(y, n)]
        around = w[low, pl.ds(y - 1, n + 2)]
        for x in range(low, high):
            above = w[x + 1, pl.ds(y - 1, n + 2)]
            centre = around[1:-1]
            link = bx[x, pl.ds(y, n)]
            beside = by[x, pl.ds(y - 1, n + 1)]
            along = bz[x, pl.ds(y, n)]
            total = link * above[1:-1] + below
            total = total + beside[1:] * around[2:] + beside[:-1] * around[:-2]
            total = total + along * z_up(centre) + z_down(along * centre)
            moved = centre + omega * (inv[x, pl.ds(y, n)] * total - centre)
            if not last:
                new[x, pl.ds(y, n)] = moved
            if rows_inside and K <= x < K + NX:
                at = (x - K, pl.ds(y - K, n))
                term = omega * centre
                if last:
                    term = term + omega_of(step + 1) * moved
                acc[at] = term if step == 0 else acc[at] + term
            below, around = link * centre, above

    if reach:
        walk(K - reach, reach, False)
        walk(K + NY, reach, False)

    @pl.loop(0, NY // 8)
    def _(i):
        walk(K + i * 8, 8, True)


def spans_of(i, k, lead, a_above):
    low, high = K - (k - 1 - i), K + NX + k - 1 - i
    cut = K + lead + i if a_above else K + NX - 1 - i
    return ((cut, high), (low, cut)) if a_above else ((low, cut), (cut, high))


def steps_of(first, k, lead, last, late, a_above, w, *arrays):
    for i in range(k):
        span = spans_of(i, k, lead, a_above)[late]
        one_step(first + i, k - 1 - i, last and i == k - 1, span, w[i % 2], w[1 - i % 2], *arrays)


def on_each_side(sides, run):
    a_above = sides.above["gx", "a"]
    pl.when(a_above)(functools.partial(run, True))
    pl.when(jnp.logical_not(a_above))(functools.partial(run, False))


def leave(k, sides, out, w, xa, xb, ya, yb):
    for axis, ab, strip in (("gy", "a", ya), ("gy", "b", yb), ("gx", "b", xb), ("gx", "a", xa)):
        first = sides.send(axis, ab, k) + K
        if axis == "gx":
            out.start(w.at[pl.ds(first, k), K : K + NY], strip)
        else:
            out.start(w.at[K : K + NX, pl.ds(first, k)], strip)


def strips_shape(k):
    x, y = rows_shape(k, NY), rows_shape(NX, k)
    return (x, x, y, y)


ALL_ROWS = (K - C, K + NY + C)
CORE = (K + 1, K + NX), (K + 1, K + NY)


def scale_kernel(w_in, bx, by, bz_in, w, bz, inv):
    scale(*CORE, w, bx, by, bz, inv)


def scale_core(w, bx, by, bz):
    w, bz, inv = pl.pallas_call(
        scale_kernel,
        out_shape=(EXT,) * 3,
        in_specs=[VMEM] * 4,
        out_specs=(VMEM,) * 3,
        input_output_aliases={0: 0, 3: 1},
        compiler_params=pltpu.CompilerParams(vmem_limit_bytes=2 * MIB),
        name="scale_core",
    )(w, bx, by, bz)
    return w, bx, by, bz, inv


def early_first_kernel(
    k, w_in, bx_in, by_in, bz_in, inv_in, xa, ya, yb, ca, w0, bx, by, bz, inv, acc, w1, sems
):
    sides = Sides()
    into = Copies(sems)
    fields = (w0, bx, by, bz)
    land_first_y(k, sides, into, {"a": ya, "b": yb}, fields)
    land_first_x("a", k, sides, into, xa, ca, None, fields)
    into.wait()

    def run(a_above):
        arrays = (w0, bx, by, bz, inv)
        scale(CORE[0], (K - C, K + 1), *arrays)
        scale(CORE[0], (K + NY, K + NY + C), *arrays)
        scale((K + NX, K + NX + C) if a_above else (K - C, K + 1), ALL_ROWS, *arrays)
        steps_of(0, k, 2, False, False, a_above, (w0, w1), bx, by, bz, inv, acc)

    on_each_side(sides, run)


def early_first(k, fields, *strips):
    return pl.pallas_call(
        functools.partial(early_first_kernel, k),
        out_shape=(EXT,) * 5 + (ACC, EXT),
        in_specs=[VMEM] * 5 + [ANY] * 4,
        out_specs=(VMEM,) * 7,
        scratch_shapes=[pltpu.SemaphoreType.DMA((20,))],
        input_output_aliases={i: i for i in range(5)},
        compiler_params=pltpu.CompilerParams(vmem_limit_bytes=2 * MIB),
        name="early_first",
    )(*fields, *strips)


def first_kernel(
    k, k_next,
    w_in, bx_in, by_in, bz_in, inv_in, acc_in, w1_in, xb, cb, z_plain, z_ends,
    w0, bx, by, bz, inv, acc, w1, xa_out, xb_out, ya_out, yb_out,
    in_sems, out_sems,
):
    sides = Sides()
    into = Copies(in_sems)
    land_first_x("b", k, sides, into, xb, cb, (z_plain, z_ends), (w0, bx, by, bz))
    into.wait()

    def run(a_above):
        scale((K - C, K + 1) if a_above else (K + NX, K + NX + C), ALL_ROWS, w0, bx, by, bz, inv)
        steps_of(0, k, 2, False, True, a_above, (w0, w1), bx, by, bz, inv, acc)

    on_each_side(sides, run)
    out = Copies(out_sems)
    leave(k_next, sides, out, (w0, w1)[k % 2], xa_out, xb_out, ya_out, yb_out)
    out.wait()


def first_round(k, k_next, *arrays):
    w0, bx, by, bz, inv, acc, w1, *strips = pl.pallas_call(
        functools.partial(first_kernel, k, k_next),
        out_shape=(EXT,) * 5 + (ACC, EXT) + strips_shape(k_next),
        in_specs=[VMEM] * 7 + [ANY] * 4,
        out_specs=(VMEM,) * 7 + (ANY,) * 4,
        scratch_shapes=[pltpu.SemaphoreType.DMA((12,)), pltpu.SemaphoreType.DMA((4,))],
        input_output_aliases={i: i for i in range(7)},
        compiler_params=pltpu.CompilerParams(vmem_limit_bytes=2 * MIB),
        name="first_round",
    )(*arrays)
    return (bx, by, bz, inv), ((w0, w1)[k % 2], (w1, w0)[k % 2], acc), strips


def early_kernel(first, k, last, bx, by, bz, inv, w_in, w1_in, acc_in, xa, ya, yb, ca, w0, w1, acc, sems):
    sides = Sides()
    into = Copies(sems)
    for ab, strip in (("a", ya), ("b", yb)):
        into.start(strip, w0.at[K : K + NX, pl.ds(sides.land("gy", ab, k), k)])
    land_later_x("a", k, sides, into, xa, ca, w0)
    into.wait()
    on_each_side(sides, lambda a_above: steps_of(first, k, 1, last, False, a_above, (w0, w1), bx, by, bz, inv, acc))


def early(first, k, last, coeffs, state, *strips):
    return pl.pallas_call(
        functools.partial(early_kernel, first, k, last),
        out_shape=(EXT, EXT, ACC),
        in_specs=[VMEM] * 7 + [ANY] * 4,
        out_specs=(VMEM,) * 3,
        scratch_shapes=[pltpu.SemaphoreType.DMA((5,))],
        input_output_aliases={4: 0, 5: 1, 6: 2},
        compiler_params=pltpu.CompilerParams(vmem_limit_bytes=2 * MIB),
        name="early",
    )(*coeffs, *state, *strips)


def later_kernel(
    first, k, k_next,
    bx, by, bz, inv, w_in, w1_in, acc_in, xb, cb,
    w0, w1, acc, xa_out, xb_out, ya_out, yb_out,
    in_sems, out_sems,
):
    sides = Sides()
    into = Copies(in_sems)
    land_later_x("b", k, sides, into, xb, cb, w0)
    into.wait()
    on_each_side(sides, lambda a_above: steps_of(first, k, 1, False, True, a_above, (w0, w1), bx, by, bz, inv, acc))
    out = Copies(out_sems)
    leave(k_next, sides, out, (w0, w1)[k % 2], xa_out, xb_out, ya_out, yb_out)
    out.wait()


def later_round(first, k, k_next, *arrays):
    w0, w1, acc, *strips = pl.pallas_call(
        functools.partial(later_kernel, first, k, k_next),
        out_shape=(EXT, EXT, ACC) + strips_shape(k_next),
        in_specs=[VMEM] * 7 + [ANY] * 2,
        out_specs=(VMEM,) * 3 + (ANY,) * 4,
        scratch_shapes=[pltpu.SemaphoreType.DMA((3,)), pltpu.SemaphoreType.DMA((4,))],
        input_output_aliases={4: 0, 5: 1, 6: 2},
        compiler_params=pltpu.CompilerParams(vmem_limit_bytes=2 * MIB),
        name="later_round",
    )(*arrays)
    return ((w0, w1)[k % 2], (w1, w0)[k % 2], acc), strips


def last_kernel(
    first, k,
    tile_rows, targets, mask, slots, bx, by, bz, inv, w_in, w1_in, acc_in, xb, cb,
    grad, sent, w0, w1, acc,
    nat, in_sems, out_sems,
):
    sides = Sides()
    into = Copies(in_sems)
    land_later_x("b", k, sides, into, xb, cb, w0)
    sent[...] = jnp.zeros_like(sent)
    peers = slots.shape[0]
    sent[pl.ds(CAP, peers, stride=CAP + 1), :] = slots[...]
    into.wait()
    on_each_side(sides, lambda a_above: steps_of(first, k, 1, True, True, a_above, (w0, w1), bx, by, bz, inv, acc))
    flat = acc.reshape(NX * NY * 8, 128)

    @pl.loop(0, NX)
    def _(x):
        for yc in range(0, NY, 8):
            for s in range(8):
                at = (x * NY + yc) * 8 + s
                nat[x, yc : yc + 8, 128 * s : 128 * s + 128] = flat[pl.ds(at, 8, stride=8), :]
        pltpu.make_async_copy(nat.at[x], grad.at[x], out_sems.at[x]).start()

    @pl.loop(0, mask.shape[0] // 8)
    def _(t8):
        for t in range(8):
            at = t8 * 8 + t
            row = flat[pl.ds(tile_rows[at], 1), :] * mask[pl.ds(at, 1), :].astype(F32)
            sent[pl.ds(targets[at], 1), :] = row

    for x in range(NX):
        pltpu.make_async_copy(nat.at[x], grad.at[x], out_sems.at[x]).wait()


def last_round(first, k, peers, *arrays):
    return pl.pallas_call(
        functools.partial(last_kernel, first, k),
        out_shape=(
            pltpu.HBM((NX, NY, 1024), F32),
            jax.ShapeDtypeStruct((peers * (CAP + 1), 128), F32),
            EXT,
            EXT,
            ACC,
        ),
        in_specs=[SMEM, SMEM] + [VMEM] * 9 + [ANY] * 2,
        out_specs=(HBM,) + (VMEM,) * 4,
        scratch_shapes=[
            pltpu.VMEM((NX, NY, 1024), F32),
            pltpu.SemaphoreType.DMA((3,)),
            pltpu.SemaphoreType.DMA((NX,)),
        ],
        input_output_aliases={8: 2, 9: 3, 10: 4},
        compiler_params=pltpu.CompilerParams(vmem_limit_bytes=6 * MIB),
        name="last_round",
    )(*arrays)[:2]


def finish_kernel(received, heights, out):
    peers = received.shape[0] // (CAP + 1)
    slots = received[pl.ds(CAP, peers, stride=CAP + 1), :].T
    n_slots = heights.shape[1]
    ids = lax.broadcasted_iota(jnp.int32, (n_slots, peers), 0).astype(F32)
    named = jnp.concatenate([(ids == slots[p : p + 1, :]).astype(jnp.bfloat16) for p in range(CAP)], axis=1)
    rest = jnp.concatenate([received[pl.ds(p, peers, stride=CAP + 1), :] for p in range(CAP)], axis=0)
    parts = []
    for _ in range(3):
        parts.append(rest.astype(jnp.bfloat16))
        rest = rest - parts[-1].astype(F32)
    sums = jnp.dot(named, jnp.concatenate(parts, axis=1), preferred_element_type=F32)
    table = sums[:, :128] + (sums[:, 128:256] + sums[:, 256:])
    slope = 0.5 * (heights[2] - heights[0])
    bend = heights[2] - 2.0 * heights[1] + heights[0]
    denom = 1.0 + slope * slope
    factor = 1.0 / (denom * jnp.sqrt(denom))
    skew_half = -1.5 * slope * bend * factor / denom
    out[0] = table * (factor - skew_half)
    out[1] = -2.0 * table * factor
    out[2] = table * (factor + skew_half)


def finish(received, heights):
    return pl.pallas_call(
        finish_kernel,
        out_shape=jax.ShapeDtypeStruct(heights.shape, F32),
        in_specs=[VMEM, VMEM],
        out_specs=VMEM,
        compiler_params=pltpu.CompilerParams(vmem_limit_bytes=8 * MIB),
        name="finish",
    )(received, heights)


def routes(tile_owner, tile_slot, peers):
    owner = tile_owner[:, 0]
    order = jnp.arange(owner.shape[0])
    before = (owner[:, None] == owner[None, :]) & (order[None, :] < order[:, None])
    position = jnp.sum(before.astype(jnp.int32), axis=1)
    is_owner = (owner[None, :] == jnp.arange(peers)[:, None]).astype(F32)
    placed = jnp.where(position[:, None] == jnp.arange(128)[None, :], tile_slot[:, None].astype(F32), 0.0)
    slots = jnp.dot(is_owner, placed, precision=lax.Precision.HIGHEST)
    return owner * (CAP + 1) + position, slots


def shards(grad_pressure, beta, tile_rows, tile_owner, tile_slot, face_mask, heights):
    peers = lax.axis_size("gx") * lax.axis_size("gy")
    targets, slots = routes(tile_owner, tile_slot, peers)
    k = ROUNDS[0]
    *fields, xa, xb, xb_z, ya, yb = pack(k, grad_pressure, beta)
    counts = [f[1:] for f in fields_of(k)]
    fields = scale_core(*fields)
    xa, xb, ya, yb, ca, cb, *routed = exchange(k, counts, xa, xb, ya, yb, xb_z, fields[-1])
    fields = early_first(k, fields, xa, ya, yb, ca)
    coeffs, state, strips = first_round(k, ROUNDS[1], *fields, xb, cb, *routed)
    done = k
    for k, k_next in zip(ROUNDS[1:-1], ROUNDS[2:]):
        xa, xb, ya, yb, ca, cb = exchange(k - 1, [(k, k - 1)], *strips)
        state = early(done, k, False, coeffs, state, xa, ya, yb, ca)
        state, strips = later_round(done, k, k_next, *coeffs, *state, xb, cb)
        done += k
    k = ROUNDS[-1]
    xa, xb, ya, yb, ca, cb = exchange(k - 1, [(k, k - 1)], *strips)
    state = early(done, k, True, coeffs, state, xa, ya, yb, ca)
    grad_rhs, sent = last_round(done, k, peers, tile_rows, targets, face_mask, slots, *coeffs, *state, xb, cb)
    sent = sent.reshape(peers, 1, (CAP + 1) * 128)
    received = lax.all_to_all(sent, ("gx", "gy"), split_axis=0, concat_axis=0, tiled=True)
    return grad_rhs, finish(received.reshape(peers * (CAP + 1), 128), heights)


def solution(mesh):
    in_specs = (
        P("gx", "gy", None),
        P(None, "gx", "gy", None),
        P(("gx", "gy")),
        P(("gx", "gy"), None),
        P(("gx", "gy")),
        P(("gx", "gy"), None),
        P(None, ("gx", "gy"), None),
    )
    out_specs = (P("gx", "gy", None), P(None, ("gx", "gy"), None))
    return jax.shard_map(shards, mesh=mesh, in_specs=in_specs, out_specs=out_specs, check_vma=False)
```

```python
import functools
import math

import jax
import jax.numpy as jnp
from jax import lax
from jax.experimental import pallas as pl
from jax.experimental.pallas import tpu as pltpu
from jax.sharding import PartitionSpec as P

STEPS = 4
CAP = 8
LOW_BOUND = 0.1
HIGH_BOUND = 1.9

ROUNDS = (3, 4, 4)
K = max(ROUNDS)
C = K - 1
NX, NY = 8, 32
EX, EY = NX + 2 * K, NY + 2 * K
TILE = (8, 128)
ANY = pl.BlockSpec(memory_space=pl.ANY)
SMEM = pl.BlockSpec(memory_space=pltpu.SMEM)
VMEM = pl.BlockSpec(memory_space=pltpu.VMEM)
HBM = pl.BlockSpec(memory_space=pltpu.HBM)
F32 = jnp.float32
MIB = 1 << 20
EXT = pltpu.VMEM((EX, EY, *TILE), F32)
ACC = pltpu.VMEM((NX, NY, *TILE), F32)


def omega_of(step):
    j = STEPS - 1 - step % STEPS
    theta = 0.5 * (HIGH_BOUND + LOW_BOUND) + 0.5 * (HIGH_BOUND - LOW_BOUND) * math.cos(
        math.pi * (2 * j + 1) / (2 * STEPS)
    )
    return 1.0 / theta


def rows_shape(*lead):
    return jax.ShapeDtypeStruct((*lead, *TILE), F32)


def z_up(v):
    r = pltpu.roll(v, 127, 2)
    lane = lax.broadcasted_iota(jnp.int32, v.shape, 2)
    return jnp.where(lane == 127, pltpu.roll(r, 7, 1), r)


def z_down(v):
    r = pltpu.roll(v, 1, 2)
    lane = lax.broadcasted_iota(jnp.int32, v.shape, 2)
    return jnp.where(lane == 0, pltpu.roll(r, 1, 1), r)


class Sides:
    def __init__(self):
        self.above = {
            (axis, ab): (lax.axis_index(axis) % 2) == (0 if ab == "a" else 1)
            for axis in ("gx", "gy")
            for ab in ("a", "b")
        }

    def send(self, axis, ab, n):
        return jnp.where(self.above[axis, ab], (NX if axis == "gx" else NY) - n, 0)

    def land(self, axis, ab, n):
        return jnp.where(self.above[axis, ab], K + (NX if axis == "gx" else NY), K - n)


class Copies:
    def __init__(self, sems):
        self.sems = sems
        self.all = []

    def start(self, src, dst):
        copy = pltpu.make_async_copy(src, dst, self.sems.at[len(self.all)])
        copy.start()
        self.all.append(copy)

    def start_either(self, first, src, other, dst):
        sem = self.sems.at[len(self.all)]
        for wanted, ref in ((first, src), (jnp.logical_not(first), other)):
            copy = pltpu.make_async_copy(ref, dst, sem)
            pl.when(wanted)(copy.start)
        self.all.append(copy)

    def wait(self):
        for copy in self.all:
            copy.wait()


def fields_of(k):
    return ((k, k, k - 1), (k + 1, k, k), (k, k + 1, k), (k, k, k - 1))


def pack_kernel(k, g, beta, w, bx, by, bz, xa, xb, xb_z, ya, yb, nat, in_sems, out_sems):
    sides = Sides()
    copies = []
    for x in range(NX):
        copies.append(
            (
                pltpu.make_async_copy(g.at[x], nat.at[0, x], in_sems.at[0, x]),
                pltpu.make_async_copy(beta.at[:, x], nat.at[1:4, x], in_sems.at[1, x]),
            )
        )
        for c in copies[-1]:
            c.start()
    fields = (w, bx, by, bz)
    for x in range(NX):
        for c in copies[x]:
            c.wait()
        for a, field in enumerate(fields):
            flat = field.reshape(EX * EY * 8, 128)

            @pl.loop(0, NY // 8)
            def _(yc, x=x, a=a, flat=flat):
                y = pl.multiple_of(yc * 8, 8)
                for s in range(8):
                    at = ((x + K) * EY + K + y) * 8 + s
                    flat[pl.ds(at, 8, stride=8), :] = nat[a, x, pl.ds(y, 8), 128 * s : 128 * s + 128]

    out = Copies(out_sems)
    for axis, ab, strip in (("gy", "a", ya), ("gy", "b", yb), ("gx", "b", xb), ("gx", "a", xa)):
        at = 0
        for field, (in_x, in_y, _) in zip(fields, fields_of(k)):
            n = in_x if axis == "gx" else in_y
            first = sides.send(axis, ab, n) + K
            if axis == "gx":
                into = xb_z if ab == "b" and field is bz else strip.at[at : at + n]
                out.start(field.at[pl.ds(first, n), K : K + NY], into)
            else:
                out.start(field.at[K : K + NX, pl.ds(first, n)], strip.at[:, at : at + n])
            at += n
    out.wait()


def pack(k, g, beta):
    n = 4 * k + 1
    return pl.pallas_call(
        functools.partial(pack_kernel, k),
        out_shape=(EXT,) * 4
        + (rows_shape(n, NY), rows_shape(n - k, NY), rows_shape(k, NY), rows_shape(NX, n), rows_shape(NX, n)),
        in_specs=[HBM] * 2,
        out_specs=(VMEM,) * 4 + (ANY,) * 5,
        scratch_shapes=[
            pltpu.VMEM((4, NX, NY, 1024), F32),
            pltpu.SemaphoreType.DMA((2, NX)),
            pltpu.SemaphoreType.DMA((16,)),
        ],
        compiler_params=pltpu.CompilerParams(vmem_limit_bytes=8 * MIB),
        name="pack",
    )(*(pltpu.with_memory_space_constraint(array, pltpu.HBM) for array in (g, beta)))


def corner_kernel(planes, counts, ya, yb, *refs):
    ca, cb, sems = refs[-3:]
    sides = Sides()
    out = Copies(sems)
    for ab, corner in (("b", cb), ("a", ca)):
        first = sides.send("gx", ab, planes)
        for j, (other, strip) in enumerate((("a", ya), ("b", yb))):
            at = done = 0
            for n, kept in counts:
                skip = jnp.where(sides.above["gy", other], 0, n - kept)
                out.start(
                    strip.at[pl.ds(first, planes), pl.ds(at + skip, kept)],
                    corner.at[j, :, done : done + kept],
                )
                at, done = at + n, done + kept
    out.wait()


def corners(planes, counts, ya, yb, *after):
    shape = rows_shape(2, planes, sum(kept for _, kept in counts))
    return pl.pallas_call(
        functools.partial(corner_kernel, planes, counts),
        out_shape=(shape, shape),
        in_specs=[ANY] * (2 + len(after)),
        out_specs=(ANY,) * 2,
        scratch_shapes=[pltpu.SemaphoreType.DMA((4 * len(counts),))],
        compiler_params=pltpu.CompilerParams(vmem_limit_bytes=MIB),
        cost_estimate=pl.CostEstimate(flops=10**10 if len(counts) == 1 else 0, bytes_accessed=MIB, transcendentals=0),
        name="corners",
    )(ya, yb, *after)


def swap(array, axis, ab):
    size = lax.axis_size(axis)
    pairs = [(i, i ^ 1 if ab == "a" else ((i + 1) ^ 1) - 1) for i in range(size)]
    return lax.ppermute(array, axis, [(i, j) for i, j in pairs if 0 <= j < size])


def relay_kernel(array, after, out, sem):
    copy = pltpu.make_async_copy(array, out, sem)
    copy.start()
    copy.wait()


def relay(array, after):
    return pl.pallas_call(
        relay_kernel,
        out_shape=jax.ShapeDtypeStruct(array.shape, F32),
        in_specs=[ANY] * 2,
        out_specs=ANY,
        scratch_shapes=[pltpu.SemaphoreType.DMA(())],
        compiler_params=pltpu.CompilerParams(vmem_limit_bytes=MIB),
        name="relay",
    )(array, after)


def exchange(planes, counts, xa, xb, ya, yb, xb_z=None, meanwhile=None):
    size = lax.axis_size("gx")
    middle = size // 2
    if xb_z is not None:
        pairs = [(i, ((i + 1) ^ 1) - 1) for i in range(1, size - 1) if i not in (middle - 1, middle)]
        xb_z = lax.ppermute(xb_z, "gx", pairs + [(middle - 1, 0), (middle, size - 1)])
    ya, yb = swap(ya, "gy", "a"), swap(yb, "gy", "b")
    xb, xa = swap(xb, "gx", "b"), swap(xa, "gx", "a")
    worked = meanwhile(xa) if meanwhile else ()
    ca, cb = corners(planes, counts, ya, yb, *worked[-1:])
    cb, ca = swap(cb, "gx", "b"), swap(ca, "gx", "a")
    if xb_z is None:
        return xa, xb, ya, yb, ca, cb
    onward = lax.ppermute(relay(xb_z, ca), "gx", [(0, middle), (size - 1, middle - 1)])
    return worked, xb, ya, yb, ca, cb, xb_z, onward


def land_first_y(k, sides, into, ys, fields):
    at = 0
    for field, (_, n, _) in zip(fields, fields_of(k)):
        for ab in ("a", "b"):
            into.start(ys[ab].at[:, at : at + n], field.at[K : K + NX, pl.ds(sides.land("gy", ab, n), n)])
        at += n


def land_first_x(ab, k, sides, into, strip, corner, routed, fields):
    at_x = at_c = 0
    for i, (in_x, _, in_c) in enumerate(fields_of(k)):
        x_halo = fields[i].at[pl.ds(sides.land("gx", ab, in_x), in_x), K : K + NY]
        if strip is not None and ab == "b" and i == 3:
            me, size = lax.axis_index("gx"), lax.axis_size("gx")
            by_ends = (me == 0) | (me == size // 2 - 1) | (me == size // 2) | (me == size - 1)
            into.start_either(by_ends, routed[1], routed[0], x_halo)
        elif strip is not None:
            into.start(strip.at[at_x : at_x + in_x], x_halo)
        x = sides.land("gx", ab, k)
        for j, other in enumerate(("a", "b")):
            if corner is not None:
                y = sides.land("gy", other, in_c)
                into.start(corner.at[j, :, at_c : at_c + in_c], fields[i].at[pl.ds(x, k), pl.ds(y, in_c)])
        at_x, at_c = at_x + in_x, at_c + in_c


def land_later_x(ab, k, sides, into, strip, corner, w):
    into.start(strip, w.at[pl.ds(sides.land("gx", ab, k), k), K : K + NY])
    x = sides.land("gx", ab, k - 1)
    for j, other in enumerate(("a", "b")):
        y = sides.land("gy", other, k - 1)
        into.start(corner.at[j], w.at[pl.ds(x, k - 1), pl.ds(y, k - 1)])


def chunks(low, high, size=8):
    return [(y, min(size, high - y)) for y in range(low, high, size)]


def scale(planes, rows, w, bx, by, bz, inv):
    @pl.loop(*planes)
    def _(x):
        for y, n in chunks(*rows):
            b = bz[x, y : y + n]
            sub = lax.broadcasted_iota(jnp.int32, b.shape, 1)
            lane = lax.broadcasted_iota(jnp.int32, b.shape, 2)
            inner = jnp.where((sub == 7) & (lane == 127), 0.0, b)
            beside = by[x, y - 1 : y + n]
            diagonal = bx[x, y : y + n] + bx[x - 1, y : y + n] + beside[1:] + beside[:-1] + b + z_down(inner)
            inverse = jnp.where(b > 0.0, 1.0 / jnp.where(b > 0.0, diagonal, 1.0), 0.0)
            inv[x, y : y + n] = inverse
            w[x, y : y + n] = w[x, y : y + n] * inverse
            bz[x, y : y + n] = inner


def one_step(step, reach, last, span, w, new, bx, by, bz, inv, acc):
    omega = omega_of(step)

    low, high = span

    def walk(y, n, rows_inside):
        below = bx[low - 1, pl.ds(y, n)] * w[low - 1, pl.ds(y, n)]
        around = w[low, pl.ds(y - 1, n + 2)]
        for x in range(low, high):
            above = w[x + 1, pl.ds(y - 1, n + 2)]
            centre = around[1:-1]
            link = bx[x, pl.ds(y, n)]
            beside = by[x, pl.ds(y - 1, n + 1)]
            along = bz[x, pl.ds(y, n)]
            total = link * above[1:-1] + below
            total = total + beside[1:] * around[2:] + beside[:-1] * around[:-2]
            total = total + along * z_up(centre) + z_down(along * centre)
            moved = centre + omega * (inv[x, pl.ds(y, n)] * total - centre)
            if not last:
                new[x, pl.ds(y, n)] = moved
            if rows_inside and K <= x < K + NX:
                at = (x - K, pl.ds(y - K, n))
                term = omega * centre
                if last:
                    term = term + omega_of(step + 1) * moved
                acc[at] = term if step == 0 else acc[at] + term
            below, around = link * centre, above

    if reach:
        walk(K - reach, reach, False)
        walk(K + NY, reach, False)

    @pl.loop(0, NY // 8)
    def _(i):
        walk(K + i * 8, 8, True)


def spans_of(i, k, lead, a_above):
    low, high = K - (k - 1 - i), K + NX + k - 1 - i
    cut = K + lead + i if a_above else K + NX - 1 - i
    return ((cut, high), (low, cut)) if a_above else ((low, cut), (cut, high))


def steps_of(first, k, lead, last, late, a_above, w, *arrays):
    for i in range(k):
        span = spans_of(i, k, lead, a_above)[late]
        one_step(first + i, k - 1 - i, last and i == k - 1, span, w[i % 2], w[1 - i % 2], *arrays)


def on_each_side(sides, run):
    a_above = sides.above["gx", "a"]
    pl.when(a_above)(functools.partial(run, True))
    pl.when(jnp.logical_not(a_above))(functools.partial(run, False))


def leave(k, sides, out, w, xa, xb, ya, yb):
    for axis, ab, strip in (("gy", "a", ya), ("gy", "b", yb), ("gx", "b", xb), ("gx", "a", xa)):
        first = sides.send(axis, ab, k) + K
        if axis == "gx":
            out.start(w.at[pl.ds(first, k), K : K + NY], strip)
        else:
            out.start(w.at[K : K + NX, pl.ds(first, k)], strip)


def strips_shape(k):
    x, y = rows_shape(k, NY), rows_shape(NX, k)
    return (x, x, y, y)


ALL_ROWS = (K - C, K + NY + C)
CORE_ROWS = (K + 1, K + NY)


def early_planes(a_above):
    return (K + 1, K + NX + C) if a_above else (K - C, K + NX)


def scale_kernel(k, w_in, bx_in, by_in, bz_in, xa, w, bx, by, bz, inv, sems):
    sides = Sides()
    into = Copies(sems)
    land_first_x("a", k, sides, into, xa, None, None, (w, bx, by, bz))
    into.wait()
    on_each_side(sides, lambda a_above: scale(early_planes(a_above), CORE_ROWS, w, bx, by, bz, inv))


def scale_core(k, fields, xa):
    return pl.pallas_call(
        functools.partial(scale_kernel, k),
        out_shape=(EXT,) * 5,
        in_specs=[VMEM] * 4 + [ANY],
        out_specs=(VMEM,) * 5,
        scratch_shapes=[pltpu.SemaphoreType.DMA((4,))],
        input_output_aliases={i: i for i in range(4)},
        compiler_params=pltpu.CompilerParams(vmem_limit_bytes=2 * MIB),
        name="scale_core",
    )(*fields, xa)


def early_first_kernel(
    k, w_in, bx_in, by_in, bz_in, inv_in, ya, yb, ca, w0, bx, by, bz, inv, acc, w1, sems
):
    sides = Sides()
    into = Copies(sems)
    fields = (w0, bx, by, bz)
    land_first_y(k, sides, into, {"a": ya, "b": yb}, fields)
    land_first_x("a", k, sides, into, None, ca, None, fields)
    into.wait()

    def run(a_above):
        arrays = (w0, bx, by, bz, inv)
        scale(early_planes(a_above), (K - C, K + 1), *arrays)
        scale(early_planes(a_above), (K + NY, K + NY + C), *arrays)
        steps_of(0, k, 2, False, False, a_above, (w0, w1), bx, by, bz, inv, acc)

    on_each_side(sides, run)


def early_first(k, fields, *strips):
    return pl.pallas_call(
        functools.partial(early_first_kernel, k),
        out_shape=(EXT,) * 5 + (ACC, EXT),
        in_specs=[VMEM] * 5 + [ANY] * 3,
        out_specs=(VMEM,) * 7,
        scratch_shapes=[pltpu.SemaphoreType.DMA((16,))],
        input_output_aliases={i: i for i in range(5)},
        compiler_params=pltpu.CompilerParams(vmem_limit_bytes=2 * MIB),
        name="early_first",
    )(*fields, *strips)


def first_kernel(
    k, k_next,
    w_in, bx_in, by_in, bz_in, inv_in, acc_in, w1_in, xb, cb, z_plain, z_ends,
    w0, bx, by, bz, inv, acc, w1, xa_out, xb_out, ya_out, yb_out,
    in_sems, out_sems,
):
    sides = Sides()
    into = Copies(in_sems)
    land_first_x("b", k, sides, into, xb, cb, (z_plain, z_ends), (w0, bx, by, bz))
    into.wait()

    def run(a_above):
        scale((K - C, K + 1) if a_above else (K + NX, K + NX + C), ALL_ROWS, w0, bx, by, bz, inv)
        steps_of(0, k, 2, False, True, a_above, (w0, w1), bx, by, bz, inv, acc)

    on_each_side(sides, run)
    out = Copies(out_sems)
    leave(k_next, sides, out, (w0, w1)[k % 2], xa_out, xb_out, ya_out, yb_out)
    out.wait()


def first_round(k, k_next, *arrays):
    w0, bx, by, bz, inv, acc, w1, *strips = pl.pallas_call(
        functools.partial(first_kernel, k, k_next),
        out_shape=(EXT,) * 5 + (ACC, EXT) + strips_shape(k_next),
        in_specs=[VMEM] * 7 + [ANY] * 4,
        out_specs=(VMEM,) * 7 + (ANY,) * 4,
        scratch_shapes=[pltpu.SemaphoreType.DMA((12,)), pltpu.SemaphoreType.DMA((4,))],
        input_output_aliases={i: i for i in range(7)},
        compiler_params=pltpu.CompilerParams(vmem_limit_bytes=2 * MIB),
        name="first_round",
    )(*arrays)
    return (bx, by, bz, inv), ((w0, w1)[k % 2], (w1, w0)[k % 2], acc), strips


def early_kernel(first, k, last, bx, by, bz, inv, w_in, w1_in, acc_in, xa, ya, yb, ca, w0, w1, acc, sems):
    sides = Sides()
    into = Copies(sems)
    for ab, strip in (("a", ya), ("b", yb)):
        into.start(strip, w0.at[K : K + NX, pl.ds(sides.land("gy", ab, k), k)])
    land_later_x("a", k, sides, into, xa, ca, w0)
    into.wait()
    on_each_side(sides, lambda a_above: steps_of(first, k, 1, last, False, a_above, (w0, w1), bx, by, bz, inv, acc))


def early(first, k, last, coeffs, state, *strips):
    return pl.pallas_call(
        functools.partial(early_kernel, first, k, last),
        out_shape=(EXT, EXT, ACC),
        in_specs=[VMEM] * 7 + [ANY] * 4,
        out_specs=(VMEM,) * 3,
        scratch_shapes=[pltpu.SemaphoreType.DMA((5,))],
        input_output_aliases={4: 0, 5: 1, 6: 2},
        compiler_params=pltpu.CompilerParams(vmem_limit_bytes=2 * MIB),
        name="early",
    )(*coeffs, *state, *strips)


def later_kernel(
    first, k, k_next,
    bx, by, bz, inv, w_in, w1_in, acc_in, xb, cb,
    w0, w1, acc, xa_out, xb_out, ya_out, yb_out,
    in_sems, out_sems,
):
    sides = Sides()
    into = Copies(in_sems)
    land_later_x("b", k, sides, into, xb, cb, w0)
    into.wait()
    on_each_side(sides, lambda a_above: steps_of(first, k, 1, False, True, a_above, (w0, w1), bx, by, bz, inv, acc))
    out = Copies(out_sems)
    leave(k_next, sides, out, (w0, w1)[k % 2], xa_out, xb_out, ya_out, yb_out)
    out.wait()


def later_round(first, k, k_next, *arrays):
    w0, w1, acc, *strips = pl.pallas_call(
        functools.partial(later_kernel, first, k, k_next),
        out_shape=(EXT, EXT, ACC) + strips_shape(k_next),
        in_specs=[VMEM] * 7 + [ANY] * 2,
        out_specs=(VMEM,) * 3 + (ANY,) * 4,
        scratch_shapes=[pltpu.SemaphoreType.DMA((3,)), pltpu.SemaphoreType.DMA((4,))],
        input_output_aliases={4: 0, 5: 1, 6: 2},
        compiler_params=pltpu.CompilerParams(vmem_limit_bytes=2 * MIB),
        name="later_round",
    )(*arrays)
    return ((w0, w1)[k % 2], (w1, w0)[k % 2], acc), strips


def last_kernel(
    first, k,
    tile_rows, targets, mask, slots, bx, by, bz, inv, w_in, w1_in, acc_in, xb, cb,
    grad, sent, w0, w1, acc,
    nat, in_sems, out_sems,
):
    sides = Sides()
    into = Copies(in_sems)
    land_later_x("b", k, sides, into, xb, cb, w0)
    sent[...] = jnp.zeros_like(sent)
    peers = slots.shape[0]
    sent[pl.ds(CAP, peers, stride=CAP + 1), :] = slots[...]
    into.wait()
    on_each_side(sides, lambda a_above: steps_of(first, k, 1, True, True, a_above, (w0, w1), bx, by, bz, inv, acc))
    flat = acc.reshape(NX * NY * 8, 128)

    @pl.loop(0, NX)
    def _(x):
        for yc in range(0, NY, 8):
            for s in range(8):
                at = (x * NY + yc) * 8 + s
                nat[x, yc : yc + 8, 128 * s : 128 * s + 128] = flat[pl.ds(at, 8, stride=8), :]
        pltpu.make_async_copy(nat.at[x], grad.at[x], out_sems.at[x]).start()

    @pl.loop(0, mask.shape[0] // 8)
    def _(t8):
        for t in range(8):
            at = t8 * 8 + t
            row = flat[pl.ds(tile_rows[at], 1), :] * mask[pl.ds(at, 1), :].astype(F32)
            sent[pl.ds(targets[at], 1), :] = row

    for x in range(NX):
        pltpu.make_async_copy(nat.at[x], grad.at[x], out_sems.at[x]).wait()


def last_round(first, k, peers, *arrays):
    return pl.pallas_call(
        functools.partial(last_kernel, first, k),
        out_shape=(
            pltpu.HBM((NX, NY, 1024), F32),
            jax.ShapeDtypeStruct((peers * (CAP + 1), 128), F32),
            EXT,
            EXT,
            ACC,
        ),
        in_specs=[SMEM, SMEM] + [VMEM] * 9 + [ANY] * 2,
        out_specs=(HBM,) + (VMEM,) * 4,
        scratch_shapes=[
            pltpu.VMEM((NX, NY, 1024), F32),
            pltpu.SemaphoreType.DMA((3,)),
            pltpu.SemaphoreType.DMA((NX,)),
        ],
        input_output_aliases={8: 2, 9: 3, 10: 4},
        compiler_params=pltpu.CompilerParams(vmem_limit_bytes=6 * MIB),
        name="last_round",
    )(*arrays)[:2]


def finish_kernel(received, heights, out):
    peers = received.shape[0] // (CAP + 1)
    slots = received[pl.ds(CAP, peers, stride=CAP + 1), :].T
    n_slots = heights.shape[1]
    ids = lax.broadcasted_iota(jnp.int32, (n_slots, peers), 0).astype(F32)
    named = jnp.concatenate([(ids == slots[p : p + 1, :]).astype(jnp.bfloat16) for p in range(CAP)], axis=1)
    rest = jnp.concatenate([received[pl.ds(p, peers, stride=CAP + 1), :] for p in range(CAP)], axis=0)
    parts = []
    for _ in range(3):
        parts.append(rest.astype(jnp.bfloat16))
        rest = rest - parts[-1].astype(F32)
    sums = jnp.dot(named, jnp.concatenate(parts, axis=1), preferred_element_type=F32)
    table = sums[:, :128] + (sums[:, 128:256] + sums[:, 256:])
    slope = 0.5 * (heights[2] - heights[0])
    bend = heights[2] - 2.0 * heights[1] + heights[0]
    denom = 1.0 + slope * slope
    factor = 1.0 / (denom * jnp.sqrt(denom))
    skew_half = -1.5 * slope * bend * factor / denom
    out[0] = table * (factor - skew_half)
    out[1] = -2.0 * table * factor
    out[2] = table * (factor + skew_half)


def finish(received, heights):
    return pl.pallas_call(
        finish_kernel,
        out_shape=jax.ShapeDtypeStruct(heights.shape, F32),
        in_specs=[VMEM, VMEM],
        out_specs=VMEM,
        compiler_params=pltpu.CompilerParams(vmem_limit_bytes=8 * MIB),
        name="finish",
    )(received, heights)


def routes(tile_owner, tile_slot, peers):
    owner = tile_owner[:, 0]
    order = jnp.arange(owner.shape[0])
    before = (owner[:, None] == owner[None, :]) & (order[None, :] < order[:, None])
    position = jnp.sum(before.astype(jnp.int32), axis=1)
    is_owner = (owner[None, :] == jnp.arange(peers)[:, None]).astype(F32)
    placed = jnp.where(position[:, None] == jnp.arange(128)[None, :], tile_slot[:, None].astype(F32), 0.0)
    slots = jnp.dot(is_owner, placed, precision=lax.Precision.HIGHEST)
    return owner * (CAP + 1) + position, slots


def shards(grad_pressure, beta, tile_rows, tile_owner, tile_slot, face_mask, heights):
    peers = lax.axis_size("gx") * lax.axis_size("gy")
    targets, slots = routes(tile_owner, tile_slot, peers)
    k = ROUNDS[0]
    *fields, xa, xb, xb_z, ya, yb = pack(k, grad_pressure, beta)
    counts = [f[1:] for f in fields_of(k)]
    scaled, xb, ya, yb, ca, cb, *routed = exchange(
        k, counts, xa, xb, ya, yb, xb_z, functools.partial(scale_core, k, fields)
    )
    fields = early_first(k, scaled, ya, yb, ca)
    coeffs, state, strips = first_round(k, ROUNDS[1], *fields, xb, cb, *routed)
    done = k
    for k, k_next in zip(ROUNDS[1:-1], ROUNDS[2:]):
        xa, xb, ya, yb, ca, cb = exchange(k - 1, [(k, k - 1)], *strips)
        state = early(done, k, False, coeffs, state, xa, ya, yb, ca)
        state, strips = later_round(done, k, k_next, *coeffs, *state, xb, cb)
        done += k
    k = ROUNDS[-1]
    xa, xb, ya, yb, ca, cb = exchange(k - 1, [(k, k - 1)], *strips)
    state = early(done, k, True, coeffs, state, xa, ya, yb, ca)
    grad_rhs, sent = last_round(done, k, peers, tile_rows, targets, face_mask, slots, *coeffs, *state, xb, cb)
    sent = sent.reshape(peers, 1, (CAP + 1) * 128)
    received = lax.all_to_all(sent, ("gx", "gy"), split_axis=0, concat_axis=0, tiled=True)
    return grad_rhs, finish(received.reshape(peers * (CAP + 1), 128), heights)


def solution(mesh):
    in_specs = (
        P("gx", "gy", None),
        P(None, "gx", "gy", None),
        P(("gx", "gy")),
        P(("gx", "gy"), None),
        P(("gx", "gy")),
        P(("gx", "gy"), None),
        P(None, ("gx", "gy"), None),
    )
    out_specs = (P("gx", "gy", None), P(None, ("gx", "gy"), None))
    return jax.shard_map(shards, mesh=mesh, in_specs=in_specs, out_specs=out_specs, check_vma=False)
```
